32 devices in a mesh: panel: 2 (over core), lat: 4 (over z), lon: 4 (over y, x).
Axes of the slice: x: 2, y: 2, z: 4, core: 2. Of those that a mesh axis runs over, the one named last changes fastest.
Arguments:
- tracers: float32 [2, 4, 8, 32, 512], P('panel', None, None, 'lat', 'lon'), may hold values from 0.2 to 4
- courant_lon: float32 [2, 8, 32, 512], P('panel', None, 'lat', 'lon'), may hold values from -0.45 to 0.45
- courant_lat: float32 [2, 8, 32, 512], P('panel', None, 'lat', 'lon'), may hold values from -0.45 to 0.45
- cell_mass: float32 [2, 8, 32, 512], P('panel', None, 'lat', 'lon'), as said below
- donor_cell: int32 [2, 4, 4, 4, 64], P('panel', 'lat', 'lon'), may hold values from 0 to 636, as said below
- donor_frac: float32 [2, 2, 4, 4, 4, 64], P(None, 'panel', 'lat', 'lon'), may hold values from 0 to 1
- target_cell: int32 [2, 4, 4, 4, 64], P('panel', 'lat', 'lon'), may hold values from 0 to 1023, as said below
- live_count: int32 [2, 4, 4, 4], P('panel', 'lat', 'lon'), may hold values from 0 to 64, as said below
Outputs:
- updated: float32 [2, 4, 8, 32, 512], P('panel', None, None, 'lat', 'lon')
The draws below stay inside these ranges and needn't reach their ends.
Inputs may be any that keep to these rules, and one draw needn't show every extreme that they name: `donor_cell`: entry [p, a, b, d, k] is r * 128 + c with 0 <= r <= 4 and 0 <= c <= 124, so the whole stencil lies in the block of (p, a, b). `target_cell`: entry [p, d, b, s, k] is a flattened cell of the block of (p, d, b); the 256 entries of one device are all distinct. `live_count`: slots k >= the count carry nothing. `cell_mass`: the cell masses are positive.
All inputs are finite; a program needn't handle non-finite values.
Results may differ from the reference program's by a relative error of at most 0.0003.
Values sent between devices are 32-bit elements; how exact they have to be, the bound alone decides.
No kernel may reach another device: no remote copies, remote signals or barrier semaphores. Data moves between devices by JAX's collectives and lax.ppermute only.
A program may use at most 64 MiB of HBM per device.

```python
import jax
import jax.numpy as jnp
from jax import lax

TRACERS = 4
LEVELS = 8
ROWS_DEV = 8
COLS_DEV = 128
SLOTS = 64
LAT_CELLS = 32
LON_CELLS = 512
N_LAT = 4
N_LON = 4


def draw_tracers(key, part):
    shape = (2, TRACERS, LEVELS, N_LAT * ROWS_DEV, N_LON * COLS_DEV)
    first_key = jax.random.fold_in(jax.random.fold_in(key, 3), 0)
    panel_factor = 1.0 + lax.broadcasted_iota(jnp.float32, shape, 0)
    base = jax.random.uniform(first_key, shape, jnp.float32, 0.2, 2.0)
    return (base * panel_factor).astype(jnp.float32)


def draw_cell_mass(key, part):
    shape = (2, LEVELS, N_LAT * ROWS_DEV, N_LON * COLS_DEV)
    first_key = jax.random.fold_in(jax.random.fold_in(key, 5), 0)
    row_share = lax.broadcasted_iota(jnp.float32, shape, 2) / (N_LAT * ROWS_DEV - 1)
    panel_factor = 2.0 - lax.broadcasted_iota(jnp.float32, shape, 0)
    ramp = (1.0 + 2.0 * row_share) * panel_factor
    factor = jnp.exp(jax.random.uniform(first_key, shape, jnp.float32, jnp.log(0.5), jnp.log(2.0)))
    return (factor * ramp).astype(jnp.float32)


def draw_donor_cell(key, part):
    row_key, column_key = jax.random.split(jax.random.fold_in(key, 11))
    shape = (2, N_LAT, N_LON, N_LAT, SLOTS)
    row_start = jax.random.randint(row_key, shape, 0, ROWS_DEV - 3)
    column_start = jax.random.randint(column_key, shape, 0, COLS_DEV - 3)
    return (row_start * COLS_DEV + column_start).astype(jnp.int32)


def draw_target_cell(key, part):
    device_keys = jax.random.split(jax.random.fold_in(key, 23), 2 * N_LAT * N_LON)
    orders = jax.vmap(lambda single: jax.random.permutation(single, ROWS_DEV * COLS_DEV)[:N_LAT * SLOTS])(device_keys)
    return orders.reshape(2, N_LAT, N_LON, N_LAT, SLOTS).astype(jnp.int32)


def draw_live_count(key, part):
    high_key, low_key = jax.random.split(jax.random.fold_in(key, 37))
    shape = (2, N_LAT, N_LON, N_LAT)
    row_place = lax.broadcasted_iota(jnp.int32, shape, 1)
    column_place = lax.broadcasted_iota(jnp.int32, shape, 2)
    edge_row = (row_place == 0) | (row_place == N_LAT - 1)
    edge_column = (column_place == 0) | (column_place == N_LON - 1)
    high_count = jax.random.randint(high_key, shape, SLOTS // 4, SLOTS + 1)
    low_count = jax.random.randint(low_key, shape, 0, SLOTS // 4 + 1)
    return jnp.where(edge_row, SLOTS, jnp.where(edge_column, high_count, low_count)).astype(jnp.int32)


def shard_levels(own_key, dims, pieces, low, high):
    gain, own = 1.0, jax.random.fold_in(own_key, 6)
    for axis_at, parts in pieces:
        heights = jnp.exp(jax.random.uniform(jax.random.fold_in(own, axis_at), (parts,), jnp.float32, low / len(pieces), high / len(pieces)))
        gain = gain * jnp.repeat(heights, dims[axis_at] // parts).reshape([-1 if axis == axis_at else 1 for axis in range(len(dims))])
    return gain


def setup_inputs(seed: int = 0) -> dict:
    streams_of = jax.random.split(jax.random.key(seed), 9)
    tracers = draw_tracers(jax.random.fold_in(streams_of[8], 71), 0)
    courant_lon = jnp.clip(jax.random.uniform(streams_of[1], (2, LEVELS, LAT_CELLS, LON_CELLS), jnp.float32, -0.45, 0.45) * shard_levels(streams_of[1], (2, LEVELS, LAT_CELLS, LON_CELLS), ((0, 2), (2, 4), (3, 4)), -0.4, 0.0), -0.45, 0.45)
    courant_lat = jnp.clip(jax.random.uniform(streams_of[2], (2, LEVELS, LAT_CELLS, LON_CELLS), jnp.float32, -0.45, 0.45) * shard_levels(streams_of[2], (2, LEVELS, LAT_CELLS, LON_CELLS), ((0, 2), (2, 4), (3, 4)), -0.4, 0.0), -0.45, 0.45)
    cell_mass = draw_cell_mass(jax.random.fold_in(streams_of[8], 71), 0)
    donor_cell = draw_donor_cell(jax.random.fold_in(streams_of[8], 71), 0)
    donor_frac = jnp.clip(1.0 * jax.random.uniform(streams_of[5], (2, 2, N_LAT, N_LON, N_LAT, SLOTS), jnp.float32) ** shard_levels(streams_of[5], (2, 2, N_LAT, N_LON, N_LAT, SLOTS), ((1, 2), (2, 4), (3, 4)), -0.2, 0.2), 0.0, 1.0)
    target_cell = draw_target_cell(jax.random.fold_in(streams_of[8], 71), 0)
    live_count = draw_live_count(jax.random.fold_in(streams_of[8], 71), 0)
    return {"tracers": tracers, "courant_lon": courant_lon, "courant_lat": courant_lat, "cell_mass": cell_mass, "donor_cell": donor_cell, "donor_frac": donor_frac, "target_cell": target_cell, "live_count": live_count}


def cut(source, begin_at, end_at, dim_index):
    return lax.slice_in_dim(source, begin_at, end_at, axis=dim_index)


def face_flux(padded_field, courant, length, from_end):
    dim_index = padded_field.ndim - from_end
    edge_values = (7.0 / 12.0) * (cut(padded_field, 1, length + 4, dim_index) + cut(padded_field, 2, length + 5, dim_index)) - (1.0 / 12.0) * (cut(padded_field, 0, length + 3, dim_index) + cut(padded_field, 3, length + 6, dim_index))
    edge_left = cut(edge_values, 0, length + 1, dim_index)
    edge_middle = cut(edge_values, 1, length + 2, dim_index)
    edge_right = cut(edge_values, 2, length + 3, dim_index)
    cell_left = cut(padded_field, 2, length + 3, dim_index)
    cell_right = cut(padded_field, 3, length + 4, dim_index)
    number = cut(courant, 3, length + 4, dim_index)
    slope_left = edge_middle - edge_left
    curve_left = 6.0 * (cell_left - 0.5 * (edge_left + edge_middle))
    flux_positive = number * (edge_middle - 0.5 * number * (slope_left - (1.0 - (2.0 / 3.0) * number) * curve_left))
    reverse_speed = -number
    slope_right = edge_right - edge_middle
    curve_right = 6.0 * (cell_right - 0.5 * (edge_middle + edge_right))
    flux_negative = number * (edge_middle + 0.5 * reverse_speed * (slope_right + (1.0 - (2.0 / 3.0) * reverse_speed) * curve_right))
    return jnp.where(number > 0.0, flux_positive, flux_negative)


def advect(padded_field, zonal_padded, meridional_padded):
    row_total = padded_field.shape[-2] - 6
    column_total = padded_field.shape[-1] - 6
    zonal_flux = face_flux(padded_field[..., 3:3 + row_total, :], zonal_padded[..., 3:3 + row_total, :], column_total, 1)
    meridional_flux = face_flux(padded_field[..., 3:3 + column_total], meridional_padded[..., 3:3 + column_total], row_total, 2)
    center = padded_field[..., 3:3 + row_total, 3:3 + column_total]
    return center - (zonal_flux[..., 1:] - zonal_flux[..., :-1]) - (meridional_flux[..., 1:, :] - meridional_flux[..., :-1, :])


def cubic_weights(fraction):
    return jnp.stack([-fraction * (fraction - 1.0) * (fraction - 2.0) / 6.0, (fraction + 1.0) * (fraction - 1.0) * (fraction - 2.0) / 2.0, -(fraction + 1.0) * fraction * (fraction - 2.0) / 2.0, (fraction + 1.0) * fraction * (fraction - 1.0) / 6.0], axis=-1)


def interpolate(flat_field, base_cell, fraction_row, fraction_column, column_total):
    row_weights = cubic_weights(fraction_row)
    column_weights = cubic_weights(fraction_column)
    total = jnp.zeros((flat_field.shape[0], base_cell.shape[0]), jnp.float32)
    for step_row in range(4):
        for step_column in range(4):
            spots = (base_cell + step_row * column_total + step_column).astype(jnp.int32)
            factor = row_weights[:, step_row] * column_weights[:, step_column]
            total = total + factor[None, :] * jnp.take(flat_field, spots, axis=1)
    return total


def reference(tracers, courant_lon, courant_lat, cell_mass, donor_cell, donor_frac, target_cell, live_count):
    pad_widths = ((0, 0), (0, 0), (3, 3), (3, 3))
    zonal_padded = jnp.pad(courant_lon, pad_widths)
    meridional_padded = jnp.pad(courant_lat, pad_widths)

    def one_tracer(tracer_field):
        return advect(jnp.pad(tracer_field, pad_widths), zonal_padded, meridional_padded)

    advected = jnp.moveaxis(lax.map(one_tracer, jnp.moveaxis(tracers, 1, 0)), 0, 1)
    stack_rows = TRACERS * LEVELS
    cell_total = ROWS_DEV * COLS_DEV
    device_total = 2 * N_LAT * N_LON
    slot_total = N_LAT * SLOTS
    blocks = advected.reshape(2, stack_rows, N_LAT, ROWS_DEV, N_LON, COLS_DEV).transpose(0, 2, 4, 1, 3, 5).reshape(device_total, stack_rows, cell_total)

    def donate(member):
        flat_field, base_cell, fraction_row, fraction_column = member
        return interpolate(flat_field, base_cell, fraction_row, fraction_column, COLS_DEV)

    interpolated = lax.map(donate, (blocks, donor_cell.reshape(device_total, slot_total), donor_frac[0].reshape(device_total, slot_total), donor_frac[1].reshape(device_total, slot_total))).transpose(0, 2, 1)
    arrived = interpolated.reshape(2, N_LAT, N_LON, N_LAT, SLOTS, stack_rows)[::-1].transpose(0, 3, 2, 1, 4, 5).reshape(device_total, slot_total, stack_rows)
    slot_index = jnp.arange(SLOTS, dtype=jnp.int32)
    live_slots = slot_index[None, None, None, None, :] < live_count[..., None]
    targets = jnp.where(live_slots, target_cell, cell_total).reshape(device_total, slot_total).astype(jnp.int32)

    def receive(member):
        flat_field, values_in, target_spots = member
        return flat_field.at[:, target_spots].set(values_in.T, mode="drop")

    merged = lax.map(receive, (blocks, arrived, targets))
    intersected = merged.reshape(2, N_LAT, N_LON, TRACERS, LEVELS, ROWS_DEV, COLS_DEV).transpose(0, 3, 4, 1, 5, 2, 6).reshape(2, TRACERS, LEVELS, N_LAT * ROWS_DEV, N_LON * COLS_DEV)
    mass_old = jnp.sum(cell_mass[:, None] * tracers, axis=(0, 2, 3, 4))
    mass_new = jnp.sum(cell_mass[:, None] * intersected, axis=(0, 2, 3, 4))
    return intersected * (mass_old / mass_new)[None, :, None, None, None]
```

```python
import functools

import jax
import jax.numpy as jnp
from jax import lax
from jax.experimental import pallas as pl
from jax.experimental.pallas import tpu as pltpu
from jax.sharding import PartitionSpec as P

HALO = 3


def row_of(table):
    return jnp.concatenate([table[i : i + 1] for i in range(table.shape[0])], axis=1)


def live_row(live, capacity):
    slots = lax.broadcasted_iota(jnp.int32, (1, capacity), 1)
    return jnp.concatenate(
        [(slots < live[:, i : i + 1]).astype(jnp.float32) for i in range(live.shape[1])], axis=1
    )


def one_hot(spots, extent):
    places = lax.broadcasted_iota(jnp.int32, (extent, spots.shape[1]), 0)
    return (places == spots).astype(jnp.float32)


def two_parts(value):
    high = value.astype(jnp.bfloat16)
    return high, (value - high.astype(jnp.float32)).astype(jnp.bfloat16)


def three_parts(value):
    high = value.astype(jnp.bfloat16)
    rest = value - high.astype(jnp.float32)
    return (high, *two_parts(rest))


def dot(left, right, transposed=False):
    return lax.dot_general(
        left,
        right,
        (((1,), (1 if transposed else 0,)), ((), ())),
        preferred_element_type=jnp.float32,
    )


def cubic_weights(fraction):
    return (
        -fraction * (fraction - 1.0) * (fraction - 2.0) / 6.0,
        (fraction + 1.0) * (fraction - 1.0) * (fraction - 2.0) / 2.0,
        -(fraction + 1.0) * fraction * (fraction - 2.0) / 2.0,
        (fraction + 1.0) * fraction * (fraction - 1.0) / 6.0,
    )


def stencil_weights(start, fraction, extent):
    step = lax.broadcasted_iota(jnp.int32, (extent, start.shape[1]), 0) - start
    spread = jnp.zeros(step.shape, jnp.float32)
    for at, weight in enumerate(cubic_weights(fraction)):
        spread = jnp.where(step == at, weight, spread)
    return spread


def face_flux(cells, number):
    edge_left, edge, edge_right = (
        7.0 / 12.0 * (cells[i + 1] + cells[i + 2]) - 1.0 / 12.0 * (cells[i] + cells[i + 3])
        for i in range(3)
    )
    positive = number > 0.0
    speed = jnp.abs(number)
    far = jnp.where(positive, edge_left, edge_right)
    cell = jnp.where(positive, cells[2], cells[3])
    curve = 6.0 * (cell - 0.5 * (far + edge))
    return number * (edge - 0.5 * speed * ((edge - far) - (1.0 - 2.0 / 3.0 * speed) * curve))


def pack_kernel(
    field, zonal, meridional, mass, target, live, columns, northward, southward, target_mass
):
    rows, width = target_mass.shape[-2], field.shape[1]
    levels = rows
    block_rows = zonal.shape[0] // levels
    fields = field.shape[0] // block_rows
    turned = jnp.concatenate([field[...], zonal[...]], axis=0).T
    columns[0:HALO] = turned[width - HALO : width]
    columns[HALO : 2 * HALO] = turned[0:HALO]
    columns[2 * HALO :] = jnp.zeros((columns.shape[0] - 2 * HALO, columns.shape[1]), jnp.float32)
    for i in range(HALO):
        northward[pl.ds(i * fields, fields), :] = field[
            pl.ds(block_rows - HALO + i, fields, stride=block_rows), :
        ]
        southward[pl.ds(i * fields, fields), :] = field[pl.ds(i, fields, stride=block_rows), :]
    southward[pl.ds(HALO * fields, levels), :] = meridional[pl.ds(0, levels, stride=block_rows), :]
    capacity = target.shape[1]
    spots = row_of(target[...])
    row_hot = one_hot(spots // width, block_rows)
    column_hot = one_hot(lax.rem(spots, width), width).astype(jnp.bfloat16)
    picked = sum(dot(part, column_hot) for part in three_parts(mass[...]))
    picked = jnp.sum(
        picked.reshape(levels, block_rows, spots.shape[1]) * row_hot[None], axis=1
    ) * live_row(live[...], capacity)
    mine = lax.axis_index("panel")
    for block in range(target.shape[0]):
        part = picked[:, block * capacity : (block + 1) * capacity]
        part = jnp.concatenate([part, jnp.zeros((levels, width - capacity), jnp.float32)], axis=1)
        for panel in range(2):
            target_mass[panel, block] = jnp.where(mine == panel, 0.0, part)


def main_kernel(
    field, zonal, meridional, mass, columns, from_west, from_east, from_south, from_north,
    donor, fraction, target, live, target_mass, advected, outgoing, edge_rows, flux_rows,
):
    total_rows, width = field.shape
    levels = target_mass.shape[-2]
    block_rows = zonal.shape[0] // levels
    fields = total_rows // block_rows
    tracers = fields // levels
    span = levels * block_rows
    east_cells = [from_east[HALO + i : HALO + i + 1, :total_rows] for i in range(HALO)]
    own_cells = [columns[i : i + 1, :total_rows] for i in range(HALO)]
    east_number = jnp.concatenate([from_east[HALO : HALO + 1, total_rows:]] * tracers, axis=1)
    east_flux = face_flux(own_cells + east_cells, east_number)
    gap = width - 2 * HALO - 1
    lanes = jnp.concatenate(
        [
            *east_cells,
            east_flux,
            jnp.zeros((gap, total_rows), jnp.float32),
            from_west[0:HALO, :total_rows],
        ],
        axis=0,
    ).T
    for i in range(HALO):
        edge_rows[pl.ds(block_rows - HALO + i, fields, stride=block_rows), :] = from_south[
            pl.ds(i * fields, fields), :
        ]
        edge_rows[pl.ds(i, fields, stride=block_rows), :] = from_north[
            pl.ds(i * fields, fields), :
        ]
    last_rows = [
        field[pl.ds(block_rows - HALO + i, fields, stride=block_rows), :] for i in range(HALO)
    ]
    next_rows = [from_north[pl.ds(i * fields, fields), :] for i in range(HALO)]
    north_number = jnp.concatenate([from_north[pl.ds(HALO * fields, levels), :]] * tracers, axis=0)
    north_flux = face_flux(last_rows + next_rows, north_number)
    column = lax.broadcasted_iota(jnp.int32, (span, width), 1)
    row = lax.broadcasted_iota(jnp.int32, (levels, block_rows, width), 1)
    flux_rows[pl.ds(0, fields, stride=block_rows), :] = north_flux

    capacity = target.shape[1]
    spots = row_of(target[...])
    alive = live_row(live[...], capacity)
    row_hit = (one_hot(spots // width, block_rows) * alive).astype(jnp.bfloat16)
    column_hot = one_hot(lax.rem(spots, width), width).astype(jnp.bfloat16)
    kept = 1.0 - dot(row_hit, column_hot, True)
    weights = mass[...].reshape(levels, block_rows, width)

    starts = row_of(donor[...])
    row_weight = stencil_weights(starts // width, row_of(fraction[0]), block_rows)
    column_weight = stencil_weights(lax.rem(starts, width), row_of(fraction[1]), width)
    weight_high, weight_low = two_parts(column_weight)
    arriving_mass = jnp.concatenate(
        [
            target_mass[0, i, :, 0:capacity] + target_mass[1, i, :, 0:capacity]
            for i in range(target_mass.shape[1])
        ],
        axis=1,
    )

    half = fields // 2
    for tracer in range(tracers):
        part = pl.ds(tracer * span, span)
        cells = field[part, :]
        halo = lanes[tracer * span : (tracer + 1) * span]
        number = zonal[...]
        along = []
        for shift in (3, 2, 1, 0, -1, -2):
            if shift > 0:
                along.append(
                    pltpu.roll(jnp.where(column >= width - shift, halo, cells), shift, 1)
                )
            elif shift < 0:
                along.append(
                    pltpu.roll(jnp.where(column < -shift, halo, cells), width + shift, 1)
                )
            else:
                along.append(cells)
        flux = face_flux(along, number)
        next_flux = pltpu.roll(
            jnp.where(column == 0, halo[:, HALO : HALO + 1], flux), width - 1, 1
        )
        result = cells - (next_flux - flux)
        cells3 = cells.reshape(levels, block_rows, width)
        halo3 = edge_rows[part, :].reshape(levels, block_rows, width)
        along = []
        for shift in (3, 2, 1, 0, -1, -2):
            if shift > 0:
                along.append(
                    pltpu.roll(jnp.where(row >= block_rows - shift, halo3, cells3), shift, 1)
                )
            elif shift < 0:
                along.append(
                    pltpu.roll(jnp.where(row < -shift, halo3, cells3), block_rows + shift, 1)
                )
            else:
                along.append(cells3)
        flux = face_flux(along, meridional[...].reshape(levels, block_rows, width))
        edge3 = flux_rows[part, :].reshape(levels, block_rows, width)
        next_flux = pltpu.roll(jnp.where(row == 0, edge3, flux), block_rows - 1, 1)
        result = result.reshape(levels, block_rows, width) - (next_flux - flux)
        flat = result.reshape(span, width)
        advected[part, :] = flat

        high, low = two_parts(flat)
        across = dot(high, weight_high) + (dot(high, weight_low) + dot(low, weight_high))
        payload = jnp.sum(
            across.reshape(levels, block_rows, starts.shape[1]) * row_weight[None], axis=1
        )
        before = jnp.sum(weights * cells3, axis=(0, 1))[None]
        after = jnp.sum(weights * result * kept[None], axis=(0, 1))[None]
        given = jnp.sum(arriving_mass * payload, axis=0, keepdims=True)
        for block in range(target.shape[0]):
            at = block * capacity
            piece = payload[:, at : at + capacity]
            base, side = (tracer * levels) % half, (tracer * levels) // half
            for panel in range(outgoing.shape[0]):
                for place in range(outgoing.shape[2]):
                    outgoing[
                        panel, block, place, base : base + levels,
                        side * capacity : (side + 1) * capacity,
                    ] = piece
        for at in range(0, given.shape[1], width):
            after = after + given[:, at : at + width]
        sums = jnp.broadcast_to(after, outgoing.shape[:3] + (1, width))
        outgoing[:, :, :, half + tracer : half + tracer + 1, :] = sums
        sums = jnp.broadcast_to(before, outgoing.shape[:3] + (1, width))
        outgoing[:, :, :, half + tracers + tracer : half + tracers + tracer + 1, :] = sums


def fill_kernel(advected, incoming, target, live, updated):
    panels, blocks, places, payload_rows, width = incoming.shape
    _, tracers, levels, block_rows, _ = updated.shape
    fields = tracers * levels
    half = fields // 2
    capacity = target.shape[1]
    other = 1 - lax.axis_index("panel")
    place = lax.axis_index("lon")
    arrived = []
    for block in range(blocks):
        piece = incoming[other, block, place, 0:half, :]
        arrived.append(
            jnp.concatenate([piece[:, :capacity], piece[:, capacity : 2 * capacity]], axis=0)
        )
    arrived = jnp.concatenate(arrived, axis=1)
    spots = row_of(target[...])
    row_hit = one_hot(spots // width, block_rows) * live_row(live[...], capacity)
    column_hot = one_hot(lax.rem(spots, width), width).astype(jnp.bfloat16)
    hit = dot(row_hit.astype(jnp.bfloat16), column_hot, True)
    sums = jnp.sum(incoming[:, :, :, half : half + 2 * tracers, :], axis=(0, 1, 2))
    sums = jnp.sum(sums, axis=1, keepdims=True)
    scale = sums[tracers:] / sums[:tracers]
    for tracer in range(tracers):
        values = arrived[tracer * levels : (tracer + 1) * levels]
        spread = (values[:, None, :] * row_hit[None]).reshape(levels * block_rows, -1)
        placed = sum(dot(part, column_hot, True) for part in three_parts(spread))
        kept = advected[pl.ds(tracer * levels * block_rows, levels * block_rows), :]
        merged = kept.reshape(levels, block_rows, width) * (1.0 - hit)[None] + placed.reshape(
            levels, block_rows, width
        )
        updated[0, tracer] = merged * scale[tracer : tracer + 1].reshape(1, 1, 1)


def shifted(value, axis, step):
    count = lax.axis_size(axis)
    pairs = [(i, i + step) for i in range(count) if 0 <= i + step < count]
    return lax.ppermute(value, axis, pairs)


def body(
    tracers, courant_lon, courant_lat, cell_mass, donor_cell, donor_frac, target_cell, live_count
):
    _, tracer_count, levels, rows, width = tracers.shape
    blocks, capacity = donor_cell.shape[3:]
    fields = tracer_count * levels
    places = lax.axis_size("lon")
    field = tracers.reshape(fields * rows, width)
    zonal = courant_lon.reshape(levels * rows, width)
    meridional = courant_lat.reshape(levels * rows, width)
    mass = cell_mass.reshape(levels * rows, width)
    donor = donor_cell.reshape(blocks, capacity)
    fraction = donor_frac.reshape(2, blocks, capacity)
    target = target_cell.reshape(blocks, capacity)
    live = live_count.reshape(1, blocks)
    f32 = jnp.float32
    columns, northward, southward, target_mass = pl.pallas_call(
        pack_kernel,
        out_shape=(
            jax.ShapeDtypeStruct((8, (fields + levels) * rows), f32),
            jax.ShapeDtypeStruct((HALO * fields, width), f32),
            jax.ShapeDtypeStruct((HALO * fields + levels, width), f32),
            jax.ShapeDtypeStruct((2, blocks, levels, width), f32),
        ),
        name="pack_edges",
    )(field, zonal, meridional, mass, target, live)
    from_south = shifted(northward, "lat", 1)
    from_north = shifted(southward, "lat", -1)
    from_west = shifted(columns, "lon", 1)
    from_east = shifted(columns, "lon", -1)
    target_mass = lax.all_to_all(
        target_mass.reshape(2 * blocks, levels, width), ("panel", "lat"), 0, 0, tiled=True
    ).reshape(2, blocks, levels, width)
    payload_rows = fields // 2 + 2 * tracer_count
    advected, outgoing = pl.pallas_call(
        main_kernel,
        out_shape=(
            jax.ShapeDtypeStruct((fields * rows, width), f32),
            jax.ShapeDtypeStruct((2, blocks, places, payload_rows, width), f32),
        ),
        scratch_shapes=[
            pltpu.VMEM((fields * rows, width), f32),
            pltpu.VMEM((fields * rows, width), f32),
        ],
        name="advect_and_interpolate",
    )(
        field, zonal, meridional, mass, columns, from_west, from_east, from_south, from_north,
        donor, fraction, target, live, target_mass,
    )
    incoming = lax.all_to_all(
        outgoing.reshape(2 * blocks * places, payload_rows, width),
        ("panel", "lat", "lon"), 0, 0, tiled=True,
    ).reshape(2, blocks, places, payload_rows, width)
    return pl.pallas_call(
        fill_kernel,
        out_shape=jax.ShapeDtypeStruct((1, tracer_count, levels, rows, width), f32),
        name="fill_and_scale",
    )(advected, incoming, target, live)


def solution(mesh):
    in_specs = (
        P("panel", None, None, "lat", "lon"),
        P("panel", None, "lat", "lon"),
        P("panel", None, "lat", "lon"),
        P("panel", None, "lat", "lon"),
        P("panel", "lat", "lon", None, None),
        P(None, "panel", "lat", "lon", None, None),
        P("panel", "lat", "lon", None, None),
        P("panel", "lat", "lon", None),
    )
    out_specs = P("panel", None, None, "lat", "lon")
    return jax.shard_map(body, mesh=mesh, in_specs=in_specs, out_specs=out_specs, check_vma=False)
```

```python
import functools
from typing import NamedTuple

import jax
import jax.numpy as jnp
from jax import lax
from jax.experimental import pallas as pl
from jax.experimental.pallas import tpu as pltpu
from jax.sharding import PartitionSpec as P

HALO = 3


class Sizes(NamedTuple):
    tracers: int
    levels: int
    rows: int
    width: int
    blocks: int
    capacity: int
    places: int

    @property
    def fields(self):
        return self.tracers * self.levels

    @property
    def sides(self):
        return self.width // self.capacity

    @property
    def margin_rows(self):
        return self.fields // self.sides

    @property
    def halo_rows(self):
        return HALO * self.fields + self.levels

    def spot(self, tracer):
        start = tracer * self.levels
        return start % self.margin_rows, start // self.margin_rows * self.capacity


def row_of(table):
    return jnp.concatenate([table[i : i + 1] for i in range(table.shape[0])], axis=1)


def live_row(live, capacity):
    slots = lax.broadcasted_iota(jnp.int32, (1, capacity), 1)
    return jnp.concatenate(
        [(slots < live[:, i : i + 1]).astype(jnp.float32) for i in range(live.shape[1])], axis=1
    )


def one_hot(spots, extent):
    places = lax.broadcasted_iota(jnp.int32, (extent, spots.shape[1]), 0)
    return (places == spots).astype(jnp.float32)


def two_parts(value):
    high = value.astype(jnp.bfloat16)
    return high, (value - high.astype(jnp.float32)).astype(jnp.bfloat16)


def three_parts(value):
    high = value.astype(jnp.bfloat16)
    rest = value - high.astype(jnp.float32)
    return (high, *two_parts(rest))


def dot(left, right, transposed=False):
    return lax.dot_general(
        left,
        right,
        (((1,), (1 if transposed else 0,)), ((), ())),
        preferred_element_type=jnp.float32,
    )


def cubic_weights(fraction):
    return (
        -fraction * (fraction - 1.0) * (fraction - 2.0) / 6.0,
        (fraction + 1.0) * (fraction - 1.0) * (fraction - 2.0) / 2.0,
        -(fraction + 1.0) * fraction * (fraction - 2.0) / 2.0,
        (fraction + 1.0) * fraction * (fraction - 1.0) / 6.0,
    )


def stencil_weights(start, fraction, extent):
    step = lax.broadcasted_iota(jnp.int32, (extent, start.shape[1]), 0) - start
    spread = jnp.zeros(step.shape, jnp.float32)
    for at, weight in enumerate(cubic_weights(fraction)):
        spread = jnp.where(step == at, weight, spread)
    return spread


def face_flux(cells, number):
    edge_left, edge, edge_right = (
        7.0 / 12.0 * (cells[i + 1] + cells[i + 2]) - 1.0 / 12.0 * (cells[i] + cells[i + 3])
        for i in range(3)
    )
    positive = number > 0.0
    speed = jnp.abs(number)
    far = jnp.where(positive, edge_left, edge_right)
    cell = jnp.where(positive, cells[2], cells[3])
    curve = 6.0 * (cell - 0.5 * (far + edge))
    return number * (edge - 0.5 * speed * ((edge - far) - (1.0 - 2.0 / 3.0 * speed) * curve))


def pack_kernel(sizes, field, zonal, meridional, mass, target, live, columns, lat_blocks):
    _, levels, rows, width, blocks, capacity, _ = sizes
    fields = sizes.fields
    turned = jnp.concatenate([field[...], zonal[...]], axis=0).T
    columns[0:HALO] = turned[width - HALO : width]
    columns[HALO : 2 * HALO] = turned[0:HALO]
    columns[2 * HALO :] = jnp.zeros((columns.shape[0] - 2 * HALO, columns.shape[1]), jnp.float32)
    spots = row_of(target[...])
    row_hot = one_hot(spots // width, rows)
    column_hot = one_hot(lax.rem(spots, width), width).astype(jnp.bfloat16)
    picked = sum(dot(part, column_hot) for part in three_parts(mass[...]))
    picked = jnp.sum(
        picked.reshape(levels, rows, spots.shape[1]) * row_hot[None], axis=1
    ) * live_row(live[...], capacity)
    here = lax.axis_index("lat")
    for block in range(blocks):
        part = picked[:, block * capacity : (block + 1) * capacity]
        lat_blocks[block, pl.ds(sizes.halo_rows, levels), :] = jnp.concatenate(
            [part] * sizes.sides, axis=1
        )

        @pl.when(block > here)
        def northward():
            for i in range(HALO):
                lat_blocks[block, pl.ds(i * fields, fields), :] = field[
                    pl.ds(rows - HALO + i, fields, stride=rows), :
                ]
            lat_blocks[block, pl.ds(HALO * fields, levels), :] = jnp.zeros(
                (levels, width), jnp.float32
            )

        @pl.when(block <= here)
        def southward():
            for i in range(HALO):
                lat_blocks[block, pl.ds(i * fields, fields), :] = field[
                    pl.ds(i, fields, stride=rows), :
                ]
            lat_blocks[block, pl.ds(HALO * fields, levels), :] = meridional[
                pl.ds(0, levels, stride=rows), :
            ]


def main_kernel(
    sizes, field, zonal, meridional, mass, columns, from_west, from_east, from_lat,
    donor, fraction, target, live, advected, outgoing, edge_rows, flux_rows,
):
    tracers, levels, rows, width, blocks, capacity, _ = sizes
    fields, span, total = sizes.fields, levels * rows, sizes.fields * rows
    east_cells = [from_east[HALO + i : HALO + i + 1, :total] for i in range(HALO)]
    own_cells = [columns[i : i + 1, :total] for i in range(HALO)]
    east_number = jnp.concatenate([from_east[HALO : HALO + 1, total:]] * tracers, axis=1)
    east_flux = face_flux(own_cells + east_cells, east_number)
    lanes = jnp.concatenate(
        [
            *east_cells,
            east_flux,
            jnp.zeros((width - 2 * HALO - 1, total), jnp.float32),
            from_west[0:HALO, :total],
        ],
        axis=0,
    ).T
    here = lax.axis_index("lat")
    south, north = jnp.maximum(here - 1, 0), jnp.minimum(here + 1, blocks - 1)
    has_south, has_north = here > 0, here < blocks - 1
    next_rows = []
    for i in range(HALO):
        part = pl.ds(i * fields, fields)
        south_row = jnp.where(has_south, from_lat[south, part, :], 0.0)
        north_row = jnp.where(has_north, from_lat[north, part, :], 0.0)
        next_rows.append(north_row)
        edge_rows[pl.ds(rows - HALO + i, fields, stride=rows), :] = south_row
        edge_rows[pl.ds(i, fields, stride=rows), :] = north_row
    last_rows = [field[pl.ds(rows - HALO + i, fields, stride=rows), :] for i in range(HALO)]
    north_number = jnp.where(has_north, from_lat[north, pl.ds(HALO * fields, levels), :], 0.0)
    flux_rows[pl.ds(0, fields, stride=rows), :] = face_flux(
        last_rows + next_rows, jnp.concatenate([north_number] * tracers, axis=0)
    )
    column = lax.broadcasted_iota(jnp.int32, (span, width), 1)
    row = lax.broadcasted_iota(jnp.int32, (levels, rows, width), 1)

    spots = row_of(target[...])
    row_hit = one_hot(spots // width, rows) * live_row(live[...], capacity)
    column_hot = one_hot(lax.rem(spots, width), width).astype(jnp.bfloat16)
    kept = 1.0 - dot(row_hit.astype(jnp.bfloat16), column_hot, True)
    weights = mass[...].reshape(levels, rows, width)

    starts = row_of(donor[...])
    row_weight = stencil_weights(starts // width, row_of(fraction[0]), rows)
    column_weight = stencil_weights(lax.rem(starts, width), row_of(fraction[1]), width)
    weight_high, weight_low = two_parts(column_weight)

    sums = blocks * sizes.margin_rows
    for tracer in range(tracers):
        part = pl.ds(tracer * span, span)
        cells = field[part, :]
        halo = lanes[tracer * span : (tracer + 1) * span]
        along = []
        for shift in (3, 2, 1, 0, -1, -2):
            if shift > 0:
                along.append(
                    pltpu.roll(jnp.where(column >= width - shift, halo, cells), shift, 1)
                )
            elif shift < 0:
                along.append(
                    pltpu.roll(jnp.where(column < -shift, halo, cells), width + shift, 1)
                )
            else:
                along.append(cells)
        flux = face_flux(along, zonal[...])
        next_flux = pltpu.roll(
            jnp.where(column == 0, halo[:, HALO : HALO + 1], flux), width - 1, 1
        )
        result = cells - (next_flux - flux)
        cells3 = cells.reshape(levels, rows, width)
        halo3 = edge_rows[part, :].reshape(levels, rows, width)
        along = []
        for shift in (3, 2, 1, 0, -1, -2):
            if shift > 0:
                along.append(pltpu.roll(jnp.where(row >= rows - shift, halo3, cells3), shift, 1))
            elif shift < 0:
                along.append(pltpu.roll(jnp.where(row < -shift, halo3, cells3), rows + shift, 1))
            else:
                along.append(cells3)
        flux = face_flux(along, meridional[...].reshape(levels, rows, width))
        edge3 = flux_rows[part, :].reshape(levels, rows, width)
        next_flux = pltpu.roll(jnp.where(row == 0, edge3, flux), rows - 1, 1)
        result = result.reshape(levels, rows, width) - (next_flux - flux)
        flat = result.reshape(span, width)
        advected[part, :] = flat

        high, low = two_parts(flat)
        across = dot(high, weight_high) + (dot(high, weight_low) + dot(low, weight_high))
        payload = jnp.sum(
            across.reshape(levels, rows, starts.shape[1]) * row_weight[None], axis=1
        )
        base, lane = sizes.spot(tracer)
        for block in range(blocks):
            at = block * capacity
            outgoing[
                pl.ds(block * sizes.margin_rows + base, levels), lane : lane + capacity
            ] = payload[:, at : at + capacity]
        outgoing[sums + tracer : sums + tracer + 1, :] = jnp.sum(
            weights * result * kept[None], axis=(0, 1)
        )[None]
        outgoing[sums + tracers + tracer : sums + tracers + tracer + 1, :] = jnp.sum(
            weights * cells3, axis=(0, 1)
        )[None]


def blocks_kernel(sizes, own, given, from_lat, other_lat, lon_blocks):
    tracers, levels, _, width, blocks, capacity, places = sizes
    size = sizes.margin_rows
    sums = pl.ds(blocks * size, 2 * tracers)
    weighed = jnp.zeros((size, width), jnp.float32)
    for block in range(blocks):
        margin = given[pl.ds(block * size, size), :]
        for sent, masses in ((margin, from_lat), (own[pl.ds(block * size, size), :], other_lat)):
            mass = masses[block, pl.ds(sizes.halo_rows, levels), :]
            weighed = weighed + sent * jnp.concatenate([mass] * (size // levels), axis=0)
        lon_blocks[block, :, 0:size, :] = jnp.broadcast_to(margin[None], (places, size, width))
    column = lax.broadcasted_iota(jnp.int32, (1, width), 1)
    partial = own[sums, :] + given[sums, :]
    added = []
    for tracer in range(tracers):
        base, lane = sizes.spot(tracer)
        row = jnp.sum(weighed[base : base + levels], axis=0, keepdims=True)
        added.append(jnp.where((column >= lane) & (column < lane + capacity), row, 0.0))
    partial = partial + jnp.concatenate(
        added + [jnp.zeros((tracers, width), jnp.float32)], axis=0
    )
    lon_blocks[:, :, size:, :] = jnp.broadcast_to(
        partial[None, None], (blocks, places, 2 * tracers, width)
    )


def fill_kernel(sizes, advected, incoming, target, live, updated):
    tracers, levels, rows, width, blocks, capacity, _ = sizes
    size = sizes.margin_rows
    place = lax.axis_index("lon")
    arrived = []
    for block in range(blocks):
        piece = incoming[block, place, 0:size, :]
        arrived.append(
            jnp.concatenate(
                [piece[:, i * capacity : (i + 1) * capacity] for i in range(sizes.sides)], axis=0
            )
        )
    arrived = jnp.concatenate(arrived, axis=1)
    spots = row_of(target[...])
    row_hit = one_hot(spots // width, rows) * live_row(live[...], capacity)
    column_hot = one_hot(lax.rem(spots, width), width).astype(jnp.bfloat16)
    kept = 1.0 - dot(row_hit.astype(jnp.bfloat16), column_hot, True)
    sums = jnp.sum(incoming[:, :, size:, :], axis=(0, 1))
    sums = jnp.sum(sums, axis=1, keepdims=True)
    scale = sums[tracers:] / sums[:tracers]
    for tracer in range(tracers):
        values = arrived[tracer * levels : (tracer + 1) * levels]
        spread = (values[:, None, :] * row_hit[None]).reshape(levels * rows, -1)
        placed = sum(dot(part, column_hot, True) for part in three_parts(spread))
        old = advected[pl.ds(tracer * levels * rows, levels * rows), :]
        merged = old.reshape(levels, rows, width) * kept[None] + placed.reshape(
            levels, rows, width
        )
        updated[0, tracer] = merged * scale[tracer : tracer + 1].reshape(1, 1, 1)


def shifted(value, axis, step):
    count = lax.axis_size(axis)
    pairs = [(i, i + step) for i in range(count) if 0 <= i + step < count]
    return lax.ppermute(value, axis, pairs)


def body(
    tracers, courant_lon, courant_lat, cell_mass, donor_cell, donor_frac, target_cell, live_count
):
    sizes = Sizes(*tracers.shape[1:], *donor_cell.shape[3:], lax.axis_size("lon"))
    _, levels, rows, width, blocks, capacity, places = sizes
    fields = sizes.fields
    field = tracers.reshape(fields * rows, width)
    zonal = courant_lon.reshape(levels * rows, width)
    meridional = courant_lat.reshape(levels * rows, width)
    mass = cell_mass.reshape(levels * rows, width)
    donor = donor_cell.reshape(blocks, capacity)
    fraction = donor_frac.reshape(2, blocks, capacity)
    target = target_cell.reshape(blocks, capacity)
    live = live_count.reshape(1, blocks)

    def shape(*dims):
        return jax.ShapeDtypeStruct(dims, jnp.float32)

    columns, lat_blocks = pl.pallas_call(
        functools.partial(pack_kernel, sizes),
        out_shape=(
            shape(8, (fields + levels) * rows),
            shape(blocks, sizes.halo_rows + levels, width),
        ),
        name="pack_edges",
    )(field, zonal, meridional, mass, target, live)
    from_lat = lax.all_to_all(lat_blocks, "lat", 0, 0, tiled=True)
    other_lat = lax.ppermute(from_lat, "panel", [(0, 1), (1, 0)])
    from_west = shifted(columns, "lon", 1)
    from_east = shifted(columns, "lon", -1)
    payload_rows = sizes.margin_rows + 2 * sizes.tracers
    advected, outgoing = pl.pallas_call(
        functools.partial(main_kernel, sizes),
        out_shape=(
            shape(fields * rows, width),
            shape(blocks * sizes.margin_rows + 2 * sizes.tracers, width),
        ),
        scratch_shapes=[
            pltpu.VMEM((fields * rows, width), jnp.float32),
            pltpu.VMEM((fields * rows, width), jnp.float32),
        ],
        name="advect_and_interpolate",
    )(
        field, zonal, meridional, mass, columns, from_west, from_east, from_lat,
        donor, fraction, target, live,
    )
    given = lax.ppermute(outgoing, "panel", [(0, 1), (1, 0)])
    lon_blocks = pl.pallas_call(
        functools.partial(blocks_kernel, sizes),
        out_shape=shape(blocks, places, payload_rows, width),
        name="margin_blocks",
    )(outgoing, given, from_lat, other_lat)
    incoming = lax.all_to_all(
        lon_blocks.reshape(blocks * places, payload_rows, width), ("lat", "lon"), 0, 0, tiled=True
    ).reshape(blocks, places, payload_rows, width)
    return pl.pallas_call(
        functools.partial(fill_kernel, sizes),
        out_shape=shape(1, sizes.tracers, levels, rows, width),
        name="fill_and_scale",
    )(advected, incoming, target, live)


def solution(mesh):
    in_specs = (
        P("panel", None, None, "lat", "lon"),
        P("panel", None, "lat", "lon"),
        P("panel", None, "lat", "lon"),
        P("panel", None, "lat", "lon"),
        P("panel", "lat", "lon", None, None),
        P(None, "panel", "lat", "lon", None, None),
        P("panel", "lat", "lon", None, None),
        P("panel", "lat", "lon", None),
    )
    out_specs = P("panel", None, None, "lat", "lon")
    return jax.shard_map(body, mesh=mesh, in_specs=in_specs, out_specs=out_specs, check_vma=False)
```

```python
import functools
from typing import NamedTuple

import jax
import jax.numpy as jnp
from jax import lax
from jax.experimental import pallas as pl
from jax.experimental.pallas import tpu as pltpu
from jax.sharding import PartitionSpec as P

HALO = 3


class Sizes(NamedTuple):
    tracers: int
    levels: int
    rows: int
    width: int
    blocks: int
    capacity: int
    places: int

    @property
    def fields(self):
        return self.tracers * self.levels

    @property
    def sides(self):
        return self.width // self.capacity

    @property
    def margin_rows(self):
        return self.fields // self.sides

    @property
    def halo_rows(self):
        return HALO * self.fields + self.levels

    def spot(self, tracer):
        start = tracer * self.levels
        return start % self.margin_rows, start // self.margin_rows * self.capacity


def row_of(table):
    return jnp.concatenate([table[i : i + 1] for i in range(table.shape[0])], axis=1)


def live_row(live, capacity):
    slots = lax.broadcasted_iota(jnp.int32, (1, capacity), 1)
    return jnp.concatenate(
        [(slots < live[:, i : i + 1]).astype(jnp.float32) for i in range(live.shape[1])], axis=1
    )


def one_hot(spots, extent):
    places = lax.broadcasted_iota(jnp.int32, (extent, spots.shape[1]), 0)
    return (places == spots).astype(jnp.float32)


def two_parts(value):
    high = value.astype(jnp.bfloat16)
    return high, (value - high.astype(jnp.float32)).astype(jnp.bfloat16)


def three_parts(value):
    high = value.astype(jnp.bfloat16)
    rest = value - high.astype(jnp.float32)
    return (high, *two_parts(rest))


def dot(left, right, transposed=False):
    return lax.dot_general(
        left,
        right,
        (((1,), (1 if transposed else 0,)), ((), ())),
        preferred_element_type=jnp.float32,
    )


def cubic_weights(fraction):
    return (
        -fraction * (fraction - 1.0) * (fraction - 2.0) / 6.0,
        (fraction + 1.0) * (fraction - 1.0) * (fraction - 2.0) / 2.0,
        -(fraction + 1.0) * fraction * (fraction - 2.0) / 2.0,
        (fraction + 1.0) * fraction * (fraction - 1.0) / 6.0,
    )


def stencil_weights(start, fraction, extent):
    step = lax.broadcasted_iota(jnp.int32, (extent, start.shape[1]), 0) - start
    spread = jnp.zeros(step.shape, jnp.float32)
    for at, weight in enumerate(cubic_weights(fraction)):
        spread = jnp.where(step == at, weight, spread)
    return spread


def face_flux(cells, number):
    edge_left, edge, edge_right = (
        7.0 / 12.0 * (cells[i + 1] + cells[i + 2]) - 1.0 / 12.0 * (cells[i] + cells[i + 3])
        for i in range(3)
    )
    positive = number > 0.0
    speed = jnp.abs(number)
    far = jnp.where(positive, edge_left, edge_right)
    cell = jnp.where(positive, cells[2], cells[3])
    curve = 6.0 * (cell - 0.5 * (far + edge))
    return number * (edge - 0.5 * speed * ((edge - far) - (1.0 - 2.0 / 3.0 * speed) * curve))


def pack_kernel(sizes, field, zonal, meridional, mass, target, live, columns, lat_blocks):
    _, levels, rows, width, blocks, capacity, _ = sizes
    fields = sizes.fields
    turned = jnp.concatenate([field[...], zonal[...]], axis=0).T
    columns[0:HALO] = turned[width - HALO : width]
    columns[HALO : 2 * HALO] = turned[0:HALO]
    columns[2 * HALO :] = jnp.zeros((columns.shape[0] - 2 * HALO, columns.shape[1]), jnp.float32)
    spots = row_of(target[...])
    row_hot = one_hot(spots // width, rows)
    column_hot = one_hot(lax.rem(spots, width), width).astype(jnp.bfloat16)
    picked = sum(dot(part, column_hot) for part in three_parts(mass[...]))
    picked = jnp.sum(
        picked.reshape(levels, rows, spots.shape[1]) * row_hot[None], axis=1
    ) * live_row(live[...], capacity)
    here = lax.axis_index("lat")
    for block in range(blocks):
        part = picked[:, block * capacity : (block + 1) * capacity]
        lat_blocks[block, pl.ds(sizes.halo_rows, levels), :] = jnp.concatenate(
            [part] * sizes.sides, axis=1
        )

        @pl.when(block > here)
        def northward():
            for i in range(HALO):
                lat_blocks[block, pl.ds(i * fields, fields), :] = field[
                    pl.ds(rows - HALO + i, fields, stride=rows), :
                ]
            lat_blocks[block, pl.ds(HALO * fields, levels), :] = jnp.zeros(
                (levels, width), jnp.float32
            )

        @pl.when(block <= here)
        def southward():
            for i in range(HALO):
                lat_blocks[block, pl.ds(i * fields, fields), :] = field[
                    pl.ds(i, fields, stride=rows), :
                ]
            lat_blocks[block, pl.ds(HALO * fields, levels), :] = meridional[
                pl.ds(0, levels, stride=rows), :
            ]


def main_kernel(
    sizes, field, zonal, meridional, mass, columns, from_west, from_east, from_lat,
    donor, fraction, target, live, advected, outgoing, edge_rows, flux_rows,
):
    tracers, levels, rows, width, blocks, capacity, _ = sizes
    fields, span, total = sizes.fields, levels * rows, sizes.fields * rows
    east_cells = [from_east[HALO + i : HALO + i + 1, :total] for i in range(HALO)]
    own_cells = [columns[i : i + 1, :total] for i in range(HALO)]
    east_number = jnp.concatenate([from_east[HALO : HALO + 1, total:]] * tracers, axis=1)
    east_flux = face_flux(own_cells + east_cells, east_number)
    lanes = jnp.concatenate(
        [
            *east_cells,
            east_flux,
            jnp.zeros((width - 2 * HALO - 1, total), jnp.float32),
            from_west[0:HALO, :total],
        ],
        axis=0,
    ).T
    here = lax.axis_index("lat")
    south, north = jnp.maximum(here - 1, 0), jnp.minimum(here + 1, blocks - 1)
    has_south, has_north = here > 0, here < blocks - 1
    next_rows = []
    for i in range(HALO):
        part = pl.ds(i * fields, fields)
        south_row = jnp.where(has_south, from_lat[south, part, :], 0.0)
        north_row = jnp.where(has_north, from_lat[north, part, :], 0.0)
        next_rows.append(north_row)
        edge_rows[pl.ds(rows - HALO + i, fields, stride=rows), :] = south_row
        edge_rows[pl.ds(i, fields, stride=rows), :] = north_row
    last_rows = [field[pl.ds(rows - HALO + i, fields, stride=rows), :] for i in range(HALO)]
    north_number = jnp.where(has_north, from_lat[north, pl.ds(HALO * fields, levels), :], 0.0)
    flux_rows[pl.ds(0, fields, stride=rows), :] = face_flux(
        last_rows + next_rows, jnp.concatenate([north_number] * tracers, axis=0)
    )
    column = lax.broadcasted_iota(jnp.int32, (span, width), 1)
    row = lax.broadcasted_iota(jnp.int32, (levels, rows, width), 1)

    spots = row_of(target[...])
    row_hit = one_hot(spots // width, rows) * live_row(live[...], capacity)
    column_hot = one_hot(lax.rem(spots, width), width).astype(jnp.bfloat16)
    kept = 1.0 - dot(row_hit.astype(jnp.bfloat16), column_hot, True)
    weights = mass[...].reshape(levels, rows, width)

    starts = row_of(donor[...])
    row_weight = stencil_weights(starts // width, row_of(fraction[0]), rows)
    column_weight = stencil_weights(lax.rem(starts, width), row_of(fraction[1]), width)
    weight_high, weight_low = two_parts(column_weight)

    sums = blocks * sizes.margin_rows
    for tracer in range(tracers):
        part = pl.ds(tracer * span, span)
        cells = field[part, :]
        halo = lanes[tracer * span : (tracer + 1) * span]
        along = []
        for shift in (3, 2, 1, 0, -1, -2):
            if shift > 0:
                along.append(
                    pltpu.roll(jnp.where(column >= width - shift, halo, cells), shift, 1)
                )
            elif shift < 0:
                along.append(
                    pltpu.roll(jnp.where(column < -shift, halo, cells), width + shift, 1)
                )
            else:
                along.append(cells)
        flux = face_flux(along, zonal[...])
        next_flux = pltpu.roll(
            jnp.where(column == 0, halo[:, HALO : HALO + 1], flux), width - 1, 1
        )
        result = cells - (next_flux - flux)
        cells3 = cells.reshape(levels, rows, width)
        halo3 = edge_rows[part, :].reshape(levels, rows, width)
        along = []
        for shift in (3, 2, 1, 0, -1, -2):
            if shift > 0:
                along.append(pltpu.roll(jnp.where(row >= rows - shift, halo3, cells3), shift, 1))
            elif shift < 0:
                along.append(pltpu.roll(jnp.where(row < -shift, halo3, cells3), rows + shift, 1))
            else:
                along.append(cells3)
        flux = face_flux(along, meridional[...].reshape(levels, rows, width))
        edge3 = flux_rows[part, :].reshape(levels, rows, width)
        next_flux = pltpu.roll(jnp.where(row == 0, edge3, flux), rows - 1, 1)
        result = result.reshape(levels, rows, width) - (next_flux - flux)
        flat = result.reshape(span, width)
        advected[part, :] = flat

        high, low = two_parts(flat)
        across = dot(high, weight_high) + (dot(high, weight_low) + dot(low, weight_high))
        payload = jnp.sum(
            across.reshape(levels, rows, starts.shape[1]) * row_weight[None], axis=1
        )
        base, lane = sizes.spot(tracer)
        for block in range(blocks):
            at = block * capacity
            outgoing[
                pl.ds(block * sizes.margin_rows + base, levels), lane : lane + capacity
            ] = payload[:, at : at + capacity]
        outgoing[sums + tracer : sums + tracer + 1, :] = jnp.sum(
            weights * result * kept[None], axis=(0, 1)
        )[None]
        outgoing[sums + tracers + tracer : sums + tracers + tracer + 1, :] = jnp.sum(
            weights * cells3, axis=(0, 1)
        )[None]


def blocks_kernel(sizes, own, given, from_lat, other_lat, lon_blocks):
    tracers, levels, _, width, blocks, capacity, places = sizes
    size = sizes.margin_rows
    sums = pl.ds(blocks * size, 2 * tracers)
    weighed = jnp.zeros((size, width), jnp.float32)
    for block in range(blocks):
        margin = given[pl.ds(block * size, size), :]
        for sent, masses in ((margin, from_lat), (own[pl.ds(block * size, size), :], other_lat)):
            mass = masses[block, pl.ds(sizes.halo_rows, levels), :]
            weighed = weighed + sent * jnp.concatenate([mass] * (size // levels), axis=0)
        lon_blocks[block, :, 0:size, :] = jnp.broadcast_to(margin[None], (places, size, width))
    column = lax.broadcasted_iota(jnp.int32, (1, width), 1)
    partial = own[sums, :] + given[sums, :]
    added = []
    for tracer in range(tracers):
        base, lane = sizes.spot(tracer)
        row = jnp.sum(weighed[base : base + levels], axis=0, keepdims=True)
        added.append(jnp.where((column >= lane) & (column < lane + capacity), row, 0.0))
    partial = partial + jnp.concatenate(
        added + [jnp.zeros((tracers, width), jnp.float32)], axis=0
    )
    lon_blocks[:, :, size:, :] = jnp.broadcast_to(
        partial[None, None], (blocks, places, 2 * tracers, width)
    )


def fill_kernel(sizes, advected, incoming, target, live, updated):
    tracers, levels, rows, width, blocks, capacity, _ = sizes
    size = sizes.margin_rows
    place = lax.axis_index("lon")
    arrived = []
    for block in range(blocks):
        piece = incoming[block, place, 0:size, :]
        arrived.append(
            jnp.concatenate(
                [piece[:, i * capacity : (i + 1) * capacity] for i in range(sizes.sides)], axis=0
            )
        )
    arrived = jnp.concatenate(arrived, axis=1)
    spots = row_of(target[...])
    row_hit = one_hot(spots // width, rows) * live_row(live[...], capacity)
    column_hot = one_hot(lax.rem(spots, width), width).astype(jnp.bfloat16)
    kept = 1.0 - dot(row_hit.astype(jnp.bfloat16), column_hot, True)
    sums = jnp.sum(incoming[:, :, size:, :], axis=(0, 1))
    sums = jnp.sum(sums, axis=1, keepdims=True)
    scale = sums[tracers:] / sums[:tracers]
    for tracer in range(tracers):
        values = arrived[tracer * levels : (tracer + 1) * levels]
        spread = (values[:, None, :] * row_hit[None]).reshape(levels * rows, -1)
        placed = sum(dot(part, column_hot, True) for part in three_parts(spread))
        old = advected[pl.ds(tracer * levels * rows, levels * rows), :]
        merged = old.reshape(levels, rows, width) * kept[None] + placed.reshape(
            levels, rows, width
        )
        updated[0, tracer] = merged * scale[tracer : tracer + 1].reshape(1, 1, 1)


def shifted(value, axis, step):
    count = lax.axis_size(axis)
    pairs = [(i, i + step) for i in range(count) if 0 <= i + step < count]
    return lax.ppermute(value, axis, pairs)


def body(
    tracers, courant_lon, courant_lat, cell_mass, donor_cell, donor_frac, target_cell, live_count
):
    sizes = Sizes(*tracers.shape[1:], *donor_cell.shape[3:], lax.axis_size("lon"))
    _, levels, rows, width, blocks, capacity, places = sizes
    fields = sizes.fields
    field = tracers.reshape(fields * rows, width)
    zonal = courant_lon.reshape(levels * rows, width)
    meridional = courant_lat.reshape(levels * rows, width)
    mass = cell_mass.reshape(levels * rows, width)
    donor = donor_cell.reshape(blocks, capacity)
    fraction = donor_frac.reshape(2, blocks, capacity)
    target = target_cell.reshape(blocks, capacity)
    live = live_count.reshape(1, blocks)

    def shape(*dims):
        return pltpu.VMEM(dims, jnp.float32)

    def near(*values):
        return (pltpu.with_memory_space_constraint(value, pltpu.VMEM) for value in values)

    columns, lat_blocks = pl.pallas_call(
        functools.partial(pack_kernel, sizes),
        out_shape=(
            shape(8, (fields + levels) * rows),
            shape(blocks, sizes.halo_rows + levels, width),
        ),
        name="pack_edges",
    )(field, zonal, meridional, mass, target, live)
    from_lat = lax.all_to_all(lat_blocks, "lat", 0, 0, tiled=True)
    from_west = shifted(columns, "lon", 1)
    from_east = shifted(columns, "lon", -1)
    from_lat, from_west, from_east = lax.optimization_barrier((from_lat, from_west, from_east))
    other_lat = lax.ppermute(from_lat, "panel", [(0, 1), (1, 0)])
    payload_rows = sizes.margin_rows + 2 * sizes.tracers
    advected, outgoing = pl.pallas_call(
        functools.partial(main_kernel, sizes),
        out_shape=(
            shape(fields * rows, width),
            shape(blocks * sizes.margin_rows + 2 * sizes.tracers, width),
        ),
        scratch_shapes=[
            pltpu.VMEM((fields * rows, width), jnp.float32),
            pltpu.VMEM((fields * rows, width), jnp.float32),
        ],
        name="advect_and_interpolate",
    )(
        field, zonal, meridional, mass, *near(columns, from_west, from_east, from_lat),
        donor, fraction, target, live,
    )
    given = lax.ppermute(outgoing, "panel", [(0, 1), (1, 0)])
    lon_blocks = pl.pallas_call(
        functools.partial(blocks_kernel, sizes),
        out_shape=shape(blocks, places, payload_rows, width),
        name="margin_blocks",
    )(*near(outgoing, given, from_lat, other_lat))
    incoming = lax.all_to_all(
        lon_blocks.reshape(blocks * places, payload_rows, width), ("lat", "lon"), 0, 0, tiled=True
    ).reshape(blocks, places, payload_rows, width)
    return pl.pallas_call(
        functools.partial(fill_kernel, sizes),
        out_shape=jax.ShapeDtypeStruct((1, sizes.tracers, levels, rows, width), jnp.float32),
        name="fill_and_scale",
    )(*near(advected, incoming), target, live)


def solution(mesh):
    in_specs = (
        P("panel", None, None, "lat", "lon"),
        P("panel", None, "lat", "lon"),
        P("panel", None, "lat", "lon"),
        P("panel", None, "lat", "lon"),
        P("panel", "lat", "lon", None, None),
        P(None, "panel", "lat", "lon", None, None),
        P("panel", "lat", "lon", None, None),
        P("panel", "lat", "lon", None),
    )
    out_specs = P("panel", None, None, "lat", "lon")
    return jax.shard_map(body, mesh=mesh, in_specs=in_specs, out_specs=out_specs, check_vma=False)
```

```python
import functools
from typing import NamedTuple

import jax
import jax.numpy as jnp
from jax import lax
from jax.experimental import pallas as pl
from jax.experimental.pallas import tpu as pltpu
from jax.sharding import PartitionSpec as P

HALO = 3


class Sizes(NamedTuple):
    tracers: int
    levels: int
    rows: int
    width: int
    blocks: int
    capacity: int
    places: int

    @property
    def fields(self):
        return self.tracers * self.levels

    @property
    def sides(self):
        return self.width // self.capacity

    @property
    def margin_rows(self):
        return self.fields // self.sides

    @property
    def halo_rows(self):
        return HALO * self.fields + self.levels

    def spot(self, tracer):
        start = tracer * self.levels
        return start % self.margin_rows, start // self.margin_rows * self.capacity


def row_of(table):
    return jnp.concatenate([table[i : i + 1] for i in range(table.shape[0])], axis=1)


def live_row(live, capacity):
    slots = lax.broadcasted_iota(jnp.int32, (1, capacity), 1)
    return jnp.concatenate(
        [(slots < live[:, i : i + 1]).astype(jnp.float32) for i in range(live.shape[1])], axis=1
    )


def one_hot(spots, extent):
    places = lax.broadcasted_iota(jnp.int32, (extent, spots.shape[1]), 0)
    return (places == spots).astype(jnp.float32)


def two_parts(value):
    high = value.astype(jnp.bfloat16)
    return high, (value - high.astype(jnp.float32)).astype(jnp.bfloat16)


def three_parts(value):
    high = value.astype(jnp.bfloat16)
    rest = value - high.astype(jnp.float32)
    return (high, *two_parts(rest))


def dot(left, right, transposed=False):
    return lax.dot_general(
        left,
        right,
        (((1,), (1 if transposed else 0,)), ((), ())),
        preferred_element_type=jnp.float32,
    )


def cubic_weights(fraction):
    return (
        -fraction * (fraction - 1.0) * (fraction - 2.0) / 6.0,
        (fraction + 1.0) * (fraction - 1.0) * (fraction - 2.0) / 2.0,
        -(fraction + 1.0) * fraction * (fraction - 2.0) / 2.0,
        (fraction + 1.0) * fraction * (fraction - 1.0) / 6.0,
    )


def stencil_weights(start, fraction, extent):
    step = lax.broadcasted_iota(jnp.int32, (extent, start.shape[1]), 0) - start
    spread = jnp.zeros(step.shape, jnp.float32)
    for at, weight in enumerate(cubic_weights(fraction)):
        spread = jnp.where(step == at, weight, spread)
    return spread


def face_flux(cells, number):
    edge_left, edge, edge_right = (
        7.0 / 12.0 * (cells[i + 1] + cells[i + 2]) - 1.0 / 12.0 * (cells[i] + cells[i + 3])
        for i in range(3)
    )
    positive = number > 0.0
    speed = jnp.abs(number)
    far = jnp.where(positive, edge_left, edge_right)
    cell = jnp.where(positive, cells[2], cells[3])
    curve = 6.0 * (cell - 0.5 * (far + edge))
    return number * (edge - 0.5 * speed * ((edge - far) - (1.0 - 2.0 / 3.0 * speed) * curve))


def pack_kernel(sizes, field, zonal, meridional, mass, target, live, columns, columns_odd, lat_blocks):
    _, levels, rows, width, blocks, capacity, _ = sizes
    fields = sizes.fields
    turned = jnp.concatenate([field[...], zonal[...]], axis=0).T
    columns[0:HALO] = turned[width - HALO : width]
    columns[HALO : 2 * HALO] = turned[0:HALO]
    columns[2 * HALO :] = jnp.zeros((columns.shape[0] - 2 * HALO, columns.shape[1]), jnp.float32)
    columns_odd[0:8] = columns[...]
    columns_odd[8:] = jnp.zeros((columns_odd.shape[0] - 8, columns.shape[1]), jnp.float32)
    spots = row_of(target[...])
    row_hot = one_hot(spots // width, rows)
    column_hot = one_hot(lax.rem(spots, width), width).astype(jnp.bfloat16)
    picked = sum(dot(part, column_hot) for part in three_parts(mass[...]))
    picked = jnp.sum(
        picked.reshape(levels, rows, spots.shape[1]) * row_hot[None], axis=1
    ) * live_row(live[...], capacity)
    here = lax.axis_index("lat")
    for block in range(blocks):
        part = picked[:, block * capacity : (block + 1) * capacity]
        lat_blocks[block, pl.ds(sizes.halo_rows, levels), :] = jnp.concatenate(
            [part] * sizes.sides, axis=1
        )

        @pl.when(block > here)
        def northward():
            for i in range(HALO):
                lat_blocks[block, pl.ds(i * fields, fields), :] = field[
                    pl.ds(rows - HALO + i, fields, stride=rows), :
                ]
            lat_blocks[block, pl.ds(HALO * fields, levels), :] = jnp.zeros(
                (levels, width), jnp.float32
            )

        @pl.when(block <= here)
        def southward():
            for i in range(HALO):
                lat_blocks[block, pl.ds(i * fields, fields), :] = field[
                    pl.ds(i, fields, stride=rows), :
                ]
            lat_blocks[block, pl.ds(HALO * fields, levels), :] = meridional[
                pl.ds(0, levels, stride=rows), :
            ]


def main_kernel(
    sizes, field, zonal, meridional, mass, columns, odd_pairs, even_pairs, from_lat,
    donor, fraction, target, live, advected, outgoing, edge_rows, flux_rows,
):
    tracers, levels, rows, width, blocks, capacity, _ = sizes
    fields, span, total = sizes.fields, levels * rows, sizes.fields * rows
    even = lax.rem(lax.axis_index("lon"), 2) == 0
    from_west = jnp.where(even, odd_pairs[0:HALO], even_pairs[0:HALO])
    from_east = jnp.where(even, even_pairs[HALO : 2 * HALO], odd_pairs[HALO : 2 * HALO])
    east_cells = [from_east[i : i + 1, :total] for i in range(HALO)]
    own_cells = [columns[i : i + 1, :total] for i in range(HALO)]
    east_number = jnp.concatenate([from_east[0:1, total:]] * tracers, axis=1)
    east_flux = face_flux(own_cells + east_cells, east_number)
    lanes = jnp.concatenate(
        [
            *east_cells,
            east_flux,
            jnp.zeros((width - 2 * HALO - 1, total), jnp.float32),
            from_west[0:HALO, :total],
        ],
        axis=0,
    ).T
    here = lax.axis_index("lat")
    south, north = jnp.maximum(here - 1, 0), jnp.minimum(here + 1, blocks - 1)
    has_south, has_north = here > 0, here < blocks - 1
    next_rows = []
    for i in range(HALO):
        part = pl.ds(i * fields, fields)
        south_row = jnp.where(has_south, from_lat[south, part, :], 0.0)
        north_row = jnp.where(has_north, from_lat[north, part, :], 0.0)
        next_rows.append(north_row)
        edge_rows[pl.ds(rows - HALO + i, fields, stride=rows), :] = south_row
        edge_rows[pl.ds(i, fields, stride=rows), :] = north_row
    last_rows = [field[pl.ds(rows - HALO + i, fields, stride=rows), :] for i in range(HALO)]
    north_number = jnp.where(has_north, from_lat[north, pl.ds(HALO * fields, levels), :], 0.0)
    flux_rows[pl.ds(0, fields, stride=rows), :] = face_flux(
        last_rows + next_rows, jnp.concatenate([north_number] * tracers, axis=0)
    )
    column = lax.broadcasted_iota(jnp.int32, (span, width), 1)
    row = lax.broadcasted_iota(jnp.int32, (levels, rows, width), 1)

    spots = row_of(target[...])
    row_hit = one_hot(spots // width, rows) * live_row(live[...], capacity)
    column_hot = one_hot(lax.rem(spots, width), width).astype(jnp.bfloat16)
    kept = 1.0 - dot(row_hit.astype(jnp.bfloat16), column_hot, True)
    weights = mass[...].reshape(levels, rows, width)

    starts = row_of(donor[...])
    row_weight = stencil_weights(starts // width, row_of(fraction[0]), rows)
    column_weight = stencil_weights(lax.rem(starts, width), row_of(fraction[1]), width)
    weight_high, weight_low = two_parts(column_weight)

    sums = blocks * sizes.margin_rows
    for block in range(blocks):
        outgoing[pl.ds(sums + 2 * tracers + block * levels, levels), :] = from_lat[
            block, pl.ds(sizes.halo_rows, levels), :
        ]
    for tracer in range(tracers):
        part = pl.ds(tracer * span, span)
        cells = field[part, :]
        halo = lanes[tracer * span : (tracer + 1) * span]
        along = []
        for shift in (3, 2, 1, 0, -1, -2):
            if shift > 0:
                along.append(
                    pltpu.roll(jnp.where(column >= width - shift, halo, cells), shift, 1)
                )
            elif shift < 0:
                along.append(
                    pltpu.roll(jnp.where(column < -shift, halo, cells), width + shift, 1)
                )
            else:
                along.append(cells)
        flux = face_flux(along, zonal[...])
        next_flux = pltpu.roll(
            jnp.where(column == 0, halo[:, HALO : HALO + 1], flux), width - 1, 1
        )
        result = cells - (next_flux - flux)
        cells3 = cells.reshape(levels, rows, width)
        halo3 = edge_rows[part, :].reshape(levels, rows, width)
        along = []
        for shift in (3, 2, 1, 0, -1, -2):
            if shift > 0:
                along.append(pltpu.roll(jnp.where(row >= rows - shift, halo3, cells3), shift, 1))
            elif shift < 0:
                along.append(pltpu.roll(jnp.where(row < -shift, halo3, cells3), rows + shift, 1))
            else:
                along.append(cells3)
        flux = face_flux(along, meridional[...].reshape(levels, rows, width))
        edge3 = flux_rows[part, :].reshape(levels, rows, width)
        next_flux = pltpu.roll(jnp.where(row == 0, edge3, flux), rows - 1, 1)
        result = result.reshape(levels, rows, width) - (next_flux - flux)
        flat = result.reshape(span, width)
        advected[part, :] = flat

        high, low = two_parts(flat)
        across = dot(high, weight_high) + (dot(high, weight_low) + dot(low, weight_high))
        payload = jnp.sum(
            across.reshape(levels, rows, starts.shape[1]) * row_weight[None], axis=1
        )
        base, lane = sizes.spot(tracer)
        for block in range(blocks):
            at = block * capacity
            outgoing[
                pl.ds(block * sizes.margin_rows + base, levels), lane : lane + capacity
            ] = payload[:, at : at + capacity]
        outgoing[sums + tracer : sums + tracer + 1, :] = jnp.sum(
            weights * result * kept[None], axis=(0, 1)
        )[None]
        outgoing[sums + tracers + tracer : sums + tracers + tracer + 1, :] = jnp.sum(
            weights * cells3, axis=(0, 1)
        )[None]


def blocks_kernel(sizes, own, given, lon_blocks):
    tracers, levels, _, width, blocks, capacity, places = sizes
    size = sizes.margin_rows
    sums = pl.ds(blocks * size, 2 * tracers)
    weighed = jnp.zeros((size, width), jnp.float32)
    for block in range(blocks):
        margin = given[pl.ds(block * size, size), :]
        masses = pl.ds(blocks * size + 2 * tracers + block * levels, levels)
        for sent, mass in ((margin, own), (own[pl.ds(block * size, size), :], given)):
            weighed = weighed + sent * jnp.concatenate([mass[masses, :]] * (size // levels), axis=0)
        lon_blocks[block, :, 0:size, :] = jnp.broadcast_to(margin[None], (places, size, width))
    column = lax.broadcasted_iota(jnp.int32, (1, width), 1)
    partial = own[sums, :] + given[sums, :]
    added = []
    for tracer in range(tracers):
        base, lane = sizes.spot(tracer)
        row = jnp.sum(weighed[base : base + levels], axis=0, keepdims=True)
        added.append(jnp.where((column >= lane) & (column < lane + capacity), row, 0.0))
    partial = partial + jnp.concatenate(
        added + [jnp.zeros((tracers, width), jnp.float32)], axis=0
    )
    lon_blocks[:, :, size:, :] = jnp.broadcast_to(
        partial[None, None], (blocks, places, 2 * tracers, width)
    )


def fill_kernel(sizes, advected, incoming, target, live, updated):
    tracers, levels, rows, width, blocks, capacity, _ = sizes
    size = sizes.margin_rows
    place = lax.axis_index("lon")
    arrived = []
    for block in range(blocks):
        piece = incoming[block, place, 0:size, :]
        arrived.append(
            jnp.concatenate(
                [piece[:, i * capacity : (i + 1) * capacity] for i in range(sizes.sides)], axis=0
            )
        )
    arrived = jnp.concatenate(arrived, axis=1)
    spots = row_of(target[...])
    row_hit = one_hot(spots // width, rows) * live_row(live[...], capacity)
    column_hot = one_hot(lax.rem(spots, width), width).astype(jnp.bfloat16)
    kept = 1.0 - dot(row_hit.astype(jnp.bfloat16), column_hot, True)
    sums = jnp.sum(incoming[:, :, size:, :], axis=(0, 1))
    sums = jnp.sum(sums, axis=1, keepdims=True)
    scale = sums[tracers:] / sums[:tracers]
    for tracer in range(tracers):
        values = arrived[tracer * levels : (tracer + 1) * levels]
        spread = (values[:, None, :] * row_hit[None]).reshape(levels * rows, -1)
        placed = sum(dot(part, column_hot, True) for part in three_parts(spread))
        old = advected[pl.ds(tracer * levels * rows, levels * rows), :]
        merged = old.reshape(levels, rows, width) * kept[None] + placed.reshape(
            levels, rows, width
        )
        updated[0, tracer] = merged * scale[tracer : tracer + 1].reshape(1, 1, 1)


def exchanged(value, axis, first):
    pairs = []
    for i in range(first, lax.axis_size(axis) - 1, 2):
        pairs += [(i, i + 1), (i + 1, i)]
    return lax.ppermute(value, axis, pairs)


def body(
    tracers, courant_lon, courant_lat, cell_mass, donor_cell, donor_frac, target_cell, live_count
):
    sizes = Sizes(*tracers.shape[1:], *donor_cell.shape[3:], lax.axis_size("lon"))
    _, levels, rows, width, blocks, capacity, places = sizes
    fields = sizes.fields
    field = tracers.reshape(fields * rows, width)
    zonal = courant_lon.reshape(levels * rows, width)
    meridional = courant_lat.reshape(levels * rows, width)
    mass = cell_mass.reshape(levels * rows, width)
    donor = donor_cell.reshape(blocks, capacity)
    fraction = donor_frac.reshape(2, blocks, capacity)
    target = target_cell.reshape(blocks, capacity)
    live = live_count.reshape(1, blocks)

    def shape(*dims):
        return pltpu.VMEM(dims, jnp.float32)

    def near(*values):
        return (pltpu.with_memory_space_constraint(value, pltpu.VMEM) for value in values)

    columns, columns_odd, lat_blocks = pl.pallas_call(
        functools.partial(pack_kernel, sizes),
        out_shape=(
            shape(8, (fields + levels) * rows),
            shape(32, (fields + levels) * rows),
            shape(blocks, sizes.halo_rows + levels, width),
        ),
        name="pack_edges",
    )(field, zonal, meridional, mass, target, live)
    from_lat = lax.all_to_all(lat_blocks, "lat", 0, 0, tiled=True)
    odd_pairs = exchanged(columns_odd, "lon", 1)
    even_pairs = exchanged(columns, "lon", 0)
    from_lat, odd_pairs, even_pairs = lax.optimization_barrier((from_lat, odd_pairs, even_pairs))
    payload_rows = sizes.margin_rows + 2 * sizes.tracers
    advected, outgoing = pl.pallas_call(
        functools.partial(main_kernel, sizes),
        out_shape=(
            shape(fields * rows, width),
            shape(blocks * (sizes.margin_rows + levels) + 2 * sizes.tracers, width),
        ),
        scratch_shapes=[
            pltpu.VMEM((fields * rows, width), jnp.float32),
            pltpu.VMEM((fields * rows, width), jnp.float32),
        ],
        name="advect_and_interpolate",
    )(
        *near(
            field, zonal, meridional, mass, columns, odd_pairs, even_pairs, from_lat,
            donor, fraction, target, live,
        )
    )
    given = lax.ppermute(outgoing, "panel", [(0, 1), (1, 0)])
    lon_blocks = pl.pallas_call(
        functools.partial(blocks_kernel, sizes),
        out_shape=shape(blocks, places, payload_rows, width),
        name="margin_blocks",
    )(*near(outgoing, given))
    incoming = lax.all_to_all(
        lon_blocks.reshape(blocks * places, payload_rows, width), ("lat", "lon"), 0, 0, tiled=True
    ).reshape(blocks, places, payload_rows, width)
    return pl.pallas_call(
        functools.partial(fill_kernel, sizes),
        out_shape=jax.ShapeDtypeStruct((1, sizes.tracers, levels, rows, width), jnp.float32),
        name="fill_and_scale",
    )(*near(advected, incoming, target, live))


def solution(mesh):
    in_specs = (
        P("panel", None, None, "lat", "lon"),
        P("panel", None, "lat", "lon"),
        P("panel", None, "lat", "lon"),
        P("panel", None, "lat", "lon"),
        P("panel", "lat", "lon", None, None),
        P(None, "panel", "lat", "lon", None, None),
        P("panel", "lat", "lon", None, None),
        P("panel", "lat", "lon", None),
    )
    out_specs = P("panel", None, None, "lat", "lon")
    return jax.shard_map(body, mesh=mesh, in_specs=in_specs, out_specs=out_specs, check_vma=False)
```

```python
import functools
from typing import NamedTuple

import jax
import jax.numpy as jnp
from jax import lax
from jax.experimental import pallas as pl
from jax.experimental.pallas import tpu as pltpu
from jax.sharding import PartitionSpec as P

HALO = 3


class Sizes(NamedTuple):
    tracers: int
    levels: int
    rows: int
    width: int
    blocks: int
    capacity: int
    places: int

    @property
    def fields(self):
        return self.tracers * self.levels

    @property
    def sides(self):
        return self.width // self.capacity

    @property
    def margin_rows(self):
        return self.fields // self.sides

    @property
    def halo_rows(self):
        return HALO * self.fields + self.levels

    def spot(self, tracer):
        start = tracer * self.levels
        return start % self.margin_rows, start // self.margin_rows * self.capacity


def row_of(table):
    return jnp.concatenate([table[i : i + 1] for i in range(table.shape[0])], axis=1)


def live_row(live, capacity):
    slots = lax.broadcasted_iota(jnp.int32, (1, capacity), 1)
    return jnp.concatenate(
        [(slots < live[:, i : i + 1]).astype(jnp.float32) for i in range(live.shape[1])], axis=1
    )


def one_hot(spots, extent):
    places = lax.broadcasted_iota(jnp.int32, (extent, spots.shape[1]), 0)
    return (places == spots).astype(jnp.float32)


def two_parts(value):
    high = value.astype(jnp.bfloat16)
    return high, (value - high.astype(jnp.float32)).astype(jnp.bfloat16)


def three_parts(value):
    high = value.astype(jnp.bfloat16)
    rest = value - high.astype(jnp.float32)
    return (high, *two_parts(rest))


def dot(left, right, transposed=False):
    return lax.dot_general(
        left,
        right,
        (((1,), (1 if transposed else 0,)), ((), ())),
        preferred_element_type=jnp.float32,
    )


def cubic_weights(fraction):
    return (
        -fraction * (fraction - 1.0) * (fraction - 2.0) / 6.0,
        (fraction + 1.0) * (fraction - 1.0) * (fraction - 2.0) / 2.0,
        -(fraction + 1.0) * fraction * (fraction - 2.0) / 2.0,
        (fraction + 1.0) * fraction * (fraction - 1.0) / 6.0,
    )


def stencil_weights(start, fraction, extent):
    step = lax.broadcasted_iota(jnp.int32, (extent, start.shape[1]), 0) - start
    spread = jnp.zeros(step.shape, jnp.float32)
    for at, weight in enumerate(cubic_weights(fraction)):
        spread = jnp.where(step == at, weight, spread)
    return spread


def face_flux(cells, number):
    edge_left, edge, edge_right = (
        7.0 / 12.0 * (cells[i + 1] + cells[i + 2]) - 1.0 / 12.0 * (cells[i] + cells[i + 3])
        for i in range(3)
    )
    positive = number > 0.0
    speed = jnp.abs(number)
    far = jnp.where(positive, edge_left, edge_right)
    cell = jnp.where(positive, cells[2], cells[3])
    curve = 6.0 * (cell - 0.5 * (far + edge))
    return number * (edge - 0.5 * speed * ((edge - far) - (1.0 - 2.0 / 3.0 * speed) * curve))


def pack_kernel(
    sizes, field, zonal, meridional, mass, target, live, columns, columns_odd, lat_blocks,
    north_stage, south_stage, mass_stage, sems,
):
    _, levels, rows, width, blocks, capacity, _ = sizes
    fields, halo_rows = sizes.fields, sizes.halo_rows
    here = lax.axis_index("lat")
    for i in range(HALO):
        part = pl.ds(i * fields, fields)
        north_stage[part, :] = field[pl.ds(rows - HALO + i, fields, stride=rows), :]
        south_stage[part, :] = field[pl.ds(i, fields, stride=rows), :]
    south_stage[pl.ds(HALO * fields, levels), :] = meridional[pl.ds(0, levels, stride=rows), :]
    north = jnp.minimum(here + 1, blocks - 1)
    south = jnp.maximum(here - 1, 0)
    copies = [
        pltpu.make_async_copy(
            north_stage, lat_blocks.at[north, pl.ds(0, HALO * fields)], sems.at[0]
        ),
        pltpu.make_async_copy(south_stage, lat_blocks.at[south, pl.ds(0, halo_rows)], sems.at[1]),
    ]
    for copy in copies:
        copy.start()
    spots = row_of(target[...])
    row_hot = one_hot(spots // width, rows)
    column_hot = one_hot(lax.rem(spots, width), width).astype(jnp.bfloat16)
    picked = sum(dot(part, column_hot) for part in three_parts(mass[...]))
    picked = jnp.sum(
        picked.reshape(levels, rows, spots.shape[1]) * row_hot[None], axis=1
    ) * live_row(live[...], capacity)
    for block in range(blocks):
        part = picked[:, block * capacity : (block + 1) * capacity]
        mass_stage[block] = jnp.concatenate([part] * sizes.sides, axis=1)
    copy = pltpu.make_async_copy(
        mass_stage, lat_blocks.at[:, pl.ds(halo_rows, levels)], sems.at[2]
    )
    copy.start()
    copies.append(copy)
    turned = jnp.concatenate([field[...], zonal[...]], axis=0).T
    edges = jnp.concatenate(
        [
            turned[width - HALO : width],
            turned[0:HALO],
            jnp.zeros((columns.shape[0] - 2 * HALO, columns.shape[1]), jnp.float32),
        ],
        axis=0,
    )
    columns[...] = edges
    columns_odd[0 : columns.shape[0]] = edges
    columns_odd[columns.shape[0] :] = jnp.zeros(
        (columns_odd.shape[0] - columns.shape[0], columns.shape[1]), jnp.float32
    )
    for copy in copies:
        copy.wait()


def tables_kernel(
    sizes, donor, fraction, target, live, kept, row_hit, column_hot, row_weight, high, low
):
    _, _, rows, width, _, capacity, _ = sizes
    spots = row_of(target[...])
    row_hit[...] = one_hot(spots // width, rows) * live_row(live[...], capacity)
    column_hot[...] = one_hot(lax.rem(spots, width), width).astype(jnp.bfloat16)
    kept[...] = 1.0 - dot(row_hit[...].astype(jnp.bfloat16), column_hot[...], True)
    starts = row_of(donor[...])
    row_weight[...] = stencil_weights(starts // width, row_of(fraction[0]), rows)
    high[...], low[...] = two_parts(
        stencil_weights(lax.rem(starts, width), row_of(fraction[1]), width)
    )


def main_kernel(
    sizes, field, zonal, meridional, mass, columns, odd_pairs, even_pairs, from_lat,
    kept, row_weight, weight_high, weight_low, advected, outgoing, edge_rows, flux_rows,
):
    tracers, levels, rows, width, blocks, capacity, _ = sizes
    fields, span, total = sizes.fields, levels * rows, sizes.fields * rows
    even = lax.rem(lax.axis_index("lon"), 2) == 0
    from_west = jnp.where(even, odd_pairs[0:HALO], even_pairs[0:HALO])
    from_east = jnp.where(even, even_pairs[HALO : 2 * HALO], odd_pairs[HALO : 2 * HALO])
    east_cells = [from_east[i : i + 1, :total] for i in range(HALO)]
    own_cells = [columns[i : i + 1, :total] for i in range(HALO)]
    east_number = jnp.concatenate([from_east[0:1, total:]] * tracers, axis=1)
    east_flux = face_flux(own_cells + east_cells, east_number)
    lanes = jnp.concatenate(
        [
            *east_cells,
            east_flux,
            jnp.zeros((width - 2 * HALO - 1, total), jnp.float32),
            from_west[0:HALO, :total],
        ],
        axis=0,
    ).T
    here = lax.axis_index("lat")
    south, north = jnp.maximum(here - 1, 0), jnp.minimum(here + 1, blocks - 1)
    has_south, has_north = here > 0, here < blocks - 1
    next_rows = []
    for i in range(HALO):
        part = pl.ds(i * fields, fields)
        south_row = jnp.where(has_south, from_lat[south, part, :], 0.0)
        north_row = jnp.where(has_north, from_lat[north, part, :], 0.0)
        next_rows.append(north_row)
        edge_rows[pl.ds(rows - HALO + i, fields, stride=rows), :] = south_row
        edge_rows[pl.ds(i, fields, stride=rows), :] = north_row
    last_rows = [field[pl.ds(rows - HALO + i, fields, stride=rows), :] for i in range(HALO)]
    north_number = jnp.where(has_north, from_lat[north, pl.ds(HALO * fields, levels), :], 0.0)
    flux_rows[pl.ds(0, fields, stride=rows), :] = face_flux(
        last_rows + next_rows, jnp.concatenate([north_number] * tracers, axis=0)
    )
    column = lax.broadcasted_iota(jnp.int32, (span, width), 1)
    row = lax.broadcasted_iota(jnp.int32, (levels, rows, width), 1)

    weights = mass[...].reshape(levels, rows, width)
    sums = blocks * sizes.margin_rows
    for block in range(blocks):
        outgoing[pl.ds(sums + 2 * tracers + block * levels, levels), :] = from_lat[
            block, pl.ds(sizes.halo_rows, levels), :
        ]
    for tracer in range(tracers):
        part = pl.ds(tracer * span, span)
        cells = field[part, :]
        halo = lanes[tracer * span : (tracer + 1) * span]
        along = []
        for shift in (3, 2, 1, 0, -1, -2):
            if shift > 0:
                along.append(
                    pltpu.roll(jnp.where(column >= width - shift, halo, cells), shift, 1)
                )
            elif shift < 0:
                along.append(
                    pltpu.roll(jnp.where(column < -shift, halo, cells), width + shift, 1)
                )
            else:
                along.append(cells)
        flux = face_flux(along, zonal[...])
        next_flux = pltpu.roll(
            jnp.where(column == 0, halo[:, HALO : HALO + 1], flux), width - 1, 1
        )
        result = cells - (next_flux - flux)
        cells3 = cells.reshape(levels, rows, width)
        halo3 = edge_rows[part, :].reshape(levels, rows, width)
        along = []
        for shift in (3, 2, 1, 0, -1, -2):
            if shift > 0:
                along.append(pltpu.roll(jnp.where(row >= rows - shift, halo3, cells3), shift, 1))
            elif shift < 0:
                along.append(pltpu.roll(jnp.where(row < -shift, halo3, cells3), rows + shift, 1))
            else:
                along.append(cells3)
        flux = face_flux(along, meridional[...].reshape(levels, rows, width))
        edge3 = flux_rows[part, :].reshape(levels, rows, width)
        next_flux = pltpu.roll(jnp.where(row == 0, edge3, flux), rows - 1, 1)
        result = result.reshape(levels, rows, width) - (next_flux - flux)
        flat = result.reshape(span, width)
        remaining = result * kept[...][None]
        advected[part, :] = remaining.reshape(span, width)

        high, low = two_parts(flat)
        across = dot(high, weight_high[...]) + (
            dot(high, weight_low[...]) + dot(low, weight_high[...])
        )
        payload = jnp.sum(across.reshape(levels, rows, -1) * row_weight[...][None], axis=1)
        base, lane = sizes.spot(tracer)
        for block in range(blocks):
            at = block * capacity
            outgoing[
                pl.ds(block * sizes.margin_rows + base, levels), lane : lane + capacity
            ] = payload[:, at : at + capacity]
        outgoing[sums + tracer : sums + tracer + 1, :] = jnp.sum(
            weights * remaining, axis=(0, 1)
        )[None]
        outgoing[sums + tracers + tracer : sums + tracers + tracer + 1, :] = jnp.sum(
            weights * cells3, axis=(0, 1)
        )[None]


def blocks_kernel(sizes, own, given, lon_blocks):
    tracers, levels, _, width, blocks, capacity, places = sizes
    size = sizes.margin_rows
    sums = pl.ds(blocks * size, 2 * tracers)
    weighed = jnp.zeros((size, width), jnp.float32)
    for block in range(blocks):
        margin = given[pl.ds(block * size, size), :]
        masses = pl.ds(blocks * size + 2 * tracers + block * levels, levels)
        for sent, mass in ((margin, own), (own[pl.ds(block * size, size), :], given)):
            weighed = weighed + sent * jnp.concatenate([mass[masses, :]] * (size // levels), axis=0)
        for place in range(places):
            lon_blocks[pl.ds((block * places + place) * (size + 1), size), :] = margin
    column = lax.broadcasted_iota(jnp.int32, (1, width), 1)
    partial = own[sums, :] + given[sums, :]
    added = []
    for tracer in range(tracers):
        base, lane = sizes.spot(tracer)
        row = jnp.sum(weighed[base : base + levels], axis=0, keepdims=True)
        added.append(jnp.where((column >= lane) & (column < lane + capacity), row, 0.0))
    partial = partial + jnp.concatenate(
        added + [jnp.zeros((tracers, width), jnp.float32)], axis=0
    )
    totals = jnp.sum(partial, axis=1, keepdims=True)
    line = jnp.zeros((1, width), jnp.float32)
    for i in range(2 * tracers):
        line = jnp.where(column == i, totals[i : i + 1], line)
    for block in range(blocks * places):
        lon_blocks[pl.ds(block * (size + 1) + size, 1), :] = line


def fill_kernel(sizes, advected, incoming, row_hit, column_hot, updated):
    tracers, levels, rows, width, blocks, capacity, places = sizes
    size = sizes.margin_rows
    place = lax.axis_index("lon")
    arrived = []
    for block in range(blocks):
        piece = incoming[pl.ds((block * places + place) * (size + 1), size), :]
        arrived.append(
            jnp.concatenate(
                [piece[:, i * capacity : (i + 1) * capacity] for i in range(sizes.sides)], axis=0
            )
        )
    arrived = jnp.concatenate(arrived, axis=1)
    line = jnp.sum(
        incoming[pl.ds(size, blocks * places, stride=size + 1), :], axis=0, keepdims=True
    )
    for tracer in range(tracers):
        values = arrived[tracer * levels : (tracer + 1) * levels]
        spread = (values[:, None, :] * row_hit[...][None]).reshape(levels * rows, -1)
        placed = sum(dot(part, column_hot[...], True) for part in three_parts(spread))
        old = advected[pl.ds(tracer * levels * rows, levels * rows), :]
        scale = line[:, tracers + tracer : tracers + tracer + 1] / line[:, tracer : tracer + 1]
        updated[0, tracer] = ((old + placed) * scale).reshape(levels, rows, width)


def exchanged(value, axis, first):
    pairs = []
    for i in range(first, lax.axis_size(axis) - 1, 2):
        pairs += [(i, i + 1), (i + 1, i)]
    return lax.ppermute(value, axis, pairs)


def body(
    tracers, courant_lon, courant_lat, cell_mass, donor_cell, donor_frac, target_cell, live_count
):
    sizes = Sizes(*tracers.shape[1:], *donor_cell.shape[3:], lax.axis_size("lon"))
    _, levels, rows, width, blocks, capacity, places = sizes
    fields = sizes.fields
    field = tracers.reshape(fields * rows, width)
    zonal = courant_lon.reshape(levels * rows, width)
    meridional = courant_lat.reshape(levels * rows, width)
    mass = cell_mass.reshape(levels * rows, width)
    donor = donor_cell.reshape(blocks, capacity)
    fraction = donor_frac.reshape(2, blocks, capacity)
    target = target_cell.reshape(blocks, capacity)
    live = live_count.reshape(1, blocks)

    def shape(*dims):
        return pltpu.VMEM(dims, jnp.float32)

    def near(*values):
        return (pltpu.with_memory_space_constraint(value, pltpu.VMEM) for value in values)

    slots = blocks * capacity
    columns, columns_odd, lat_blocks = pl.pallas_call(
        functools.partial(pack_kernel, sizes),
        out_shape=(
            shape(8, (fields + levels) * rows),
            shape(32, (fields + levels) * rows),
            jax.ShapeDtypeStruct((blocks, sizes.halo_rows + levels, width), jnp.float32),
        ),
        out_specs=(
            pl.BlockSpec(memory_space=pltpu.VMEM),
            pl.BlockSpec(memory_space=pltpu.VMEM),
            pl.BlockSpec(memory_space=pl.ANY),
        ),
        scratch_shapes=[
            pltpu.VMEM((HALO * fields, width), jnp.float32),
            pltpu.VMEM((sizes.halo_rows, width), jnp.float32),
            pltpu.VMEM((blocks, levels, width), jnp.float32),
            pltpu.SemaphoreType.DMA((3,)),
        ],
        name="pack_edges",
    )(field, zonal, meridional, mass, target, live)
    from_lat = lax.all_to_all(lat_blocks, "lat", 0, 0, tiled=True)
    odd_pairs = exchanged(columns_odd, "lon", 1)
    even_pairs = exchanged(columns, "lon", 0)
    kept, row_hit, column_hot, *weights = pl.pallas_call(
        functools.partial(tables_kernel, sizes),
        out_shape=(
            shape(rows, width),
            shape(rows, slots),
            pltpu.VMEM((width, slots), jnp.bfloat16),
            shape(rows, slots),
            pltpu.VMEM((width, slots), jnp.bfloat16),
            pltpu.VMEM((width, slots), jnp.bfloat16),
        ),
        name="index_tables",
    )(donor, fraction, target, live)
    from_lat, odd_pairs, even_pairs = lax.optimization_barrier((from_lat, odd_pairs, even_pairs))
    advected, outgoing = pl.pallas_call(
        functools.partial(main_kernel, sizes),
        out_shape=(
            shape(fields * rows, width),
            shape(blocks * (sizes.margin_rows + levels) + 2 * sizes.tracers, width),
        ),
        scratch_shapes=[
            pltpu.VMEM((fields * rows, width), jnp.float32),
            pltpu.VMEM((fields * rows, width), jnp.float32),
        ],
        name="advect_and_interpolate",
    )(
        *near(
            field, zonal, meridional, mass, columns, odd_pairs, even_pairs, from_lat,
            kept, *weights,
        )
    )
    given = lax.ppermute(outgoing, "panel", [(0, 1), (1, 0)])
    block_rows = sizes.margin_rows + 1
    lon_blocks = pl.pallas_call(
        functools.partial(blocks_kernel, sizes),
        out_shape=shape(blocks * places * block_rows, width),
        name="margin_blocks",
    )(*near(outgoing, given))
    incoming = lax.all_to_all(
        lon_blocks.reshape(blocks * places, 1, block_rows * width), ("lat", "lon"), 0, 0, tiled=True
    ).reshape(blocks * places * block_rows, width)
    return pl.pallas_call(
        functools.partial(fill_kernel, sizes),
        out_shape=jax.ShapeDtypeStruct((1, sizes.tracers, levels, rows, width), jnp.float32),
        name="fill_and_scale",
    )(*near(advected, incoming, row_hit, column_hot))


def solution(mesh):
    in_specs = (
        P("panel", None, None, "lat", "lon"),
        P("panel", None, "lat", "lon"),
        P("panel", None, "lat", "lon"),
        P("panel", None, "lat", "lon"),
        P("panel", "lat", "lon", None, None),
        P(None, "panel", "lat", "lon", None, None),
        P("panel", "lat", "lon", None, None),
        P("panel", "lat", "lon", None),
    )
    out_specs = P("panel", None, None, "lat", "lon")
    return jax.shard_map(body, mesh=mesh, in_specs=in_specs, out_specs=out_specs, check_vma=False)
```

```python
import functools
from typing import NamedTuple

import jax
import jax.numpy as jnp
from jax import lax
from jax.experimental import pallas as pl
from jax.experimental.pallas import tpu as pltpu
from jax.sharding import PartitionSpec as P

HALO = 3
MASS_ROWS = 64


class Sizes(NamedTuple):
    tracers: int
    levels: int
    rows: int
    width: int
    blocks: int
    capacity: int
    places: int

    @property
    def fields(self):
        return self.tracers * self.levels

    @property
    def sides(self):
        return self.width // self.capacity

    @property
    def margin_rows(self):
        return self.fields // self.sides

    @property
    def halo_rows(self):
        return HALO * self.fields + self.levels

    def spot(self, tracer):
        start = tracer * self.levels
        return start % self.margin_rows, start // self.margin_rows * self.capacity


def row_of(table):
    return jnp.concatenate([table[i : i + 1] for i in range(table.shape[0])], axis=1)


def live_row(live, capacity):
    slots = lax.broadcasted_iota(jnp.int32, (1, capacity), 1)
    return jnp.concatenate(
        [(slots < live[:, i : i + 1]).astype(jnp.float32) for i in range(live.shape[1])], axis=1
    )


def one_hot(spots, extent):
    places = lax.broadcasted_iota(jnp.int32, (extent, spots.shape[1]), 0)
    return (places == spots).astype(jnp.float32)


def two_parts(value):
    high = value.astype(jnp.bfloat16)
    return high, (value - high.astype(jnp.float32)).astype(jnp.bfloat16)


def three_parts(value):
    high = value.astype(jnp.bfloat16)
    rest = value - high.astype(jnp.float32)
    return (high, *two_parts(rest))


def dot(left, right, transposed=False):
    return lax.dot_general(
        left,
        right,
        (((1,), (1 if transposed else 0,)), ((), ())),
        preferred_element_type=jnp.float32,
    )


def cubic_weights(fraction):
    return (
        -fraction * (fraction - 1.0) * (fraction - 2.0) / 6.0,
        (fraction + 1.0) * (fraction - 1.0) * (fraction - 2.0) / 2.0,
        -(fraction + 1.0) * fraction * (fraction - 2.0) / 2.0,
        (fraction + 1.0) * fraction * (fraction - 1.0) / 6.0,
    )


def stencil_weights(start, fraction, extent):
    step = lax.broadcasted_iota(jnp.int32, (extent, start.shape[1]), 0) - start
    spread = jnp.zeros(step.shape, jnp.float32)
    for at, weight in enumerate(cubic_weights(fraction)):
        spread = jnp.where(step == at, weight, spread)
    return spread


def face_flux(cells, number):
    edge_left, edge, edge_right = (
        7.0 / 12.0 * (cells[i + 1] + cells[i + 2]) - 1.0 / 12.0 * (cells[i] + cells[i + 3])
        for i in range(3)
    )
    positive = number > 0.0
    speed = jnp.abs(number)
    far = jnp.where(positive, edge_left, edge_right)
    cell = jnp.where(positive, cells[2], cells[3])
    curve = 6.0 * (cell - 0.5 * (far + edge))
    return number * (edge - 0.5 * speed * ((edge - far) - (1.0 - 2.0 / 3.0 * speed) * curve))


def pack_kernel(
    sizes, field, zonal, meridional, mass, target, live, donor, fraction,
    columns, columns_odd, lat_even, lat_odd, masses, *index_copies,
):
    _, levels, rows, width, blocks, capacity, _ = sizes
    fields = sizes.fields
    here = lax.axis_index("lat")
    for copy, source in zip(index_copies, (donor, fraction, target, live), strict=True):
        copy[...] = source[...]
    even = lax.rem(here, 2) == 0
    for i in range(HALO):
        part = pl.ds(i * fields, fields)
        northward = field[pl.ds(rows - HALO + i, fields, stride=rows), :]
        southward = field[pl.ds(i, fields, stride=rows), :]
        lat_even[part, :] = jnp.where(even, northward, southward)
        lat_odd[part, :] = jnp.where(even, southward, northward)
    number = meridional[pl.ds(0, levels, stride=rows), :]
    lat_even[pl.ds(HALO * fields, levels), :] = number
    lat_odd[pl.ds(HALO * fields, levels), :] = number
    spots = row_of(target[...])
    row_hot = one_hot(spots // width, rows)
    column_hot = one_hot(lax.rem(spots, width), width).astype(jnp.bfloat16)
    picked = sum(dot(part, column_hot) for part in three_parts(mass[...]))
    picked = jnp.sum(
        picked.reshape(levels, rows, spots.shape[1]) * row_hot[None], axis=1
    ) * live_row(live[...], capacity)
    for block in range(blocks):
        part = picked[:, block * capacity : (block + 1) * capacity]
        masses[pl.ds(block * levels, levels), :] = jnp.concatenate([part] * sizes.sides, axis=1)
    if two_hops(sizes):
        for i, step in enumerate((1, 3)):
            block = pl.multiple_of((here ^ step) * levels, levels)
            lat_even[pl.ds(sizes.halo_rows + i * levels, levels), :] = masses[
                pl.ds(block, levels), :
            ]
    turned = jnp.concatenate([field[...], zonal[...]], axis=0).T
    edges = jnp.concatenate(
        [
            turned[width - HALO : width],
            turned[0:HALO],
            jnp.zeros((columns.shape[0] - 2 * HALO, columns.shape[1]), jnp.float32),
        ],
        axis=0,
    )
    columns[...] = edges
    columns_odd[0 : columns.shape[0]] = edges
    columns_odd[columns.shape[0] :] = jnp.zeros(
        (columns_odd.shape[0] - columns.shape[0], columns.shape[1]), jnp.float32
    )


def two_hops(sizes):
    return sizes.blocks == 4


def forward_kernel(sizes, masses, lat_even, forwarded):
    levels = sizes.levels
    block = pl.multiple_of((lax.axis_index("lat") ^ 2) * levels, levels)
    forwarded[0:levels, :] = masses[pl.ds(block, levels), :]
    forwarded[levels:, :] = lat_even[pl.ds(sizes.halo_rows + levels, levels), :]


def masses_kernel(sizes, masses, lat_even, forwarded, received):
    levels = sizes.levels
    here = lax.axis_index("lat")
    own = pl.multiple_of(here * levels, levels)
    pieces = (
        masses[pl.ds(own, levels), :],
        lat_even[pl.ds(sizes.halo_rows, levels), :],
        forwarded[0:levels, :],
        forwarded[levels:, :],
    )
    spare = received.shape[0] - len(pieces) * levels
    received[pl.ds(len(pieces) * levels, spare), :] = jnp.zeros((spare, sizes.width), jnp.float32)
    for step, piece in enumerate(pieces):
        received[pl.ds(pl.multiple_of((here ^ step) * levels, levels), levels), :] = piece


def tables_kernel(
    sizes, donor, fraction, target, live, kept, row_hit, column_hot, row_weight, high, low
):
    _, _, rows, width, _, capacity, _ = sizes
    spots = row_of(target[...])
    row_hit[...] = one_hot(spots // width, rows) * live_row(live[...], capacity)
    column_hot[...] = one_hot(lax.rem(spots, width), width).astype(jnp.bfloat16)
    kept[...] = 1.0 - dot(row_hit[...].astype(jnp.bfloat16), column_hot[...], True)
    starts = row_of(donor[...])
    row_weight[...] = stencil_weights(starts // width, row_of(fraction[0]), rows)
    high[...], low[...] = two_parts(
        stencil_weights(lax.rem(starts, width), row_of(fraction[1]), width)
    )


def main_kernel(
    sizes, field, zonal, meridional, mass, columns, odd_pairs, even_pairs, lat_odd, lat_even,
    kept, row_weight, weight_high, weight_low, advected, outgoing, edge_rows, flux_rows,
):
    tracers, levels, rows, width, blocks, capacity, _ = sizes
    fields, span, total = sizes.fields, levels * rows, sizes.fields * rows
    even = lax.rem(lax.axis_index("lon"), 2) == 0
    from_west = jnp.where(even, odd_pairs[0:HALO], even_pairs[0:HALO])
    from_east = jnp.where(even, even_pairs[HALO : 2 * HALO], odd_pairs[HALO : 2 * HALO])
    east_cells = [from_east[i : i + 1, :total] for i in range(HALO)]
    own_cells = [columns[i : i + 1, :total] for i in range(HALO)]
    east_number = jnp.concatenate([from_east[0:1, total:]] * tracers, axis=1)
    east_flux = face_flux(own_cells + east_cells, east_number)
    lanes = jnp.concatenate(
        [
            *east_cells,
            east_flux,
            jnp.zeros((width - 2 * HALO - 1, total), jnp.float32),
            from_west[0:HALO, :total],
        ],
        axis=0,
    ).T
    even = lax.rem(lax.axis_index("lat"), 2) == 0
    next_rows = []
    for i in range(HALO):
        part = pl.ds(i * fields, fields)
        first, second = lat_even[part, :], lat_odd[part, :]
        north_row = jnp.where(even, first, second)
        next_rows.append(north_row)
        edge_rows[pl.ds(rows - HALO + i, fields, stride=rows), :] = jnp.where(even, second, first)
        edge_rows[pl.ds(i, fields, stride=rows), :] = north_row
    last_rows = [field[pl.ds(rows - HALO + i, fields, stride=rows), :] for i in range(HALO)]
    part = pl.ds(HALO * fields, levels)
    north_number = jnp.where(even, lat_even[part, :], lat_odd[part, :])
    flux_rows[pl.ds(0, fields, stride=rows), :] = face_flux(
        last_rows + next_rows, jnp.concatenate([north_number] * tracers, axis=0)
    )
    column = lax.broadcasted_iota(jnp.int32, (span, width), 1)
    row = lax.broadcasted_iota(jnp.int32, (levels, rows, width), 1)

    weights = mass[...].reshape(levels, rows, width)
    sums = blocks * sizes.margin_rows
    for tracer in range(tracers):
        part = pl.ds(tracer * span, span)
        cells = field[part, :]
        halo = lanes[tracer * span : (tracer + 1) * span]
        along = []
        for shift in (3, 2, 1, 0, -1, -2):
            if shift > 0:
                along.append(
                    pltpu.roll(jnp.where(column >= width - shift, halo, cells), shift, 1)
                )
            elif shift < 0:
                along.append(
                    pltpu.roll(jnp.where(column < -shift, halo, cells), width + shift, 1)
                )
            else:
                along.append(cells)
        flux = face_flux(along, zonal[...])
        next_flux = pltpu.roll(
            jnp.where(column == 0, halo[:, HALO : HALO + 1], flux), width - 1, 1
        )
        result = cells - (next_flux - flux)
        cells3 = cells.reshape(levels, rows, width)
        halo3 = edge_rows[part, :].reshape(levels, rows, width)
        along = []
        for shift in (3, 2, 1, 0, -1, -2):
            if shift > 0:
                along.append(pltpu.roll(jnp.where(row >= rows - shift, halo3, cells3), shift, 1))
            elif shift < 0:
                along.append(pltpu.roll(jnp.where(row < -shift, halo3, cells3), rows + shift, 1))
            else:
                along.append(cells3)
        flux = face_flux(along, meridional[...].reshape(levels, rows, width))
        edge3 = flux_rows[part, :].reshape(levels, rows, width)
        next_flux = pltpu.roll(jnp.where(row == 0, edge3, flux), rows - 1, 1)
        result = result.reshape(levels, rows, width) - (next_flux - flux)
        flat = result.reshape(span, width)
        remaining = result * kept[...][None]
        advected[part, :] = remaining.reshape(span, width)

        high, low = two_parts(flat)
        across = dot(high, weight_high[...]) + (
            dot(high, weight_low[...]) + dot(low, weight_high[...])
        )
        payload = jnp.sum(across.reshape(levels, rows, -1) * row_weight[...][None], axis=1)
        base, lane = sizes.spot(tracer)
        for block in range(blocks):
            at = block * capacity
            outgoing[
                pl.ds(block * sizes.margin_rows + base, levels), lane : lane + capacity
            ] = payload[:, at : at + capacity]
        outgoing[sums + tracer : sums + tracer + 1, :] = jnp.sum(
            weights * remaining, axis=(0, 1)
        )[None]
        outgoing[sums + tracers + tracer : sums + tracers + tracer + 1, :] = jnp.sum(
            weights * cells3, axis=(0, 1)
        )[None]


def blocks_kernel(sizes, own, given, own_masses, given_masses, lon_blocks):
    tracers, levels, _, width, blocks, capacity, places = sizes
    size = sizes.margin_rows
    sums = pl.ds(blocks * size, 2 * tracers)
    weighed = jnp.zeros((size, width), jnp.float32)
    for block in range(blocks):
        margin = given[pl.ds(block * size, size), :]
        part = pl.ds(block * levels, levels)
        for sent, mass in (
            (margin, own_masses[part, :]),
            (own[pl.ds(block * size, size), :], given_masses[part, :]),
        ):
            weighed = weighed + sent * jnp.concatenate([mass] * (size // levels), axis=0)
        for place in range(places):
            lon_blocks[pl.ds((block * places + place) * (size + 1), size), :] = margin
    column = lax.broadcasted_iota(jnp.int32, (1, width), 1)
    partial = own[sums, :] + given[sums, :]
    added = []
    for tracer in range(tracers):
        base, lane = sizes.spot(tracer)
        row = jnp.sum(weighed[base : base + levels], axis=0, keepdims=True)
        added.append(jnp.where((column >= lane) & (column < lane + capacity), row, 0.0))
    partial = partial + jnp.concatenate(
        added + [jnp.zeros((tracers, width), jnp.float32)], axis=0
    )
    totals = jnp.sum(partial, axis=1, keepdims=True)
    line = jnp.zeros((1, width), jnp.float32)
    for i in range(2 * tracers):
        line = jnp.where(column == i, totals[i : i + 1], line)
    for block in range(blocks * places):
        lon_blocks[pl.ds(block * (size + 1) + size, 1), :] = line


def fill_kernel(sizes, advected, incoming, row_hit, column_hot, updated):
    tracers, levels, rows, width, blocks, capacity, places = sizes
    size = sizes.margin_rows
    place = lax.axis_index("lon")
    arrived = []
    for block in range(blocks):
        piece = incoming[pl.ds((block * places + place) * (size + 1), size), :]
        arrived.append(
            jnp.concatenate(
                [piece[:, i * capacity : (i + 1) * capacity] for i in range(sizes.sides)], axis=0
            )
        )
    arrived = jnp.concatenate(arrived, axis=1)
    line = jnp.sum(
        incoming[pl.ds(size, blocks * places, stride=size + 1), :], axis=0, keepdims=True
    )
    for tracer in range(tracers):
        values = arrived[tracer * levels : (tracer + 1) * levels]
        spread = (values[:, None, :] * row_hit[...][None]).reshape(levels * rows, -1)
        placed = sum(dot(part, column_hot[...], True) for part in three_parts(spread))
        old = advected[pl.ds(tracer * levels * rows, levels * rows), :]
        scale = line[:, tracers + tracer : tracers + tracer + 1] / line[:, tracer : tracer + 1]
        updated[0, tracer] = ((old + placed) * scale).reshape(levels, rows, width)


def exchanged(value, axis, first):
    pairs = []
    for i in range(first, lax.axis_size(axis) - 1, 2):
        pairs += [(i, i + 1), (i + 1, i)]
    return lax.ppermute(value, axis, pairs)


def body(
    tracers, courant_lon, courant_lat, cell_mass, donor_cell, donor_frac, target_cell, live_count
):
    sizes = Sizes(*tracers.shape[1:], *donor_cell.shape[3:], lax.axis_size("lon"))
    _, levels, rows, width, blocks, capacity, places = sizes
    fields = sizes.fields
    field = tracers.reshape(fields * rows, width)
    zonal = courant_lon.reshape(levels * rows, width)
    meridional = courant_lat.reshape(levels * rows, width)
    mass = cell_mass.reshape(levels * rows, width)
    donor = donor_cell.reshape(blocks, capacity)
    fraction = donor_frac.reshape(2, blocks, capacity)
    target = target_cell.reshape(blocks, capacity)
    live = live_count.reshape(1, blocks)

    def shape(*dims):
        return pltpu.VMEM(dims, jnp.float32)

    def near(*values):
        return (pltpu.with_memory_space_constraint(value, pltpu.VMEM) for value in values)

    slots = blocks * capacity
    columns, columns_odd, lat_even, lat_odd, masses, *index_copies = pl.pallas_call(
        functools.partial(pack_kernel, sizes),
        out_shape=(
            shape(8, (fields + levels) * rows),
            shape(16, (fields + levels) * rows),
            shape(sizes.halo_rows + (2 * levels if two_hops(sizes) else 0), width),
            shape(sizes.halo_rows, width),
            shape(blocks * levels, width),
            pltpu.VMEM(donor.shape, donor.dtype),
            pltpu.VMEM(fraction.shape, fraction.dtype),
            pltpu.VMEM(target.shape, target.dtype),
            pltpu.VMEM(live.shape, live.dtype),
        ),
        name="pack_edges",
    )(field, zonal, meridional, mass, target, live, donor, fraction)
    lat_even = exchanged(lat_even, "lat", 0)
    odd_pairs = exchanged(columns_odd, "lon", 1)
    lat_odd = exchanged(lat_odd, "lat", 1)
    even_pairs = exchanged(columns, "lon", 0)
    if two_hops(sizes):
        forwarded = pl.pallas_call(
            functools.partial(forward_kernel, sizes),
            out_shape=shape(2 * levels, width),
            name="forward_masses",
        )(*near(masses, lat_even))
        forwarded = lax.ppermute(forwarded, "lat", [(i, i ^ 2) for i in range(blocks)])
        masses = pl.pallas_call(
            functools.partial(masses_kernel, sizes),
            out_shape=shape(MASS_ROWS, width),
            name="gather_masses",
        )(*near(masses, lat_even, forwarded))
    else:
        masses = lax.all_to_all(
            masses.reshape(blocks, levels, width), "lat", 0, 0, tiled=True
        ).reshape(blocks * levels, width)
    given_masses = lax.ppermute(masses, "panel", [(0, 1), (1, 0)])
    kept, row_hit, column_hot, *weights = pl.pallas_call(
        functools.partial(tables_kernel, sizes),
        out_shape=(
            shape(rows, width),
            shape(rows, slots),
            pltpu.VMEM((width, slots), jnp.bfloat16),
            shape(rows, slots),
            pltpu.VMEM((width, slots), jnp.bfloat16),
            pltpu.VMEM((width, slots), jnp.bfloat16),
        ),
        name="index_tables",
    )(*near(*index_copies))
    advected, outgoing = pl.pallas_call(
        functools.partial(main_kernel, sizes),
        out_shape=(
            shape(fields * rows, width),
            shape(blocks * sizes.margin_rows + 2 * sizes.tracers, width),
        ),
        scratch_shapes=[
            pltpu.VMEM((fields * rows, width), jnp.float32),
            pltpu.VMEM((fields * rows, width), jnp.float32),
        ],
        name="advect_and_interpolate",
    )(
        *near(
            field, zonal, meridional, mass, columns, odd_pairs, even_pairs, lat_odd, lat_even,
            kept, *weights,
        )
    )
    given = lax.ppermute(outgoing, "panel", [(0, 1), (1, 0)])
    block_rows = sizes.margin_rows + 1
    lon_blocks = pl.pallas_call(
        functools.partial(blocks_kernel, sizes),
        out_shape=shape(blocks * places * block_rows, width),
        name="margin_blocks",
    )(*near(outgoing, given, masses, given_masses))
    incoming = lax.all_to_all(
        lon_blocks.reshape(blocks * places, 1, block_rows * width), ("lat", "lon"), 0, 0, tiled=True
    ).reshape(blocks * places * block_rows, width)
    return pl.pallas_call(
        functools.partial(fill_kernel, sizes),
        out_shape=jax.ShapeDtypeStruct((1, sizes.tracers, levels, rows, width), jnp.float32),
        name="fill_and_scale",
    )(*near(advected, incoming, row_hit, column_hot))


def solution(mesh):
    in_specs = (
        P("panel", None, None, "lat", "lon"),
        P("panel", None, "lat", "lon"),
        P("panel", None, "lat", "lon"),
        P("panel", None, "lat", "lon"),
        P("panel", "lat", "lon", None, None),
        P(None, "panel", "lat", "lon", None, None),
        P("panel", "lat", "lon", None, None),
        P("panel", "lat", "lon", None),
    )
    out_specs = P("panel", None, None, "lat", "lon")
    return jax.shard_map(body, mesh=mesh, in_specs=in_specs, out_specs=out_specs, check_vma=False)
```

```python
import functools
from typing import NamedTuple

import jax
import jax.numpy as jnp
from jax import lax
from jax.experimental import pallas as pl
from jax.experimental.pallas import tpu as pltpu
from jax.sharding import PartitionSpec as P

HALO = 3
FORWARD_ROWS = 68


class Sizes(NamedTuple):
    tracers: int
    levels: int
    rows: int
    width: int
    blocks: int
    capacity: int
    places: int

    @property
    def fields(self):
        return self.tracers * self.levels

    @property
    def sides(self):
        return self.width // self.capacity

    @property
    def margin_rows(self):
        return self.fields // self.sides

    @property
    def halo_rows(self):
        return HALO * self.fields + self.levels

    def spot(self, tracer):
        start = tracer * self.levels
        return start % self.margin_rows, start // self.margin_rows * self.capacity


def row_of(table):
    return jnp.concatenate([table[i : i + 1] for i in range(table.shape[0])], axis=1)


def live_row(live, capacity):
    slots = lax.broadcasted_iota(jnp.int32, (1, capacity), 1)
    return jnp.concatenate(
        [(slots < live[:, i : i + 1]).astype(jnp.float32) for i in range(live.shape[1])], axis=1
    )


def one_hot(spots, extent):
    places = lax.broadcasted_iota(jnp.int32, (extent, spots.shape[1]), 0)
    return (places == spots).astype(jnp.float32)


def two_parts(value):
    high = value.astype(jnp.bfloat16)
    return high, (value - high.astype(jnp.float32)).astype(jnp.bfloat16)


def three_parts(value):
    high = value.astype(jnp.bfloat16)
    rest = value - high.astype(jnp.float32)
    return (high, *two_parts(rest))


def dot(left, right, transposed=False):
    return lax.dot_general(
        left,
        right,
        (((1,), (1 if transposed else 0,)), ((), ())),
        preferred_element_type=jnp.float32,
    )


def cubic_weights(fraction):
    return (
        -fraction * (fraction - 1.0) * (fraction - 2.0) / 6.0,
        (fraction + 1.0) * (fraction - 1.0) * (fraction - 2.0) / 2.0,
        -(fraction + 1.0) * fraction * (fraction - 2.0) / 2.0,
        (fraction + 1.0) * fraction * (fraction - 1.0) / 6.0,
    )


def stencil_weights(start, fraction, extent):
    step = lax.broadcasted_iota(jnp.int32, (extent, start.shape[1]), 0) - start
    spread = jnp.zeros(step.shape, jnp.float32)
    for at, weight in enumerate(cubic_weights(fraction)):
        spread = jnp.where(step == at, weight, spread)
    return spread


def face_flux(cells, number):
    edge_left, edge, edge_right = (
        7.0 / 12.0 * (cells[i + 1] + cells[i + 2]) - 1.0 / 12.0 * (cells[i] + cells[i + 3])
        for i in range(3)
    )
    positive = number > 0.0
    speed = jnp.abs(number)
    far = jnp.where(positive, edge_left, edge_right)
    cell = jnp.where(positive, cells[2], cells[3])
    curve = 6.0 * (cell - 0.5 * (far + edge))
    return number * (edge - 0.5 * speed * ((edge - far) - (1.0 - 2.0 / 3.0 * speed) * curve))


def pack_kernel(
    sizes, field, zonal, meridional, mass, target, live, donor, fraction,
    columns, columns_odd, lat_even, lat_odd, masses, *index_copies,
):
    _, levels, rows, width, blocks, capacity, _ = sizes
    fields = sizes.fields
    here = lax.axis_index("lat")
    for copy, source in zip(index_copies, (donor, fraction, target, live), strict=True):
        copy[...] = source[...]
    even = lax.rem(here, 2) == 0
    for i in range(HALO):
        part = pl.ds(i * fields, fields)
        northward = field[pl.ds(rows - HALO + i, fields, stride=rows), :]
        southward = field[pl.ds(i, fields, stride=rows), :]
        lat_even[part, :] = jnp.where(even, northward, southward)
        lat_odd[part, :] = jnp.where(even, southward, northward)
    number = meridional[pl.ds(0, levels, stride=rows), :]
    lat_even[pl.ds(HALO * fields, levels), :] = number
    lat_odd[pl.ds(HALO * fields, levels), :] = number
    spots = row_of(target[...])
    row_hot = one_hot(spots // width, rows)
    column_hot = one_hot(lax.rem(spots, width), width).astype(jnp.bfloat16)
    picked = sum(dot(part, column_hot) for part in three_parts(mass[...]))
    picked = jnp.sum(
        picked.reshape(levels, rows, spots.shape[1]) * row_hot[None], axis=1
    ) * live_row(live[...], capacity)
    for block in range(blocks):
        part = picked[:, block * capacity : (block + 1) * capacity]
        masses[pl.ds(block * levels, levels), :] = jnp.concatenate([part] * sizes.sides, axis=1)
    if two_hops(sizes):
        for i, step in enumerate((1, 3)):
            block = pl.multiple_of((here ^ step) * levels, levels)
            lat_even[pl.ds(sizes.halo_rows + i * levels, levels), :] = masses[
                pl.ds(block, levels), :
            ]
    turned = jnp.concatenate([field[...], zonal[...]], axis=0).T
    edges = jnp.concatenate(
        [
            turned[width - HALO : width],
            turned[0:HALO],
            jnp.zeros((columns.shape[0] - 2 * HALO, columns.shape[1]), jnp.float32),
        ],
        axis=0,
    )
    columns[...] = edges
    columns_odd[0 : columns.shape[0]] = edges
    columns_odd[columns.shape[0] :] = jnp.zeros(
        (columns_odd.shape[0] - columns.shape[0], columns.shape[1]), jnp.float32
    )


def two_hops(sizes):
    return sizes.blocks == 4


def forward_kernel(sizes, masses, lat_even, forwarded):
    levels = sizes.levels
    block = pl.multiple_of((lax.axis_index("lat") ^ 2) * levels, levels)
    forwarded[0:levels, :] = masses[pl.ds(block, levels), :]
    forwarded[levels : 2 * levels, :] = lat_even[pl.ds(sizes.halo_rows + levels, levels), :]
    spare = forwarded.shape[0] - 2 * levels
    if spare:
        forwarded[pl.ds(2 * levels, spare), :] = jnp.zeros((spare, sizes.width), jnp.float32)


def masses_kernel(sizes, masses, lat_even, forwarded, received):
    levels = sizes.levels
    here = lax.axis_index("lat")
    own = pl.multiple_of(here * levels, levels)
    pieces = (
        masses[pl.ds(own, levels), :],
        lat_even[pl.ds(sizes.halo_rows, levels), :],
        forwarded[0:levels, :],
        forwarded[levels : 2 * levels, :],
    )
    for step, piece in enumerate(pieces):
        received[pl.ds(pl.multiple_of((here ^ step) * levels, levels), levels), :] = piece


def tables_kernel(
    sizes, donor, fraction, target, live, kept, row_hit, column_hot, row_weight, high, low
):
    _, _, rows, width, _, capacity, _ = sizes
    spots = row_of(target[...])
    row_hit[...] = one_hot(spots // width, rows) * live_row(live[...], capacity)
    column_hot[...] = one_hot(lax.rem(spots, width), width).astype(jnp.bfloat16)
    kept[...] = 1.0 - dot(row_hit[...].astype(jnp.bfloat16), column_hot[...], True)
    starts = row_of(donor[...])
    row_weight[...] = stencil_weights(starts // width, row_of(fraction[0]), rows)
    high[...], low[...] = two_parts(
        stencil_weights(lax.rem(starts, width), row_of(fraction[1]), width)
    )


def main_kernel(
    sizes, field, zonal, meridional, mass, columns, odd_pairs, even_pairs, lat_odd, lat_even,
    kept, row_weight, weight_high, weight_low,
    advected, outgoing, partial, edge_rows, flux_rows,
):
    tracers, levels, rows, width, blocks, capacity, _ = sizes
    fields, span, total = sizes.fields, levels * rows, sizes.fields * rows
    even = lax.rem(lax.axis_index("lon"), 2) == 0
    from_west = jnp.where(even, odd_pairs[0:HALO], even_pairs[0:HALO])
    from_east = jnp.where(even, even_pairs[HALO : 2 * HALO], odd_pairs[HALO : 2 * HALO])
    east_cells = [from_east[i : i + 1, :total] for i in range(HALO)]
    own_cells = [columns[i : i + 1, :total] for i in range(HALO)]
    east_number = jnp.concatenate([from_east[0:1, total:]] * tracers, axis=1)
    east_flux = face_flux(own_cells + east_cells, east_number)
    lanes = jnp.concatenate(
        [
            *east_cells,
            east_flux,
            jnp.zeros((width - 2 * HALO - 1, total), jnp.float32),
            from_west[0:HALO, :total],
        ],
        axis=0,
    ).T
    even = lax.rem(lax.axis_index("lat"), 2) == 0
    next_rows = []
    for i in range(HALO):
        part = pl.ds(i * fields, fields)
        first, second = lat_even[part, :], lat_odd[part, :]
        north_row = jnp.where(even, first, second)
        next_rows.append(north_row)
        edge_rows[pl.ds(rows - HALO + i, fields, stride=rows), :] = jnp.where(even, second, first)
        edge_rows[pl.ds(i, fields, stride=rows), :] = north_row
    last_rows = [field[pl.ds(rows - HALO + i, fields, stride=rows), :] for i in range(HALO)]
    part = pl.ds(HALO * fields, levels)
    north_number = jnp.where(even, lat_even[part, :], lat_odd[part, :])
    flux_rows[pl.ds(0, fields, stride=rows), :] = face_flux(
        last_rows + next_rows, jnp.concatenate([north_number] * tracers, axis=0)
    )
    column = lax.broadcasted_iota(jnp.int32, (span, width), 1)
    row = lax.broadcasted_iota(jnp.int32, (levels, rows, width), 1)

    weights = mass[...].reshape(levels, rows, width)
    for tracer in range(tracers):
        part = pl.ds(tracer * span, span)
        cells = field[part, :]
        halo = lanes[tracer * span : (tracer + 1) * span]
        along = []
        for shift in (3, 2, 1, 0, -1, -2):
            if shift > 0:
                along.append(
                    pltpu.roll(jnp.where(column >= width - shift, halo, cells), shift, 1)
                )
            elif shift < 0:
                along.append(
                    pltpu.roll(jnp.where(column < -shift, halo, cells), width + shift, 1)
                )
            else:
                along.append(cells)
        flux = face_flux(along, zonal[...])
        next_flux = pltpu.roll(
            jnp.where(column == 0, halo[:, HALO : HALO + 1], flux), width - 1, 1
        )
        result = cells - (next_flux - flux)
        cells3 = cells.reshape(levels, rows, width)
        halo3 = edge_rows[part, :].reshape(levels, rows, width)
        along = []
        for shift in (3, 2, 1, 0, -1, -2):
            if shift > 0:
                along.append(pltpu.roll(jnp.where(row >= rows - shift, halo3, cells3), shift, 1))
            elif shift < 0:
                along.append(pltpu.roll(jnp.where(row < -shift, halo3, cells3), rows + shift, 1))
            else:
                along.append(cells3)
        flux = face_flux(along, meridional[...].reshape(levels, rows, width))
        edge3 = flux_rows[part, :].reshape(levels, rows, width)
        next_flux = pltpu.roll(jnp.where(row == 0, edge3, flux), rows - 1, 1)
        result = result.reshape(levels, rows, width) - (next_flux - flux)
        flat = result.reshape(span, width)
        remaining = result * kept[...][None]
        advected[part, :] = remaining.reshape(span, width)

        high, low = two_parts(flat)
        across = dot(high, weight_high[...]) + (
            dot(high, weight_low[...]) + dot(low, weight_high[...])
        )
        payload = jnp.sum(across.reshape(levels, rows, -1) * row_weight[...][None], axis=1)
        base, lane = sizes.spot(tracer)
        for block in range(blocks):
            at = block * capacity
            outgoing[
                pl.ds(block * sizes.margin_rows + base, levels), lane : lane + capacity
            ] = payload[:, at : at + capacity]
        partial[tracer : tracer + 1, :] = jnp.sum(
            weights * remaining, axis=(0, 1)
        )[None]
        partial[tracers + tracer : tracers + tracer + 1, :] = jnp.sum(
            weights * cells3, axis=(0, 1)
        )[None]


def blocks_kernel(sizes, own, given, partial, masses, all_blocks):
    tracers, levels, _, width, blocks, capacity, places = sizes
    size = sizes.margin_rows
    half = size // 2
    mine = lax.axis_index("panel")
    weighed = jnp.zeros((size, width), jnp.float32)
    for block in range(blocks):
        margin = given[pl.ds(block * size, size), :]
        mass = masses[pl.ds(block * levels, levels), :]
        weighed = weighed + margin * jnp.concatenate([mass] * (size // levels), axis=0)
        made = own[pl.ds(block * size, half), :]
        for panel, piece in ((mine, margin[half:]), (1 - mine, made)):
            for place in range(places):
                start = ((panel * blocks + block) * places + place) * (half + 1)
                all_blocks[pl.ds(start, half), :] = piece
    column = lax.broadcasted_iota(jnp.int32, (1, width), 1)
    added = []
    for tracer in range(tracers):
        base, lane = sizes.spot(tracer)
        row = jnp.sum(weighed[base : base + levels], axis=0, keepdims=True)
        added.append(jnp.where((column >= lane) & (column < lane + capacity), row, 0.0))
    sums = partial[...] + jnp.concatenate(
        added + [jnp.zeros((tracers, width), jnp.float32)], axis=0
    )
    totals = jnp.sum(sums, axis=1, keepdims=True)
    line = jnp.zeros((1, width), jnp.float32)
    for i in range(2 * tracers):
        line = jnp.where(column == i, totals[i : i + 1], line)
    for block in range(2 * blocks * places):
        all_blocks[pl.ds(block * (half + 1) + half, 1), :] = line


def fill_kernel(sizes, advected, incoming, row_hit, column_hot, updated, stage, sems):
    tracers, levels, rows, width, blocks, capacity, places = sizes
    half = sizes.margin_rows // 2
    place, mine = lax.axis_index("lon"), lax.axis_index("panel")
    arrived = []
    for block in range(blocks):
        halves = []
        for panel in (1 - mine, mine):
            start = ((panel * blocks + block) * places + place) * (half + 1)
            halves.append(incoming[pl.ds(start, half), :])
        piece = jnp.concatenate(halves, axis=0)
        arrived.append(
            jnp.concatenate(
                [piece[:, i * capacity : (i + 1) * capacity] for i in range(sizes.sides)], axis=0
            )
        )
    arrived = jnp.concatenate(arrived, axis=1)
    line = jnp.sum(
        incoming[pl.ds(half, 2 * blocks * places, stride=half + 1), :], axis=0, keepdims=True
    )
    copies = []
    for tracer in range(tracers):
        values = arrived[tracer * levels : (tracer + 1) * levels]
        spread = (values[:, None, :] * row_hit[...][None]).reshape(levels * rows, -1)
        placed = sum(dot(part, column_hot[...], True) for part in two_parts(spread))
        old = advected[pl.ds(tracer * levels * rows, levels * rows), :]
        scale = line[:, tracers + tracer : tracers + tracer + 1] / line[:, tracer : tracer + 1]
        stage[tracer] = ((old + placed) * scale).reshape(levels, rows, width)
        copies.append(pltpu.make_async_copy(stage.at[tracer], updated.at[0, tracer], sems.at[tracer]))
        copies[-1].start()
    for copy in copies:
        copy.wait()


def exchanged(value, axis, first):
    pairs = []
    for i in range(first, lax.axis_size(axis) - 1, 2):
        pairs += [(i, i + 1), (i + 1, i)]
    return lax.ppermute(value, axis, pairs)


def body(
    tracers, courant_lon, courant_lat, cell_mass, donor_cell, donor_frac, target_cell, live_count
):
    sizes = Sizes(*tracers.shape[1:], *donor_cell.shape[3:], lax.axis_size("lon"))
    _, levels, rows, width, blocks, capacity, places = sizes
    fields = sizes.fields
    field = tracers.reshape(fields * rows, width)
    zonal = courant_lon.reshape(levels * rows, width)
    meridional = courant_lat.reshape(levels * rows, width)
    mass = cell_mass.reshape(levels * rows, width)
    donor = donor_cell.reshape(blocks, capacity)
    fraction = donor_frac.reshape(2, blocks, capacity)
    target = target_cell.reshape(blocks, capacity)
    live = live_count.reshape(1, blocks)

    def shape(*dims):
        return pltpu.VMEM(dims, jnp.float32)

    def near(*values):
        return (pltpu.with_memory_space_constraint(value, pltpu.VMEM) for value in values)

    slots = blocks * capacity
    columns, columns_odd, lat_even, lat_odd, masses, *index_copies = pl.pallas_call(
        functools.partial(pack_kernel, sizes),
        out_shape=(
            shape(8, (fields + levels) * rows),
            shape(16, (fields + levels) * rows),
            shape(sizes.halo_rows + (2 * levels if two_hops(sizes) else 0), width),
            shape(sizes.halo_rows, width),
            shape(blocks * levels, width),
            pltpu.VMEM(donor.shape, donor.dtype),
            pltpu.VMEM(fraction.shape, fraction.dtype),
            pltpu.VMEM(target.shape, target.dtype),
            pltpu.VMEM(live.shape, live.dtype),
        ),
        name="pack_edges",
    )(field, zonal, meridional, mass, target, live, donor, fraction)
    lat_even = exchanged(lat_even, "lat", 0)
    odd_pairs = exchanged(columns_odd, "lon", 1)
    lat_odd = exchanged(lat_odd, "lat", 1)
    even_pairs = exchanged(columns, "lon", 0)
    if two_hops(sizes):
        forwarded = pl.pallas_call(
            functools.partial(forward_kernel, sizes),
            out_shape=shape(FORWARD_ROWS, width),
            name="forward_masses",
        )(*near(masses, lat_even))
        forwarded = lax.ppermute(forwarded, "lat", [(i, i ^ 2) for i in range(blocks)])
        masses = pl.pallas_call(
            functools.partial(masses_kernel, sizes),
            out_shape=shape(blocks * levels, width),
            name="gather_masses",
        )(*near(masses, lat_even, forwarded))
    else:
        masses = lax.all_to_all(
            masses.reshape(blocks, levels, width), "lat", 0, 0, tiled=True
        ).reshape(blocks * levels, width)
    kept, row_hit, column_hot, *weights = pl.pallas_call(
        functools.partial(tables_kernel, sizes),
        out_shape=(
            shape(rows, width),
            shape(rows, slots),
            pltpu.VMEM((width, slots), jnp.bfloat16),
            shape(rows, slots),
            pltpu.VMEM((width, slots), jnp.bfloat16),
            pltpu.VMEM((width, slots), jnp.bfloat16),
        ),
        name="index_tables",
    )(*near(*index_copies))
    advected, outgoing, partial = pl.pallas_call(
        functools.partial(main_kernel, sizes),
        out_shape=(
            shape(fields * rows, width),
            shape(blocks * sizes.margin_rows, width),
            shape(2 * sizes.tracers, width),
        ),
        scratch_shapes=[
            pltpu.VMEM((fields * rows, width), jnp.float32),
            pltpu.VMEM((fields * rows, width), jnp.float32),
        ],
        name="advect_and_interpolate",
    )(
        *near(
            field, zonal, meridional, mass, columns, odd_pairs, even_pairs, lat_odd, lat_even,
            kept, *weights,
        )
    )
    given = lax.ppermute(outgoing, "panel", [(0, 1), (1, 0)])
    block_rows, devices = sizes.margin_rows // 2 + 1, 2 * blocks * places
    all_blocks = pl.pallas_call(
        functools.partial(blocks_kernel, sizes),
        out_shape=shape(devices * block_rows, width),
        name="margin_blocks",
    )(*near(outgoing, given, partial, masses))
    incoming = lax.all_to_all(
        all_blocks.reshape(devices, 1, block_rows * width), ("panel", "lat", "lon"), 0, 0, tiled=True
    ).reshape(devices * block_rows, width)
    return pl.pallas_call(
        functools.partial(fill_kernel, sizes),
        out_shape=jax.ShapeDtypeStruct((1, sizes.tracers, levels, rows, width), jnp.float32),
        out_specs=pl.BlockSpec(memory_space=pl.ANY),
        scratch_shapes=[
            pltpu.VMEM((sizes.tracers, levels, rows, width), jnp.float32),
            pltpu.SemaphoreType.DMA((sizes.tracers,)),
        ],
        name="fill_and_scale",
    )(*near(advected, incoming, row_hit, column_hot))


def solution(mesh):
    in_specs = (
        P("panel", None, None, "lat", "lon"),
        P("panel", None, "lat", "lon"),
        P("panel", None, "lat", "lon"),
        P("panel", None, "lat", "lon"),
        P("panel", "lat", "lon", None, None),
        P(None, "panel", "lat", "lon", None, None),
        P("panel", "lat", "lon", None, None),
        P("panel", "lat", "lon", None),
    )
    out_specs = P("panel", None, None, "lat", "lon")
    return jax.shard_map(body, mesh=mesh, in_specs=in_specs, out_specs=out_specs, check_vma=False)
```

```python
import functools
from typing import NamedTuple

import jax
import jax.numpy as jnp
from jax import lax
from jax.experimental import pallas as pl
from jax.experimental.pallas import tpu as pltpu
from jax.sharding import PartitionSpec as P

HALO = 3
COLUMN_ROWS = 48
FORWARD_ROWS = 68


class Sizes(NamedTuple):
    tracers: int
    levels: int
    rows: int
    width: int
    blocks: int
    capacity: int
    places: int

    @property
    def fields(self):
        return self.tracers * self.levels

    @property
    def sides(self):
        return self.width // self.capacity

    @property
    def margin_rows(self):
        return self.fields // self.sides

    @property
    def halo_rows(self):
        return HALO * self.fields + self.levels

    def spot(self, tracer):
        start = tracer * self.levels
        return start % self.margin_rows, start // self.margin_rows * self.capacity


def row_of(table):
    return jnp.concatenate([table[i : i + 1] for i in range(table.shape[0])], axis=1)


def live_row(live, capacity):
    slots = lax.broadcasted_iota(jnp.int32, (1, capacity), 1)
    return jnp.concatenate(
        [(slots < live[:, i : i + 1]).astype(jnp.float32) for i in range(live.shape[1])], axis=1
    )


def one_hot(spots, extent):
    places = lax.broadcasted_iota(jnp.int32, (extent, spots.shape[1]), 0)
    return (places == spots).astype(jnp.float32)


def two_parts(value):
    high = value.astype(jnp.bfloat16)
    return high, (value - high.astype(jnp.float32)).astype(jnp.bfloat16)


def three_parts(value):
    high = value.astype(jnp.bfloat16)
    rest = value - high.astype(jnp.float32)
    return (high, *two_parts(rest))


def dot(left, right, transposed=False):
    return lax.dot_general(
        left,
        right,
        (((1,), (1 if transposed else 0,)), ((), ())),
        preferred_element_type=jnp.float32,
    )


def cubic_weights(fraction):
    return (
        -fraction * (fraction - 1.0) * (fraction - 2.0) / 6.0,
        (fraction + 1.0) * (fraction - 1.0) * (fraction - 2.0) / 2.0,
        -(fraction + 1.0) * fraction * (fraction - 2.0) / 2.0,
        (fraction + 1.0) * fraction * (fraction - 1.0) / 6.0,
    )


def stencil_weights(start, fraction, extent):
    step = lax.broadcasted_iota(jnp.int32, (extent, start.shape[1]), 0) - start
    spread = jnp.zeros(step.shape, jnp.float32)
    for at, weight in enumerate(cubic_weights(fraction)):
        spread = jnp.where(step == at, weight, spread)
    return spread


def face_flux(cells, number):
    edge_left, edge, edge_right = (
        7.0 / 12.0 * (cells[i + 1] + cells[i + 2]) - 1.0 / 12.0 * (cells[i] + cells[i + 3])
        for i in range(3)
    )
    positive = number > 0.0
    speed = jnp.abs(number)
    far = jnp.where(positive, edge_left, edge_right)
    cell = jnp.where(positive, cells[2], cells[3])
    curve = 6.0 * (cell - 0.5 * (far + edge))
    return number * (edge - 0.5 * speed * ((edge - far) - (1.0 - 2.0 / 3.0 * speed) * curve))


def pack_kernel(
    sizes, field, zonal, meridional, mass, target, live, donor, fraction,
    columns, lat_even, lat_odd, masses, *index_copies,
):
    _, levels, rows, width, blocks, capacity, _ = sizes
    fields = sizes.fields
    here = lax.axis_index("lat")
    for copy, source in zip(index_copies, (donor, fraction, target, live), strict=True):
        copy[...] = source[...]
    even = lax.rem(here, 2) == 0
    for i in range(HALO):
        part = pl.ds(i * fields, fields)
        northward = field[pl.ds(rows - HALO + i, fields, stride=rows), :]
        southward = field[pl.ds(i, fields, stride=rows), :]
        lat_even[part, :] = jnp.where(even, northward, southward)
        lat_odd[part, :] = jnp.where(even, southward, northward)
    number = meridional[pl.ds(0, levels, stride=rows), :]
    lat_even[pl.ds(HALO * fields, levels), :] = number
    lat_odd[pl.ds(HALO * fields, levels), :] = number
    spots = row_of(target[...])
    row_hot = one_hot(spots // width, rows)
    column_hot = one_hot(lax.rem(spots, width), width).astype(jnp.bfloat16)
    picked = sum(dot(part, column_hot) for part in three_parts(mass[...]))
    picked = jnp.sum(
        picked.reshape(levels, rows, spots.shape[1]) * row_hot[None], axis=1
    ) * live_row(live[...], capacity)
    for block in range(blocks):
        part = picked[:, block * capacity : (block + 1) * capacity]
        masses[pl.ds(block * levels, levels), :] = jnp.concatenate([part] * sizes.sides, axis=1)
    if two_hops(sizes):
        for i, step in enumerate((1, 3)):
            block = pl.multiple_of((here ^ step) * levels, levels)
            lat_even[pl.ds(sizes.halo_rows + i * levels, levels), :] = masses[
                pl.ds(block, levels), :
            ]
    turned = jnp.concatenate([field[...], zonal[...]], axis=0).T
    edges = jnp.concatenate(
        [
            turned[width - HALO : width],
            turned[0:HALO],
            jnp.zeros((columns.shape[0] - 2 * HALO, columns.shape[1]), jnp.float32),
        ],
        axis=0,
    )
    columns[...] = edges


def relay_kernel(columns, relayed):
    relayed[...] = columns[0 : relayed.shape[0], :]


def two_hops(sizes):
    return sizes.blocks == 4


def forward_kernel(sizes, masses, lat_even, forwarded):
    levels = sizes.levels
    block = pl.multiple_of((lax.axis_index("lat") ^ 2) * levels, levels)
    forwarded[0:levels, :] = masses[pl.ds(block, levels), :]
    forwarded[levels : 2 * levels, :] = lat_even[pl.ds(sizes.halo_rows + levels, levels), :]
    spare = forwarded.shape[0] - 2 * levels
    if spare:
        forwarded[pl.ds(2 * levels, spare), :] = jnp.zeros((spare, sizes.width), jnp.float32)


def masses_kernel(sizes, masses, lat_even, forwarded, received):
    levels = sizes.levels
    here = lax.axis_index("lat")
    own = pl.multiple_of(here * levels, levels)
    pieces = (
        masses[pl.ds(own, levels), :],
        lat_even[pl.ds(sizes.halo_rows, levels), :],
        forwarded[0:levels, :],
        forwarded[levels : 2 * levels, :],
    )
    for step, piece in enumerate(pieces):
        received[pl.ds(pl.multiple_of((here ^ step) * levels, levels), levels), :] = piece


def tables_kernel(
    sizes, donor, fraction, target, live, kept, row_hit, column_hot, row_weight, high, low
):
    _, _, rows, width, _, capacity, _ = sizes
    spots = row_of(target[...])
    row_hit[...] = one_hot(spots // width, rows) * live_row(live[...], capacity)
    column_hot[...] = one_hot(lax.rem(spots, width), width).astype(jnp.bfloat16)
    kept[...] = 1.0 - dot(row_hit[...].astype(jnp.bfloat16), column_hot[...], True)
    starts = row_of(donor[...])
    row_weight[...] = stencil_weights(starts // width, row_of(fraction[0]), rows)
    high[...], low[...] = two_parts(
        stencil_weights(lax.rem(starts, width), row_of(fraction[1]), width)
    )


def main_kernel(
    sizes, field, zonal, meridional, mass, columns, odd_pairs, even_pairs, lat_odd, lat_even,
    kept, row_weight, weight_high, weight_low,
    advected, outgoing, partial, edge_rows, flux_rows,
):
    tracers, levels, rows, width, blocks, capacity, _ = sizes
    fields, span, total = sizes.fields, levels * rows, sizes.fields * rows
    place = lax.axis_index("lon")
    even = lax.rem(place, 2) == 0
    inner = (place > 0) & (place < sizes.places - 1)
    second = jnp.where(inner, odd_pairs[...], 0.0)
    from_west = jnp.where(even, second[0:HALO], even_pairs[0:HALO])
    from_east = jnp.where(even, even_pairs[HALO : 2 * HALO], second[HALO : 2 * HALO])
    east_cells = [from_east[i : i + 1, :total] for i in range(HALO)]
    own_cells = [columns[i : i + 1, :total] for i in range(HALO)]
    east_number = jnp.concatenate([from_east[0:1, total:]] * tracers, axis=1)
    east_flux = face_flux(own_cells + east_cells, east_number)
    lanes = jnp.concatenate(
        [
            *east_cells,
            east_flux,
            jnp.zeros((width - 2 * HALO - 1, total), jnp.float32),
            from_west[0:HALO, :total],
        ],
        axis=0,
    ).T
    even = lax.rem(lax.axis_index("lat"), 2) == 0
    next_rows = []
    for i in range(HALO):
        part = pl.ds(i * fields, fields)
        first, second = lat_even[part, :], lat_odd[part, :]
        north_row = jnp.where(even, first, second)
        next_rows.append(north_row)
        edge_rows[pl.ds(rows - HALO + i, fields, stride=rows), :] = jnp.where(even, second, first)
        edge_rows[pl.ds(i, fields, stride=rows), :] = north_row
    last_rows = [field[pl.ds(rows - HALO + i, fields, stride=rows), :] for i in range(HALO)]
    part = pl.ds(HALO * fields, levels)
    north_number = jnp.where(even, lat_even[part, :], lat_odd[part, :])
    flux_rows[pl.ds(0, fields, stride=rows), :] = face_flux(
        last_rows + next_rows, jnp.concatenate([north_number] * tracers, axis=0)
    )
    column = lax.broadcasted_iota(jnp.int32, (span, width), 1)
    row = lax.broadcasted_iota(jnp.int32, (levels, rows, width), 1)

    weights = mass[...].reshape(levels, rows, width)
    for tracer in range(tracers):
        part = pl.ds(tracer * span, span)
        cells = field[part, :]
        halo = lanes[tracer * span : (tracer + 1) * span]
        along = []
        for shift in (3, 2, 1, 0, -1, -2):
            if shift > 0:
                along.append(
                    pltpu.roll(jnp.where(column >= width - shift, halo, cells), shift, 1)
                )
            elif shift < 0:
                along.append(
                    pltpu.roll(jnp.where(column < -shift, halo, cells), width + shift, 1)
                )
            else:
                along.append(cells)
        flux = face_flux(along, zonal[...])
        next_flux = pltpu.roll(
            jnp.where(column == 0, halo[:, HALO : HALO + 1], flux), width - 1, 1
        )
        result = cells - (next_flux - flux)
        cells3 = cells.reshape(levels, rows, width)
        halo3 = edge_rows[part, :].reshape(levels, rows, width)
        along = []
        for shift in (3, 2, 1, 0, -1, -2):
            if shift > 0:
                along.append(pltpu.roll(jnp.where(row >= rows - shift, halo3, cells3), shift, 1))
            elif shift < 0:
                along.append(pltpu.roll(jnp.where(row < -shift, halo3, cells3), rows + shift, 1))
            else:
                along.append(cells3)
        flux = face_flux(along, meridional[...].reshape(levels, rows, width))
        edge3 = flux_rows[part, :].reshape(levels, rows, width)
        next_flux = pltpu.roll(jnp.where(row == 0, edge3, flux), rows - 1, 1)
        result = result.reshape(levels, rows, width) - (next_flux - flux)
        flat = result.reshape(span, width)
        remaining = result * kept[...][None]
        advected[part, :] = remaining.reshape(span, width)

        high, low = two_parts(flat)
        across = dot(high, weight_high[...]) + (
            dot(high, weight_low[...]) + dot(low, weight_high[...])
        )
        payload = jnp.sum(across.reshape(levels, rows, -1) * row_weight[...][None], axis=1)
        base, lane = sizes.spot(tracer)
        for block in range(blocks):
            at = block * capacity
            outgoing[
                pl.ds(block * sizes.margin_rows + base, levels), lane : lane + capacity
            ] = payload[:, at : at + capacity]
        partial[tracer : tracer + 1, :] = jnp.sum(
            weights * remaining, axis=(0, 1)
        )[None]
        partial[tracers + tracer : tracers + tracer + 1, :] = jnp.sum(
            weights * cells3, axis=(0, 1)
        )[None]


def blocks_kernel(sizes, own, given, partial, masses, all_blocks):
    tracers, levels, _, width, blocks, capacity, places = sizes
    size = sizes.margin_rows
    half = size // 2
    mine = lax.axis_index("panel")
    weighed = jnp.zeros((size, width), jnp.float32)
    for block in range(blocks):
        margin = given[pl.ds(block * size, size), :]
        mass = masses[pl.ds(block * levels, levels), :]
        weighed = weighed + margin * jnp.concatenate([mass] * (size // levels), axis=0)
        made = own[pl.ds(block * size, half), :]
        for panel, piece in ((mine, margin[half:]), (1 - mine, made)):
            for place in range(places):
                start = ((panel * blocks + block) * places + place) * (half + 1)
                all_blocks[pl.ds(start, half), :] = piece
    column = lax.broadcasted_iota(jnp.int32, (1, width), 1)
    added = []
    for tracer in range(tracers):
        base, lane = sizes.spot(tracer)
        row = jnp.sum(weighed[base : base + levels], axis=0, keepdims=True)
        added.append(jnp.where((column >= lane) & (column < lane + capacity), row, 0.0))
    sums = partial[...] + jnp.concatenate(
        added + [jnp.zeros((tracers, width), jnp.float32)], axis=0
    )
    totals = jnp.sum(sums, axis=1, keepdims=True)
    line = jnp.zeros((1, width), jnp.float32)
    for i in range(2 * tracers):
        line = jnp.where(column == i, totals[i : i + 1], line)
    for block in range(2 * blocks * places):
        all_blocks[pl.ds(block * (half + 1) + half, 1), :] = line


def fill_kernel(sizes, advected, incoming, row_hit, column_hot, updated, stage, sems):
    tracers, levels, rows, width, blocks, capacity, places = sizes
    half = sizes.margin_rows // 2
    place, mine = lax.axis_index("lon"), lax.axis_index("panel")
    arrived = []
    for block in range(blocks):
        halves = []
        for panel in (1 - mine, mine):
            start = ((panel * blocks + block) * places + place) * (half + 1)
            halves.append(incoming[pl.ds(start, half), :])
        piece = jnp.concatenate(halves, axis=0)
        arrived.append(
            jnp.concatenate(
                [piece[:, i * capacity : (i + 1) * capacity] for i in range(sizes.sides)], axis=0
            )
        )
    arrived = jnp.concatenate(arrived, axis=1)
    line = jnp.sum(
        incoming[pl.ds(half, 2 * blocks * places, stride=half + 1), :], axis=0, keepdims=True
    )
    copies = []
    for tracer in range(tracers):
        values = arrived[tracer * levels : (tracer + 1) * levels]
        spread = (values[:, None, :] * row_hit[...][None]).reshape(levels * rows, -1)
        placed = sum(dot(part, column_hot[...], True) for part in two_parts(spread))
        old = advected[pl.ds(tracer * levels * rows, levels * rows), :]
        scale = line[:, tracers + tracer : tracers + tracer + 1] / line[:, tracer : tracer + 1]
        stage[tracer] = ((old + placed) * scale).reshape(levels, rows, width)
        copies.append(pltpu.make_async_copy(stage.at[tracer], updated.at[0, tracer], sems.at[tracer]))
        copies[-1].start()
    for copy in copies:
        copy.wait()


def exchanged(value, axis, first):
    pairs = []
    for i in range(first, lax.axis_size(axis) - 1, 2):
        pairs += [(i, i + 1), (i + 1, i)]
    return lax.ppermute(value, axis, pairs)


def body(
    tracers, courant_lon, courant_lat, cell_mass, donor_cell, donor_frac, target_cell, live_count
):
    sizes = Sizes(*tracers.shape[1:], *donor_cell.shape[3:], lax.axis_size("lon"))
    _, levels, rows, width, blocks, capacity, places = sizes
    fields = sizes.fields
    field = tracers.reshape(fields * rows, width)
    zonal = courant_lon.reshape(levels * rows, width)
    meridional = courant_lat.reshape(levels * rows, width)
    mass = cell_mass.reshape(levels * rows, width)
    donor = donor_cell.reshape(blocks, capacity)
    fraction = donor_frac.reshape(2, blocks, capacity)
    target = target_cell.reshape(blocks, capacity)
    live = live_count.reshape(1, blocks)

    def shape(*dims):
        return pltpu.VMEM(dims, jnp.float32)

    def near(*values):
        return (pltpu.with_memory_space_constraint(value, pltpu.VMEM) for value in values)

    slots = blocks * capacity
    columns, lat_even, lat_odd, masses, *index_copies = pl.pallas_call(
        functools.partial(pack_kernel, sizes),
        out_shape=(
            shape(COLUMN_ROWS, (fields + levels) * rows),
            shape(sizes.halo_rows + (2 * levels if two_hops(sizes) else 0), width),
            shape(sizes.halo_rows, width),
            shape(blocks * levels, width),
            pltpu.VMEM(donor.shape, donor.dtype),
            pltpu.VMEM(fraction.shape, fraction.dtype),
            pltpu.VMEM(target.shape, target.dtype),
            pltpu.VMEM(live.shape, live.dtype),
        ),
        name="pack_edges",
    )(field, zonal, meridional, mass, target, live, donor, fraction)
    lat_even = exchanged(lat_even, "lat", 0)
    lat_odd = exchanged(lat_odd, "lat", 1)
    even_pairs = exchanged(columns, "lon", 0)
    if places == 4:
        relayed = pl.pallas_call(
            relay_kernel,
            out_shape=shape(8, even_pairs.shape[1]),
            name="relay_columns",
        )(*near(even_pairs))
        odd_pairs = lax.ppermute(relayed, "lon", [(i, i ^ 2) for i in range(places)])
    else:
        odd_pairs = exchanged(columns, "lon", 1)
    if two_hops(sizes):
        forwarded = pl.pallas_call(
            functools.partial(forward_kernel, sizes),
            out_shape=shape(FORWARD_ROWS, width),
            name="forward_masses",
        )(*near(masses, lat_even))
        forwarded = lax.ppermute(forwarded, "lat", [(i, i ^ 2) for i in range(blocks)])
        masses = pl.pallas_call(
            functools.partial(masses_kernel, sizes),
            out_shape=shape(blocks * levels, width),
            name="gather_masses",
        )(*near(masses, lat_even, forwarded))
    else:
        masses = lax.all_to_all(
            masses.reshape(blocks, levels, width), "lat", 0, 0, tiled=True
        ).reshape(blocks * levels, width)
    kept, row_hit, column_hot, *weights = pl.pallas_call(
        functools.partial(tables_kernel, sizes),
        out_shape=(
            shape(rows, width),
            shape(rows, slots),
            pltpu.VMEM((width, slots), jnp.bfloat16),
            shape(rows, slots),
            pltpu.VMEM((width, slots), jnp.bfloat16),
            pltpu.VMEM((width, slots), jnp.bfloat16),
        ),
        name="index_tables",
    )(*near(*index_copies))
    advected, outgoing, partial = pl.pallas_call(
        functools.partial(main_kernel, sizes),
        out_shape=(
            shape(fields * rows, width),
            shape(blocks * sizes.margin_rows, width),
            shape(2 * sizes.tracers, width),
        ),
        scratch_shapes=[
            pltpu.VMEM((fields * rows, width), jnp.float32),
            pltpu.VMEM((fields * rows, width), jnp.float32),
        ],
        name="advect_and_interpolate",
    )(
        *near(
            field, zonal, meridional, mass, columns, odd_pairs, even_pairs, lat_odd, lat_even,
            kept, *weights,
        )
    )
    given = lax.ppermute(outgoing, "panel", [(0, 1), (1, 0)])
    block_rows, devices = sizes.margin_rows // 2 + 1, 2 * blocks * places
    all_blocks = pl.pallas_call(
        functools.partial(blocks_kernel, sizes),
        out_shape=shape(devices * block_rows, width),
        name="margin_blocks",
    )(*near(outgoing, given, partial, masses))
    incoming = lax.all_to_all(
        all_blocks.reshape(devices, 1, block_rows * width), ("panel", "lat", "lon"), 0, 0, tiled=True
    ).reshape(devices * block_rows, width)
    return pl.pallas_call(
        functools.partial(fill_kernel, sizes),
        out_shape=jax.ShapeDtypeStruct((1, sizes.tracers, levels, rows, width), jnp.float32),
        out_specs=pl.BlockSpec(memory_space=pl.ANY),
        scratch_shapes=[
            pltpu.VMEM((sizes.tracers, levels, rows, width), jnp.float32),
            pltpu.SemaphoreType.DMA((sizes.tracers,)),
        ],
        name="fill_and_scale",
    )(*near(advected, incoming, row_hit, column_hot))


def solution(mesh):
    in_specs = (
        P("panel", None, None, "lat", "lon"),
        P("panel", None, "lat", "lon"),
        P("panel", None, "lat", "lon"),
        P("panel", None, "lat", "lon"),
        P("panel", "lat", "lon", None, None),
        P(None, "panel", "lat", "lon", None, None),
        P("panel", "lat", "lon", None, None),
        P("panel", "lat", "lon", None),
    )
    out_specs = P("panel", None, None, "lat", "lon")
    return jax.shard_map(body, mesh=mesh, in_specs=in_specs, out_specs=out_specs, check_vma=False)
```

```python
import functools
from typing import NamedTuple

import jax
import jax.numpy as jnp
from jax import lax
from jax.experimental import pallas as pl
from jax.experimental.pallas import tpu as pltpu
from jax.sharding import PartitionSpec as P

HALO = 3
COLUMN_ROWS = 44
FORWARD_ROWS = 36


class Sizes(NamedTuple):
    tracers: int
    levels: int
    rows: int
    width: int
    blocks: int
    capacity: int
    places: int

    @property
    def fields(self):
        return self.tracers * self.levels

    @property
    def sides(self):
        return self.width // self.capacity

    @property
    def margin_rows(self):
        return self.fields // self.sides

    @property
    def halo_rows(self):
        return HALO * self.fields + self.levels

    def spot(self, tracer):
        start = tracer * self.levels
        return start % self.margin_rows, start // self.margin_rows * self.capacity


def row_of(table):
    return jnp.concatenate([table[i : i + 1] for i in range(table.shape[0])], axis=1)


def live_row(live, capacity):
    slots = lax.broadcasted_iota(jnp.int32, (1, capacity), 1)
    return jnp.concatenate(
        [(slots < live[:, i : i + 1]).astype(jnp.float32) for i in range(live.shape[1])], axis=1
    )


def one_hot(spots, extent):
    places = lax.broadcasted_iota(jnp.int32, (extent, spots.shape[1]), 0)
    return (places == spots).astype(jnp.float32)


def two_parts(value):
    high = value.astype(jnp.bfloat16)
    return high, (value - high.astype(jnp.float32)).astype(jnp.bfloat16)


def three_parts(value):
    high = value.astype(jnp.bfloat16)
    rest = value - high.astype(jnp.float32)
    return (high, *two_parts(rest))


def dot(left, right, transposed=False):
    return lax.dot_general(
        left,
        right,
        (((1,), (1 if transposed else 0,)), ((), ())),
        preferred_element_type=jnp.float32,
    )


def dot_parts(parts, right, transposed=False):
    rows = parts[0].shape[0]
    product = dot(jnp.concatenate(parts, axis=0), right, transposed)
    return sum(product[i * rows : (i + 1) * rows] for i in range(len(parts)))


def cubic_weights(fraction):
    return (
        -fraction * (fraction - 1.0) * (fraction - 2.0) / 6.0,
        (fraction + 1.0) * (fraction - 1.0) * (fraction - 2.0) / 2.0,
        -(fraction + 1.0) * fraction * (fraction - 2.0) / 2.0,
        (fraction + 1.0) * fraction * (fraction - 1.0) / 6.0,
    )


def stencil_weights(start, fraction, extent):
    step = lax.broadcasted_iota(jnp.int32, (extent, start.shape[1]), 0) - start
    spread = jnp.zeros(step.shape, jnp.float32)
    for at, weight in enumerate(cubic_weights(fraction)):
        spread = jnp.where(step == at, weight, spread)
    return spread


def face_flux(cells, number):
    edge_left, edge, edge_right = (
        7.0 / 12.0 * (cells[i + 1] + cells[i + 2]) - 1.0 / 12.0 * (cells[i] + cells[i + 3])
        for i in range(3)
    )
    positive = number > 0.0
    speed = jnp.abs(number)
    far = jnp.where(positive, edge_left, edge_right)
    cell = jnp.where(positive, cells[2], cells[3])
    curve = 6.0 * (cell - 0.5 * (far + edge))
    return number * (edge - 0.5 * speed * ((edge - far) - (1.0 - 2.0 / 3.0 * speed) * curve))


def pack_kernel(
    sizes, field, zonal, meridional, mass, target, live, donor, fraction,
    columns, sides, lat_even, lat_odd, masses, *index_copies,
):
    _, levels, rows, width, blocks, capacity, _ = sizes
    fields = sizes.fields
    here = lax.axis_index("lat")
    for copy, source in zip(index_copies, (donor, fraction, target, live), strict=True):
        copy[...] = source[...]
    even = lax.rem(here, 2) == 0
    for i in range(HALO):
        part = pl.ds(i * fields, fields)
        northward = field[pl.ds(rows - HALO + i, fields, stride=rows), :]
        southward = field[pl.ds(i, fields, stride=rows), :]
        lat_even[part, :] = jnp.where(even, northward, southward)
        lat_odd[part, :] = jnp.where(even, southward, northward)
    number = meridional[pl.ds(0, levels, stride=rows), :]
    lat_even[pl.ds(HALO * fields, levels), :] = number
    lat_odd[pl.ds(HALO * fields, levels), :] = number
    spots = row_of(target[...])
    row_hot = one_hot(spots // width, rows)
    column_hot = one_hot(lax.rem(spots, width), width).astype(jnp.bfloat16)
    picked = dot_parts(three_parts(mass[...]), column_hot)
    picked = jnp.sum(
        picked.reshape(levels, rows, spots.shape[1]) * row_hot[None], axis=1
    ) * live_row(live[...], capacity)
    for block in range(blocks):
        part = picked[:, block * capacity : (block + 1) * capacity]
        masses[pl.ds(block * levels, levels), :] = jnp.concatenate([part] * sizes.sides, axis=1)
    if two_hops(sizes):
        for i, step in enumerate((1, 3)):
            block = pl.multiple_of((here ^ step) * levels, levels)
            lat_even[pl.ds(sizes.halo_rows + i * levels, levels), :] = masses[
                pl.ds(block, levels), :
            ]
    turned = jnp.concatenate([field[...], zonal[...]], axis=0).T
    edges = jnp.concatenate(
        [
            turned[width - HALO : width],
            turned[0:HALO],
            jnp.zeros((columns.shape[0] - 2 * HALO, columns.shape[1]), jnp.float32),
        ],
        axis=0,
    )
    columns[...] = edges
    sides[0 : 2 * HALO] = turned[0 : 2 * HALO]
    sides[2 * HALO : 4 * HALO] = turned[width - 2 * HALO : width]


def relay_kernel(columns, relayed):
    relayed[...] = columns[0 : relayed.shape[0], :]


def two_hops(sizes):
    return sizes.blocks == 4


def forward_kernel(sizes, masses, lat_even, forwarded):
    levels = sizes.levels
    block = pl.multiple_of((lax.axis_index("lat") ^ 2) * levels, levels)
    forwarded[0:levels, :] = masses[pl.ds(block, levels), :]
    forwarded[levels : 2 * levels, :] = lat_even[pl.ds(sizes.halo_rows + levels, levels), :]
    spare = forwarded.shape[0] - 2 * levels
    if spare:
        forwarded[pl.ds(2 * levels, spare), :] = jnp.zeros((spare, sizes.width), jnp.float32)


def masses_kernel(sizes, masses, lat_even, forwarded, received):
    levels = sizes.levels
    here = lax.axis_index("lat")
    own = pl.multiple_of(here * levels, levels)
    pieces = (
        masses[pl.ds(own, levels), :],
        lat_even[pl.ds(sizes.halo_rows, levels), :],
        forwarded[0:levels, :],
        forwarded[levels : 2 * levels, :],
    )
    for step, piece in enumerate(pieces):
        received[pl.ds(pl.multiple_of((here ^ step) * levels, levels), levels), :] = piece


def tables_kernel(
    sizes, donor, fraction, target, live, kept, row_hit, column_hot, row_weight, high, low
):
    _, _, rows, width, _, capacity, _ = sizes
    spots = row_of(target[...])
    row_hit[...] = one_hot(spots // width, rows) * live_row(live[...], capacity)
    column_hot[...] = one_hot(lax.rem(spots, width), width).astype(jnp.bfloat16)
    kept[...] = 1.0 - dot(row_hit[...].astype(jnp.bfloat16), column_hot[...], True)
    starts = row_of(donor[...])
    row_weight[...] = stencil_weights(starts // width, row_of(fraction[0]), rows)
    high[...], low[...] = two_parts(
        stencil_weights(lax.rem(starts, width), row_of(fraction[1]), width)
    )


def zonal_kernel(sizes, field, zonal, moved):
    tracers, levels, rows, width, *_ = sizes
    span = levels * rows
    for tracer in range(tracers):
        part = pl.ds(tracer * span, span)
        cells = field[part, :]
        along = [
            pltpu.roll(cells, shift % width, 1) if shift else cells
            for shift in (3, 2, 1, 0, -1, -2)
        ]
        flux = face_flux(along, zonal[...])
        moved[part, :] = cells - (pltpu.roll(flux, width - 1, 1) - flux)


def main_kernel(
    sizes, field, moved, meridional, sides, odd_pairs, even_pairs, lat_odd, lat_even,
    row_weight, weight_high, weight_low,
    advected, first_half, second_half, edge_rows, flux_rows,
):
    tracers, levels, rows, width, blocks, capacity, _ = sizes
    fields, span, total = sizes.fields, levels * rows, sizes.fields * rows
    place = lax.axis_index("lon")
    even = lax.rem(place, 2) == 0
    inner = (place > 0) & (place < sizes.places - 1)
    second = jnp.where(inner, odd_pairs[...], 0.0)
    from_west = jnp.where(even, second[0:HALO], even_pairs[0:HALO])
    from_east = jnp.where(even, even_pairs[HALO : 2 * HALO], second[HALO : 2 * HALO])
    west = jnp.concatenate([from_west, sides[0 : 2 * HALO]], axis=0)
    east = jnp.concatenate([sides[2 * HALO : 4 * HALO], from_east], axis=0)
    faces = HALO + 1
    number = jnp.concatenate(
        [west[HALO : HALO + faces, total:], east[HALO : HALO + faces, total:]], axis=0
    )
    flux = face_flux(
        [
            jnp.concatenate([west[i : i + faces, :total], east[i : i + faces, :total]], axis=0)
            for i in range(2 * HALO)
        ],
        jnp.concatenate([number] * tracers, axis=1),
    )
    change = flux[1:] - flux[:-1]
    lanes = jnp.concatenate(
        [
            sides[0:HALO, :total] - change[0:HALO],
            jnp.zeros((width - 2 * HALO, total), jnp.float32),
            sides[3 * HALO : 4 * HALO, :total] - change[faces : faces + HALO],
        ],
        axis=0,
    ).T
    even = lax.rem(lax.axis_index("lat"), 2) == 0
    next_rows = []
    for i in range(HALO):
        part = pl.ds(i * fields, fields)
        first, second = lat_even[part, :], lat_odd[part, :]
        north_row = jnp.where(even, first, second)
        next_rows.append(north_row)
        edge_rows[pl.ds(rows - HALO + i, fields, stride=rows), :] = jnp.where(even, second, first)
        edge_rows[pl.ds(i, fields, stride=rows), :] = north_row
    last_rows = [field[pl.ds(rows - HALO + i, fields, stride=rows), :] for i in range(HALO)]
    part = pl.ds(HALO * fields, levels)
    north_number = jnp.where(even, lat_even[part, :], lat_odd[part, :])
    flux_rows[pl.ds(0, fields, stride=rows), :] = face_flux(
        last_rows + next_rows, jnp.concatenate([north_number] * tracers, axis=0)
    )
    column = lax.broadcasted_iota(jnp.int32, (span, width), 1)
    row = lax.broadcasted_iota(jnp.int32, (levels, rows, width), 1)

    for tracer in range(tracers):
        part = pl.ds(tracer * span, span)
        cells = field[part, :]
        result = jnp.where(
            (column < HALO) | (column >= width - HALO),
            lanes[tracer * span : (tracer + 1) * span],
            moved[part, :],
        )
        cells3 = cells.reshape(levels, rows, width)
        halo3 = edge_rows[part, :].reshape(levels, rows, width)
        along = []
        for shift in (3, 2, 1, 0, -1, -2):
            if shift > 0:
                along.append(pltpu.roll(jnp.where(row >= rows - shift, halo3, cells3), shift, 1))
            elif shift < 0:
                along.append(pltpu.roll(jnp.where(row < -shift, halo3, cells3), rows + shift, 1))
            else:
                along.append(cells3)
        flux = face_flux(along, meridional[...].reshape(levels, rows, width))
        edge3 = flux_rows[part, :].reshape(levels, rows, width)
        next_flux = pltpu.roll(jnp.where(row == 0, edge3, flux), rows - 1, 1)
        result = result.reshape(levels, rows, width) - (next_flux - flux)
        flat = result.reshape(span, width)
        advected[part, :] = flat
    high, low = two_parts(advected[...])
    across = dot_parts((high, low), weight_high[...]) + dot(high, weight_low[...])
    payloads = jnp.sum(across.reshape(fields, rows, -1) * row_weight[...][None], axis=1)
    for tracer in range(tracers):
        payload = payloads[tracer * levels : (tracer + 1) * levels]
        base, lane = sizes.spot(tracer)
        half = sizes.margin_rows // 2
        outgoing = (first_half, second_half)[base // half]
        for block in range(blocks):
            at = block * capacity
            outgoing[pl.ds(block * half + base % half, levels), lane : lane + capacity] = payload[
                :, at : at + capacity
            ]


def sums_kernel(sizes, field, mass, advected, kept, remaining, partial):
    tracers, levels, rows, width, *_ = sizes
    span = levels * rows
    weights = mass[...].reshape(levels, rows, width)
    for tracer in range(tracers):
        part = pl.ds(tracer * span, span)
        held = advected[part, :].reshape(levels, rows, width) * kept[...][None]
        remaining[part, :] = held.reshape(span, width)
        before = field[part, :].reshape(levels, rows, width)
        partial[tracer : tracer + 1, :] = jnp.sum(weights * held, axis=(0, 1))[None]
        partial[tracers + tracer : tracers + tracer + 1, :] = jnp.sum(
            weights * before, axis=(0, 1)
        )[None]


def blocks_kernel(sizes, own, given_first, given_second, partial, masses, all_blocks):
    tracers, levels, _, width, blocks, capacity, places = sizes
    half = sizes.margin_rows // 2
    mine = lax.axis_index("panel")
    weighed = [jnp.zeros((half, width), jnp.float32) for _ in range(2)]
    for block in range(blocks):
        part = pl.ds(block * half, half)
        mass = masses[pl.ds(block * levels, levels), :]
        mass = jnp.concatenate([mass] * (half // levels), axis=0)
        margins = (given_first[part, :], given_second[part, :])
        weighed = [total + margin * mass for total, margin in zip(weighed, margins, strict=True)]
        for panel, piece in ((mine, margins[1]), (1 - mine, own[part, :])):
            for place in range(places):
                start = ((panel * blocks + block) * places + place) * (half + 1)
                all_blocks[pl.ds(start, half), :] = piece
    weighed = jnp.concatenate(weighed, axis=0)
    column = lax.broadcasted_iota(jnp.int32, (1, width), 1)
    added = []
    for tracer in range(tracers):
        base, lane = sizes.spot(tracer)
        row = jnp.sum(weighed[base : base + levels], axis=0, keepdims=True)
        added.append(jnp.where((column >= lane) & (column < lane + capacity), row, 0.0))
    sums = partial[...] + jnp.concatenate(
        added + [jnp.zeros((tracers, width), jnp.float32)], axis=0
    )
    totals = jnp.sum(sums, axis=1, keepdims=True)
    line = jnp.zeros((1, width), jnp.float32)
    for i in range(2 * tracers):
        line = jnp.where(column == i, totals[i : i + 1], line)
    for block in range(2 * blocks * places):
        all_blocks[pl.ds(block * (half + 1) + half, 1), :] = line


def fill_kernel(sizes, advected, incoming, row_hit, column_hot, updated, stage, sems):
    tracers, levels, rows, width, blocks, capacity, places = sizes
    half = sizes.margin_rows // 2
    place, mine = lax.axis_index("lon"), lax.axis_index("panel")
    arrived = []
    for block in range(blocks):
        halves = []
        for panel in (1 - mine, mine):
            start = ((panel * blocks + block) * places + place) * (half + 1)
            halves.append(incoming[pl.ds(start, half), :])
        piece = jnp.concatenate(halves, axis=0)
        arrived.append(
            jnp.concatenate(
                [piece[:, i * capacity : (i + 1) * capacity] for i in range(sizes.sides)], axis=0
            )
        )
    arrived = jnp.concatenate(arrived, axis=1)
    line = jnp.sum(
        incoming[pl.ds(half, 2 * blocks * places, stride=half + 1), :], axis=0, keepdims=True
    )
    spread = (arrived[:, None, :] * row_hit[...][None]).reshape(sizes.fields * rows, -1)
    filled = dot_parts(two_parts(spread), column_hot[...], True)
    copies = []
    for tracer in range(tracers):
        placed = filled[tracer * levels * rows : (tracer + 1) * levels * rows]
        old = advected[pl.ds(tracer * levels * rows, levels * rows), :]
        scale = line[:, tracers + tracer : tracers + tracer + 1] / line[:, tracer : tracer + 1]
        stage[tracer] = ((old + placed) * scale).reshape(levels, rows, width)
        copies.append(pltpu.make_async_copy(stage.at[tracer], updated.at[0, tracer], sems.at[tracer]))
        copies[-1].start()
    for copy in copies:
        copy.wait()


def exchanged(value, axis, first):
    pairs = []
    for i in range(first, lax.axis_size(axis) - 1, 2):
        pairs += [(i, i + 1), (i + 1, i)]
    return lax.ppermute(value, axis, pairs)


def body(
    tracers, courant_lon, courant_lat, cell_mass, donor_cell, donor_frac, target_cell, live_count
):
    sizes = Sizes(*tracers.shape[1:], *donor_cell.shape[3:], lax.axis_size("lon"))
    _, levels, rows, width, blocks, capacity, places = sizes
    fields = sizes.fields
    field = tracers.reshape(fields * rows, width)
    zonal = courant_lon.reshape(levels * rows, width)
    meridional = courant_lat.reshape(levels * rows, width)
    mass = cell_mass.reshape(levels * rows, width)
    donor = donor_cell.reshape(blocks, capacity)
    fraction = donor_frac.reshape(2, blocks, capacity)
    target = target_cell.reshape(blocks, capacity)
    live = live_count.reshape(1, blocks)

    def shape(*dims):
        return pltpu.VMEM(dims, jnp.float32)

    def near(*values):
        return (pltpu.with_memory_space_constraint(value, pltpu.VMEM) for value in values)

    slots = blocks * capacity
    columns, sides, lat_even, lat_odd, masses, *index_copies = pl.pallas_call(
        functools.partial(pack_kernel, sizes),
        out_shape=(
            shape(COLUMN_ROWS, (fields + levels) * rows),
            shape(4 * HALO, (fields + levels) * rows),
            shape(sizes.halo_rows + (2 * levels if two_hops(sizes) else 0), width),
            shape(sizes.halo_rows, width),
            shape(blocks * levels, width),
            pltpu.VMEM(donor.shape, donor.dtype),
            pltpu.VMEM(fraction.shape, fraction.dtype),
            pltpu.VMEM(target.shape, target.dtype),
            pltpu.VMEM(live.shape, live.dtype),
        ),
        name="pack_edges",
    )(field, zonal, meridional, mass, target, live, donor, fraction)
    lat_even = exchanged(lat_even, "lat", 0)
    lat_odd = exchanged(lat_odd, "lat", 1)
    even_pairs = exchanged(columns, "lon", 0)
    if places == 4:
        relayed = pl.pallas_call(
            relay_kernel,
            out_shape=shape(8, even_pairs.shape[1]),
            name="relay_columns",
        )(*near(even_pairs))
        odd_pairs = lax.ppermute(relayed, "lon", [(i, i ^ 2) for i in range(places)])
    else:
        odd_pairs = exchanged(columns, "lon", 1)
    if two_hops(sizes):
        forwarded = pl.pallas_call(
            functools.partial(forward_kernel, sizes),
            out_shape=shape(FORWARD_ROWS, width),
            name="forward_masses",
        )(*near(masses, lat_even))
        forwarded = lax.ppermute(forwarded, "lat", [(i, i ^ 2) for i in range(blocks)])
        masses = pl.pallas_call(
            functools.partial(masses_kernel, sizes),
            out_shape=shape(blocks * levels, width),
            name="gather_masses",
        )(*near(masses, lat_even, forwarded))
    else:
        masses = lax.all_to_all(
            masses.reshape(blocks, levels, width), "lat", 0, 0, tiled=True
        ).reshape(blocks * levels, width)
    kept, row_hit, column_hot, *weights = pl.pallas_call(
        functools.partial(tables_kernel, sizes),
        out_shape=(
            shape(rows, width),
            shape(rows, slots),
            pltpu.VMEM((width, slots), jnp.bfloat16),
            shape(rows, slots),
            pltpu.VMEM((width, slots), jnp.bfloat16),
            pltpu.VMEM((width, slots), jnp.bfloat16),
        ),
        name="index_tables",
    )(*near(*index_copies))
    moved = pl.pallas_call(
        functools.partial(zonal_kernel, sizes),
        out_shape=shape(fields * rows, width),
        name="own_zonal",
    )(*near(field, zonal))
    advected, first_half, second_half = pl.pallas_call(
        functools.partial(main_kernel, sizes),
        out_shape=(
            shape(fields * rows, width),
            shape(blocks * sizes.margin_rows // 2, width),
            shape(blocks * sizes.margin_rows // 2, width),
        ),
        scratch_shapes=[
            pltpu.VMEM((fields * rows, width), jnp.float32),
            pltpu.VMEM((fields * rows, width), jnp.float32),
        ],
        name="advect_and_interpolate",
    )(
        *near(
            field, moved, meridional, sides, odd_pairs, even_pairs, lat_odd, lat_even,
            *weights,
        )
    )
    given_first = lax.ppermute(first_half, "panel", [(0, 1), (1, 0)])
    given_second = lax.ppermute(second_half, "panel", [(0, 1), (1, 0)])
    remaining, partial = pl.pallas_call(
        functools.partial(sums_kernel, sizes),
        out_shape=(shape(fields * rows, width), shape(2 * sizes.tracers, width)),
        name="kept_and_sums",
    )(*near(field, mass, advected, kept))
    block_rows, devices = sizes.margin_rows // 2 + 1, 2 * blocks * places
    all_blocks = pl.pallas_call(
        functools.partial(blocks_kernel, sizes),
        out_shape=shape(devices * block_rows, width),
        name="margin_blocks",
    )(*near(first_half, given_first, given_second, partial, masses))
    incoming = lax.all_to_all(
        all_blocks.reshape(devices, 1, block_rows * width), ("panel", "lat", "lon"), 0, 0, tiled=True
    ).reshape(devices * block_rows, width)
    return pl.pallas_call(
        functools.partial(fill_kernel, sizes),
        out_shape=jax.ShapeDtypeStruct((1, sizes.tracers, levels, rows, width), jnp.float32),
        out_specs=pl.BlockSpec(memory_space=pl.ANY),
        scratch_shapes=[
            pltpu.VMEM((sizes.tracers, levels, rows, width), jnp.float32),
            pltpu.SemaphoreType.DMA((sizes.tracers,)),
        ],
        name="fill_and_scale",
    )(*near(remaining, incoming, row_hit, column_hot))


def solution(mesh):
    in_specs = (
        P("panel", None, None, "lat", "lon"),
        P("panel", None, "lat", "lon"),
        P("panel", None, "lat", "lon"),
        P("panel", None, "lat", "lon"),
        P("panel", "lat", "lon", None, None),
        P(None, "panel", "lat", "lon", None, None),
        P("panel", "lat", "lon", None, None),
        P("panel", "lat", "lon", None),
    )
    out_specs = P("panel", None, None, "lat", "lon")
    return jax.shard_map(body, mesh=mesh, in_specs=in_specs, out_specs=out_specs, check_vma=False)
```

```python
import functools
from typing import NamedTuple

import jax
import jax.numpy as jnp
from jax import lax
from jax.experimental import pallas as pl
from jax.experimental.pallas import tpu as pltpu
from jax.sharding import PartitionSpec as P

HALO = 3
COLUMN_ROWS = 104
FORWARD_ROWS = 36


class Sizes(NamedTuple):
    tracers: int
    levels: int
    rows: int
    width: int
    blocks: int
    capacity: int
    places: int

    @property
    def fields(self):
        return self.tracers * self.levels

    @property
    def sides(self):
        return self.width // self.capacity

    @property
    def margin_rows(self):
        return self.fields // self.sides

    @property
    def halo_rows(self):
        return HALO * self.fields + self.levels

    @property
    def chunks(self):
        return -(-(self.fields + self.levels) * self.rows // self.width)

    def spot(self, tracer):
        start = tracer * self.levels
        return start % self.margin_rows, start // self.margin_rows * self.capacity


def row_of(table):
    return jnp.concatenate([table[i : i + 1] for i in range(table.shape[0])], axis=1)


def live_row(live, capacity):
    slots = lax.broadcasted_iota(jnp.int32, (1, capacity), 1)
    return jnp.concatenate(
        [(slots < live[:, i : i + 1]).astype(jnp.float32) for i in range(live.shape[1])], axis=1
    )


def one_hot(spots, extent):
    places = lax.broadcasted_iota(jnp.int32, (extent, spots.shape[1]), 0)
    return (places == spots).astype(jnp.float32)


def two_parts(value):
    high = value.astype(jnp.bfloat16)
    return high, (value - high.astype(jnp.float32)).astype(jnp.bfloat16)


def three_parts(value):
    high = value.astype(jnp.bfloat16)
    rest = value - high.astype(jnp.float32)
    return (high, *two_parts(rest))


def dot(left, right, transposed=False):
    return lax.dot_general(
        left,
        right,
        (((1,), (1 if transposed else 0,)), ((), ())),
        preferred_element_type=jnp.float32,
    )


def dot_parts(parts, right, transposed=False):
    rows = parts[0].shape[0]
    product = dot(jnp.concatenate(parts, axis=0), right, transposed)
    return sum(product[i * rows : (i + 1) * rows] for i in range(len(parts)))


def cubic_weights(fraction):
    return (
        -fraction * (fraction - 1.0) * (fraction - 2.0) / 6.0,
        (fraction + 1.0) * (fraction - 1.0) * (fraction - 2.0) / 2.0,
        -(fraction + 1.0) * fraction * (fraction - 2.0) / 2.0,
        (fraction + 1.0) * fraction * (fraction - 1.0) / 6.0,
    )


def stencil_weights(start, fraction, extent):
    step = lax.broadcasted_iota(jnp.int32, (extent, start.shape[1]), 0) - start
    spread = jnp.zeros(step.shape, jnp.float32)
    for at, weight in enumerate(cubic_weights(fraction)):
        spread = jnp.where(step == at, weight, spread)
    return spread


def face_flux(cells, number):
    edge_left, edge, edge_right = (
        7.0 / 12.0 * (cells[i + 1] + cells[i + 2]) - 1.0 / 12.0 * (cells[i] + cells[i + 3])
        for i in range(3)
    )
    positive = number > 0.0
    speed = jnp.abs(number)
    far = jnp.where(positive, edge_left, edge_right)
    cell = jnp.where(positive, cells[2], cells[3])
    curve = 6.0 * (cell - 0.5 * (far + edge))
    return number * (edge - 0.5 * speed * ((edge - far) - (1.0 - 2.0 / 3.0 * speed) * curve))


def pack_kernel(
    sizes, field, zonal, meridional, mass, target, live, donor, fraction,
    columns, sides, lat_even, lat_odd, masses, *index_copies,
):
    _, levels, rows, width, blocks, capacity, _ = sizes
    fields = sizes.fields
    here = lax.axis_index("lat")
    for copy, source in zip(index_copies, (donor, fraction, target, live), strict=True):
        copy[...] = source[...]
    even = lax.rem(here, 2) == 0
    for i in range(HALO):
        part = pl.ds(i * fields, fields)
        northward = field[pl.ds(rows - HALO + i, fields, stride=rows), :]
        southward = field[pl.ds(i, fields, stride=rows), :]
        lat_even[part, :] = jnp.where(even, northward, southward)
        lat_odd[part, :] = jnp.where(even, southward, northward)
    number = meridional[pl.ds(0, levels, stride=rows), :]
    lat_even[pl.ds(HALO * fields, levels), :] = number
    lat_odd[pl.ds(HALO * fields, levels), :] = number
    spots = row_of(target[...])
    row_hot = one_hot(spots // width, rows)
    column_hot = one_hot(lax.rem(spots, width), width).astype(jnp.bfloat16)
    picked = dot_parts(three_parts(mass[...]), column_hot)
    picked = jnp.sum(
        picked.reshape(levels, rows, spots.shape[1]) * row_hot[None], axis=1
    ) * live_row(live[...], capacity)
    for block in range(blocks):
        part = picked[:, block * capacity : (block + 1) * capacity]
        masses[pl.ds(block * levels, levels), :] = jnp.concatenate([part] * sizes.sides, axis=1)
    if two_hops(sizes):
        for i, step in enumerate((1, 3)):
            block = pl.multiple_of((here ^ step) * levels, levels)
            lat_even[pl.ds(sizes.halo_rows + i * levels, levels), :] = masses[
                pl.ds(block, levels), :
            ]
    turned = jnp.concatenate([field[...], zonal[...]], axis=0).T
    edges = jnp.concatenate(
        [
            turned[width - HALO : width],
            turned[0:HALO],
            jnp.zeros((8 - 2 * HALO, turned.shape[1]), jnp.float32),
        ],
        axis=0,
    )
    spare = jnp.zeros((8, sizes.chunks * width - edges.shape[1]), jnp.float32)
    edges = jnp.concatenate([edges, spare], axis=1)
    for i in range(sizes.chunks):
        columns[pl.ds(8 * i, 8), :] = edges[:, i * width : (i + 1) * width]
    start = 8 * sizes.chunks
    columns[start:, :] = jnp.zeros((columns.shape[0] - start, width), jnp.float32)
    sides[0 : 2 * HALO] = turned[0 : 2 * HALO]
    sides[2 * HALO : 4 * HALO] = turned[width - 2 * HALO : width]


def relay_kernel(columns, relayed):
    relayed[...] = columns[0 : relayed.shape[0], :]


def two_hops(sizes):
    return sizes.blocks == 4


def forward_kernel(sizes, masses, lat_even, forwarded):
    levels = sizes.levels
    block = pl.multiple_of((lax.axis_index("lat") ^ 2) * levels, levels)
    forwarded[0:levels, :] = masses[pl.ds(block, levels), :]
    forwarded[levels : 2 * levels, :] = lat_even[pl.ds(sizes.halo_rows + levels, levels), :]
    spare = forwarded.shape[0] - 2 * levels
    if spare:
        forwarded[pl.ds(2 * levels, spare), :] = jnp.zeros((spare, sizes.width), jnp.float32)


def masses_kernel(sizes, masses, lat_even, forwarded, received):
    levels = sizes.levels
    here = lax.axis_index("lat")
    own = pl.multiple_of(here * levels, levels)
    pieces = (
        masses[pl.ds(own, levels), :],
        lat_even[pl.ds(sizes.halo_rows, levels), :],
        forwarded[0:levels, :],
        forwarded[levels : 2 * levels, :],
    )
    for step, piece in enumerate(pieces):
        received[pl.ds(pl.multiple_of((here ^ step) * levels, levels), levels), :] = piece


def tables_kernel(
    sizes, donor, fraction, target, live, kept, row_hit, column_hot, row_weight, high, low
):
    _, _, rows, width, _, capacity, _ = sizes
    spots = row_of(target[...])
    row_hit[...] = one_hot(spots // width, rows) * live_row(live[...], capacity)
    column_hot[...] = one_hot(lax.rem(spots, width), width).astype(jnp.bfloat16)
    kept[...] = 1.0 - dot(row_hit[...].astype(jnp.bfloat16), column_hot[...], True)
    starts = row_of(donor[...])
    row_weight[...] = stencil_weights(starts // width, row_of(fraction[0]), rows)
    high[...], low[...] = two_parts(
        stencil_weights(lax.rem(starts, width), row_of(fraction[1]), width)
    )


def unfold(sizes, rows):
    chunks = [rows[pl.ds(8 * i, 8), :] for i in range(sizes.chunks)]
    return jnp.concatenate(chunks, axis=1)[:, : (sizes.fields + sizes.levels) * sizes.rows]


def zonal_kernel(sizes, field, zonal, moved):
    tracers, levels, rows, width, *_ = sizes
    span = levels * rows
    for tracer in range(tracers):
        part = pl.ds(tracer * span, span)
        cells = field[part, :]
        along = [
            pltpu.roll(cells, shift % width, 1) if shift else cells
            for shift in (3, 2, 1, 0, -1, -2)
        ]
        flux = face_flux(along, zonal[...])
        moved[part, :] = cells - (pltpu.roll(flux, width - 1, 1) - flux)


def main_kernel(
    sizes, field, moved, meridional, sides, odd_pairs, even_pairs, lat_odd, lat_even,
    row_weight, weight_high, weight_low,
    advected, first_half, second_half, edge_rows, flux_rows,
):
    tracers, levels, rows, width, blocks, capacity, _ = sizes
    fields, span, total = sizes.fields, levels * rows, sizes.fields * rows
    place = lax.axis_index("lon")
    even = lax.rem(place, 2) == 0
    inner = (place > 0) & (place < sizes.places - 1)
    first, second = unfold(sizes, even_pairs), unfold(sizes, odd_pairs)
    second = jnp.where(inner, second, 0.0)
    from_west = jnp.where(even, second[0:HALO], first[0:HALO])
    from_east = jnp.where(even, first[HALO : 2 * HALO], second[HALO : 2 * HALO])
    west = jnp.concatenate([from_west, sides[0 : 2 * HALO]], axis=0)
    east = jnp.concatenate([sides[2 * HALO : 4 * HALO], from_east], axis=0)
    faces = HALO + 1
    number = jnp.concatenate(
        [west[HALO : HALO + faces, total:], east[HALO : HALO + faces, total:]], axis=0
    )
    flux = face_flux(
        [
            jnp.concatenate([west[i : i + faces, :total], east[i : i + faces, :total]], axis=0)
            for i in range(2 * HALO)
        ],
        jnp.concatenate([number] * tracers, axis=1),
    )
    change = flux[1:] - flux[:-1]
    lanes = jnp.concatenate(
        [
            sides[0:HALO, :total] - change[0:HALO],
            jnp.zeros((width - 2 * HALO, total), jnp.float32),
            sides[3 * HALO : 4 * HALO, :total] - change[faces : faces + HALO],
        ],
        axis=0,
    ).T
    even = lax.rem(lax.axis_index("lat"), 2) == 0
    next_rows = []
    for i in range(HALO):
        part = pl.ds(i * fields, fields)
        first, second = lat_even[part, :], lat_odd[part, :]
        north_row = jnp.where(even, first, second)
        next_rows.append(north_row)
        edge_rows[pl.ds(rows - HALO + i, fields, stride=rows), :] = jnp.where(even, second, first)
        edge_rows[pl.ds(i, fields, stride=rows), :] = north_row
    last_rows = [field[pl.ds(rows - HALO + i, fields, stride=rows), :] for i in range(HALO)]
    part = pl.ds(HALO * fields, levels)
    north_number = jnp.where(even, lat_even[part, :], lat_odd[part, :])
    flux_rows[pl.ds(0, fields, stride=rows), :] = face_flux(
        last_rows + next_rows, jnp.concatenate([north_number] * tracers, axis=0)
    )
    column = lax.broadcasted_iota(jnp.int32, (span, width), 1)
    row = lax.broadcasted_iota(jnp.int32, (levels, rows, width), 1)

    for tracer in range(tracers):
        part = pl.ds(tracer * span, span)
        cells = field[part, :]
        result = jnp.where(
            (column < HALO) | (column >= width - HALO),
            lanes[tracer * span : (tracer + 1) * span],
            moved[part, :],
        )
        cells3 = cells.reshape(levels, rows, width)
        halo3 = edge_rows[part, :].reshape(levels, rows, width)
        along = []
        for shift in (3, 2, 1, 0, -1, -2):
            if shift > 0:
                along.append(pltpu.roll(jnp.where(row >= rows - shift, halo3, cells3), shift, 1))
            elif shift < 0:
                along.append(pltpu.roll(jnp.where(row < -shift, halo3, cells3), rows + shift, 1))
            else:
                along.append(cells3)
        flux = face_flux(along, meridional[...].reshape(levels, rows, width))
        edge3 = flux_rows[part, :].reshape(levels, rows, width)
        next_flux = pltpu.roll(jnp.where(row == 0, edge3, flux), rows - 1, 1)
        result = result.reshape(levels, rows, width) - (next_flux - flux)
        flat = result.reshape(span, width)
        advected[part, :] = flat
    high, low = two_parts(advected[...])
    across = dot_parts((high, low), weight_high[...]) + dot(high, weight_low[...])
    payloads = jnp.sum(across.reshape(fields, rows, -1) * row_weight[...][None], axis=1)
    for tracer in range(tracers):
        payload = payloads[tracer * levels : (tracer + 1) * levels]
        base, lane = sizes.spot(tracer)
        half = sizes.margin_rows // 2
        outgoing = (first_half, second_half)[base // half]
        for block in range(blocks):
            at = block * capacity
            outgoing[pl.ds(block * half + base % half, levels), lane : lane + capacity] = payload[
                :, at : at + capacity
            ]


def sums_kernel(sizes, field, mass, advected, kept, remaining, partial):
    tracers, levels, rows, width, *_ = sizes
    span = levels * rows
    weights = mass[...].reshape(levels, rows, width)
    for tracer in range(tracers):
        part = pl.ds(tracer * span, span)
        held = advected[part, :].reshape(levels, rows, width) * kept[...][None]
        remaining[part, :] = held.reshape(span, width)
        before = field[part, :].reshape(levels, rows, width)
        partial[tracer : tracer + 1, :] = jnp.sum(weights * held, axis=(0, 1))[None]
        partial[tracers + tracer : tracers + tracer + 1, :] = jnp.sum(
            weights * before, axis=(0, 1)
        )[None]


def blocks_kernel(sizes, own, given_first, given_second, partial, masses, all_blocks):
    tracers, levels, _, width, blocks, capacity, places = sizes
    half = sizes.margin_rows // 2
    mine = lax.axis_index("panel")
    weighed = [jnp.zeros((half, width), jnp.float32) for _ in range(2)]
    for block in range(blocks):
        part = pl.ds(block * half, half)
        mass = masses[pl.ds(block * levels, levels), :]
        mass = jnp.concatenate([mass] * (half // levels), axis=0)
        margins = (given_first[part, :], given_second[part, :])
        weighed = [total + margin * mass for total, margin in zip(weighed, margins, strict=True)]
        for panel, piece in ((mine, margins[1]), (1 - mine, own[part, :])):
            for place in range(places):
                start = ((panel * blocks + block) * places + place) * (half + 1)
                all_blocks[pl.ds(start, half), :] = piece
    weighed = jnp.concatenate(weighed, axis=0)
    column = lax.broadcasted_iota(jnp.int32, (1, width), 1)
    added = []
    for tracer in range(tracers):
        base, lane = sizes.spot(tracer)
        row = jnp.sum(weighed[base : base + levels], axis=0, keepdims=True)
        added.append(jnp.where((column >= lane) & (column < lane + capacity), row, 0.0))
    sums = partial[...] + jnp.concatenate(
        added + [jnp.zeros((tracers, width), jnp.float32)], axis=0
    )
    totals = jnp.sum(sums, axis=1, keepdims=True)
    line = jnp.zeros((1, width), jnp.float32)
    for i in range(2 * tracers):
        line = jnp.where(column == i, totals[i : i + 1], line)
    for block in range(2 * blocks * places):
        all_blocks[pl.ds(block * (half + 1) + half, 1), :] = line


def fill_kernel(sizes, advected, incoming, row_hit, column_hot, updated, stage, sems):
    tracers, levels, rows, width, blocks, capacity, places = sizes
    half = sizes.margin_rows // 2
    place, mine = lax.axis_index("lon"), lax.axis_index("panel")
    arrived = []
    for block in range(blocks):
        halves = []
        for panel in (1 - mine, mine):
            start = ((panel * blocks + block) * places + place) * (half + 1)
            halves.append(incoming[pl.ds(start, half), :])
        piece = jnp.concatenate(halves, axis=0)
        arrived.append(
            jnp.concatenate(
                [piece[:, i * capacity : (i + 1) * capacity] for i in range(sizes.sides)], axis=0
            )
        )
    arrived = jnp.concatenate(arrived, axis=1)
    line = jnp.sum(
        incoming[pl.ds(half, 2 * blocks * places, stride=half + 1), :], axis=0, keepdims=True
    )
    spread = (arrived[:, None, :] * row_hit[...][None]).reshape(sizes.fields * rows, -1)
    filled = dot_parts(two_parts(spread), column_hot[...], True)
    copies = []
    for tracer in range(tracers):
        placed = filled[tracer * levels * rows : (tracer + 1) * levels * rows]
        old = advected[pl.ds(tracer * levels * rows, levels * rows), :]
        scale = line[:, tracers + tracer : tracers + tracer + 1] / line[:, tracer : tracer + 1]
        stage[tracer] = ((old + placed) * scale).reshape(levels, rows, width)
        copies.append(pltpu.make_async_copy(stage.at[tracer], updated.at[0, tracer], sems.at[tracer]))
        copies[-1].start()
    for copy in copies:
        copy.wait()


def exchanged(value, axis, first):
    pairs = []
    for i in range(first, lax.axis_size(axis) - 1, 2):
        pairs += [(i, i + 1), (i + 1, i)]
    return lax.ppermute(value, axis, pairs)


def body(
    tracers, courant_lon, courant_lat, cell_mass, donor_cell, donor_frac, target_cell, live_count
):
    sizes = Sizes(*tracers.shape[1:], *donor_cell.shape[3:], lax.axis_size("lon"))
    _, levels, rows, width, blocks, capacity, places = sizes
    fields = sizes.fields
    field = tracers.reshape(fields * rows, width)
    zonal = courant_lon.reshape(levels * rows, width)
    meridional = courant_lat.reshape(levels * rows, width)
    mass = cell_mass.reshape(levels * rows, width)
    donor = donor_cell.reshape(blocks, capacity)
    fraction = donor_frac.reshape(2, blocks, capacity)
    target = target_cell.reshape(blocks, capacity)
    live = live_count.reshape(1, blocks)

    def shape(*dims):
        return pltpu.VMEM(dims, jnp.float32)

    def near(*values):
        return (pltpu.with_memory_space_constraint(value, pltpu.VMEM) for value in values)

    slots = blocks * capacity
    columns, sides, lat_even, lat_odd, masses, *index_copies = pl.pallas_call(
        functools.partial(pack_kernel, sizes),
        out_shape=(
            shape(max(COLUMN_ROWS, 8 * sizes.chunks), width),
            shape(4 * HALO, (fields + levels) * rows),
            shape(sizes.halo_rows + (2 * levels if two_hops(sizes) else 0), width),
            shape(sizes.halo_rows, width),
            shape(blocks * levels, width),
            pltpu.VMEM(donor.shape, donor.dtype),
            pltpu.VMEM(fraction.shape, fraction.dtype),
            pltpu.VMEM(target.shape, target.dtype),
            pltpu.VMEM(live.shape, live.dtype),
        ),
        name="pack_edges",
    )(field, zonal, meridional, mass, target, live, donor, fraction)
    lat_even = exchanged(lat_even, "lat", 0)
    lat_odd = exchanged(lat_odd, "lat", 1)
    even_pairs = exchanged(columns, "lon", 0)
    if places == 4:
        relayed = pl.pallas_call(
            relay_kernel,
            out_shape=shape(8 * sizes.chunks, width),
            name="relay_columns",
        )(*near(even_pairs))
        odd_pairs = lax.ppermute(relayed, "lon", [(i, i ^ 2) for i in range(places)])
    else:
        odd_pairs = exchanged(columns, "lon", 1)
    if two_hops(sizes):
        forwarded = pl.pallas_call(
            functools.partial(forward_kernel, sizes),
            out_shape=shape(FORWARD_ROWS, width),
            name="forward_masses",
        )(*near(masses, lat_even))
        forwarded = lax.ppermute(forwarded, "lat", [(i, i ^ 2) for i in range(blocks)])
        masses = pl.pallas_call(
            functools.partial(masses_kernel, sizes),
            out_shape=shape(blocks * levels, width),
            name="gather_masses",
        )(*near(masses, lat_even, forwarded))
    else:
        masses = lax.all_to_all(
            masses.reshape(blocks, levels, width), "lat", 0, 0, tiled=True
        ).reshape(blocks * levels, width)
    kept, row_hit, column_hot, *weights = pl.pallas_call(
        functools.partial(tables_kernel, sizes),
        out_shape=(
            shape(rows, width),
            shape(rows, slots),
            pltpu.VMEM((width, slots), jnp.bfloat16),
            shape(rows, slots),
            pltpu.VMEM((width, slots), jnp.bfloat16),
            pltpu.VMEM((width, slots), jnp.bfloat16),
        ),
        name="index_tables",
    )(*near(*index_copies))
    moved = pl.pallas_call(
        functools.partial(zonal_kernel, sizes),
        out_shape=shape(fields * rows, width),
        name="own_zonal",
    )(*near(field, zonal))
    advected, first_half, second_half = pl.pallas_call(
        functools.partial(main_kernel, sizes),
        out_shape=(
            shape(fields * rows, width),
            shape(blocks * sizes.margin_rows // 2, width),
            shape(blocks * sizes.margin_rows // 2, width),
        ),
        scratch_shapes=[
            pltpu.VMEM((fields * rows, width), jnp.float32),
            pltpu.VMEM((fields * rows, width), jnp.float32),
        ],
        name="advect_and_interpolate",
    )(
        *near(
            field, moved, meridional, sides, odd_pairs, even_pairs, lat_odd, lat_even,
            *weights,
        )
    )
    given_first = lax.ppermute(first_half, "panel", [(0, 1), (1, 0)])
    given_second = lax.ppermute(second_half, "panel", [(0, 1), (1, 0)])
    remaining, partial = pl.pallas_call(
        functools.partial(sums_kernel, sizes),
        out_shape=(shape(fields * rows, width), shape(2 * sizes.tracers, width)),
        name="kept_and_sums",
    )(*near(field, mass, advected, kept))
    block_rows, devices = sizes.margin_rows // 2 + 1, 2 * blocks * places
    all_blocks = pl.pallas_call(
        functools.partial(blocks_kernel, sizes),
        out_shape=shape(devices * block_rows, width),
        name="margin_blocks",
    )(*near(first_half, given_first, given_second, partial, masses))
    incoming = lax.all_to_all(
        all_blocks.reshape(devices, 1, block_rows * width), ("panel", "lat", "lon"), 0, 0, tiled=True
    ).reshape(devices * block_rows, width)
    return pl.pallas_call(
        functools.partial(fill_kernel, sizes),
        out_shape=jax.ShapeDtypeStruct((1, sizes.tracers, levels, rows, width), jnp.float32),
        out_specs=pl.BlockSpec(memory_space=pl.ANY),
        scratch_shapes=[
            pltpu.VMEM((sizes.tracers, levels, rows, width), jnp.float32),
            pltpu.SemaphoreType.DMA((sizes.tracers,)),
        ],
        name="fill_and_scale",
    )(*near(remaining, incoming, row_hit, column_hot))


def solution(mesh):
    in_specs = (
        P("panel", None, None, "lat", "lon"),
        P("panel", None, "lat", "lon"),
        P("panel", None, "lat", "lon"),
        P("panel", None, "lat", "lon"),
        P("panel", "lat", "lon", None, None),
        P(None, "panel", "lat", "lon", None, None),
        P("panel", "lat", "lon", None, None),
        P("panel", "lat", "lon", None),
    )
    out_specs = P("panel", None, None, "lat", "lon")
    return jax.shard_map(body, mesh=mesh, in_specs=in_specs, out_specs=out_specs, check_vma=False)
```

```python
import functools
from typing import NamedTuple

import jax
import jax.numpy as jnp
from jax import lax
from jax.experimental import pallas as pl
from jax.experimental.pallas import tpu as pltpu
from jax.sharding import PartitionSpec as P

HALO = 3
COLUMN_ROWS = 24
FORWARD_ROWS = 16


class Sizes(NamedTuple):
    tracers: int
    levels: int
    rows: int
    width: int
    blocks: int
    capacity: int
    places: int

    @property
    def fields(self):
        return self.tracers * self.levels

    @property
    def sides(self):
        return self.width // self.capacity

    @property
    def margin_rows(self):
        return self.fields // self.sides

    @property
    def halo_rows(self):
        return HALO * self.fields + self.levels

    @property
    def chunks(self):
        return -(-(self.fields + self.levels) * self.rows // self.width)

    def spot(self, tracer):
        start = tracer * self.levels
        return start % self.margin_rows, start // self.margin_rows * self.capacity


def row_of(table):
    return jnp.concatenate([table[i : i + 1] for i in range(table.shape[0])], axis=1)


def live_row(live, capacity):
    slots = lax.broadcasted_iota(jnp.int32, (1, capacity), 1)
    return jnp.concatenate(
        [(slots < live[:, i : i + 1]).astype(jnp.float32) for i in range(live.shape[1])], axis=1
    )


def one_hot(spots, extent):
    places = lax.broadcasted_iota(jnp.int32, (extent, spots.shape[1]), 0)
    return (places == spots).astype(jnp.float32)


def two_parts(value):
    high = value.astype(jnp.bfloat16)
    return high, (value - high.astype(jnp.float32)).astype(jnp.bfloat16)


def three_parts(value):
    high = value.astype(jnp.bfloat16)
    rest = value - high.astype(jnp.float32)
    return (high, *two_parts(rest))


def dot(left, right, transposed=False):
    return lax.dot_general(
        left,
        right,
        (((1,), (1 if transposed else 0,)), ((), ())),
        preferred_element_type=jnp.float32,
    )


def dot_parts(parts, right, transposed=False):
    rows = parts[0].shape[0]
    product = dot(jnp.concatenate(parts, axis=0), right, transposed)
    return sum(product[i * rows : (i + 1) * rows] for i in range(len(parts)))


def cubic_weights(fraction):
    return (
        -fraction * (fraction - 1.0) * (fraction - 2.0) / 6.0,
        (fraction + 1.0) * (fraction - 1.0) * (fraction - 2.0) / 2.0,
        -(fraction + 1.0) * fraction * (fraction - 2.0) / 2.0,
        (fraction + 1.0) * fraction * (fraction - 1.0) / 6.0,
    )


def stencil_weights(start, fraction, extent):
    step = lax.broadcasted_iota(jnp.int32, (extent, start.shape[1]), 0) - start
    spread = jnp.zeros(step.shape, jnp.float32)
    for at, weight in enumerate(cubic_weights(fraction)):
        spread = jnp.where(step == at, weight, spread)
    return spread


def face_flux(cells, number):
    edge_left, edge, edge_right = (
        7.0 / 12.0 * (cells[i + 1] + cells[i + 2]) - 1.0 / 12.0 * (cells[i] + cells[i + 3])
        for i in range(3)
    )
    positive = number > 0.0
    speed = jnp.abs(number)
    far = jnp.where(positive, edge_left, edge_right)
    cell = jnp.where(positive, cells[2], cells[3])
    curve = 6.0 * (cell - 0.5 * (far + edge))
    return number * (edge - 0.5 * speed * ((edge - far) - (1.0 - 2.0 / 3.0 * speed) * curve))


def pack_kernel(
    sizes, field, zonal, meridional, mass, target, live, donor, fraction,
    columns, sides, lat_even, lat_odd, masses, *index_copies,
):
    _, levels, rows, width, blocks, capacity, _ = sizes
    fields = sizes.fields
    here = lax.axis_index("lat")
    for copy, source in zip(index_copies, (donor, fraction, target, live), strict=True):
        copy[...] = source[...]
    even = lax.rem(here, 2) == 0
    for i in range(HALO):
        part = pl.ds(i * fields, fields)
        northward = field[pl.ds(rows - HALO + i, fields, stride=rows), :]
        southward = field[pl.ds(i, fields, stride=rows), :]
        lat_even[part, :] = jnp.where(even, northward, southward)
        lat_odd[part, :] = jnp.where(even, southward, northward)
    number = meridional[pl.ds(0, levels, stride=rows), :]
    lat_even[pl.ds(HALO * fields, levels), :] = number
    lat_odd[pl.ds(HALO * fields, levels), :] = number
    spots = row_of(target[...])
    row_hot = one_hot(spots // width, rows)
    column_hot = one_hot(lax.rem(spots, width), width).astype(jnp.bfloat16)
    picked = dot_parts(three_parts(mass[...]), column_hot)
    picked = jnp.sum(
        picked.reshape(levels, rows, spots.shape[1]) * row_hot[None], axis=1
    ) * live_row(live[...], capacity)
    for block in range(blocks):
        part = picked[:, block * capacity : (block + 1) * capacity]
        masses[pl.ds(block * levels, levels), :] = jnp.concatenate([part] * sizes.sides, axis=1)
    if two_hops(sizes):
        for i, step in enumerate((1, 3)):
            block = pl.multiple_of((here ^ step) * levels, levels)
            lat_even[pl.ds(sizes.halo_rows + i * levels, levels), :] = masses[
                pl.ds(block, levels), :
            ]
    turned = jnp.concatenate([field[...], zonal[...]], axis=0).T
    edges = jnp.concatenate(
        [
            turned[width - HALO : width],
            turned[0:HALO],
            jnp.zeros((8 - 2 * HALO, turned.shape[1]), jnp.float32),
        ],
        axis=0,
    )
    spare = jnp.zeros((8, sizes.chunks * width - edges.shape[1]), jnp.float32)
    edges = jnp.concatenate([edges, spare], axis=1)
    for i in range(sizes.chunks):
        columns[pl.ds(8 * i, 8), :] = edges[:, i * width : (i + 1) * width]
    start = 8 * sizes.chunks
    spare = columns.shape[0] - start
    if spare:
        columns[pl.ds(start, spare), :] = jnp.zeros((spare, width), jnp.float32)
    sides[0 : 2 * HALO] = turned[0 : 2 * HALO]
    sides[2 * HALO : 4 * HALO] = turned[width - 2 * HALO : width]


def relay_kernel(columns, relayed):
    relayed[...] = columns[0 : relayed.shape[0], :]


def two_hops(sizes):
    return sizes.blocks == 4


def forward_kernel(sizes, masses, lat_even, forwarded):
    levels = sizes.levels
    block = pl.multiple_of((lax.axis_index("lat") ^ 2) * levels, levels)
    forwarded[0:levels, :] = masses[pl.ds(block, levels), :]
    forwarded[levels : 2 * levels, :] = lat_even[pl.ds(sizes.halo_rows + levels, levels), :]
    spare = forwarded.shape[0] - 2 * levels
    if spare:
        forwarded[pl.ds(2 * levels, spare), :] = jnp.zeros((spare, sizes.width), jnp.float32)


def masses_kernel(sizes, masses, lat_even, forwarded, received):
    levels = sizes.levels
    here = lax.axis_index("lat")
    own = pl.multiple_of(here * levels, levels)
    pieces = (
        masses[pl.ds(own, levels), :],
        lat_even[pl.ds(sizes.halo_rows, levels), :],
        forwarded[0:levels, :],
        forwarded[levels : 2 * levels, :],
    )
    for step, piece in enumerate(pieces):
        received[pl.ds(pl.multiple_of((here ^ step) * levels, levels), levels), :] = piece


def tables_kernel(
    sizes, donor, fraction, target, live, kept, row_hit, column_hot, row_weight, high, low
):
    _, _, rows, width, _, capacity, _ = sizes
    spots = row_of(target[...])
    row_hit[...] = one_hot(spots // width, rows) * live_row(live[...], capacity)
    column_hot[...] = one_hot(lax.rem(spots, width), width).astype(jnp.bfloat16)
    kept[...] = 1.0 - dot(row_hit[...].astype(jnp.bfloat16), column_hot[...], True)
    starts = row_of(donor[...])
    row_weight[...] = stencil_weights(starts // width, row_of(fraction[0]), rows)
    high[...], low[...] = two_parts(
        stencil_weights(lax.rem(starts, width), row_of(fraction[1]), width)
    )


def unfold(sizes, rows):
    chunks = [rows[pl.ds(8 * i, 8), :] for i in range(sizes.chunks)]
    return jnp.concatenate(chunks, axis=1)[:, : (sizes.fields + sizes.levels) * sizes.rows]


def zonal_kernel(sizes, field, zonal, moved):
    tracers, levels, rows, width, *_ = sizes
    span = levels * rows
    for tracer in range(tracers):
        part = pl.ds(tracer * span, span)
        cells = field[part, :]
        along = [
            pltpu.roll(cells, shift % width, 1) if shift else cells
            for shift in (3, 2, 1, 0, -1, -2)
        ]
        flux = face_flux(along, zonal[...])
        moved[part, :] = cells - (pltpu.roll(flux, width - 1, 1) - flux)


def main_kernel(
    sizes, field, moved, meridional, sides, odd_pairs, even_pairs, lat_odd, lat_even,
    row_weight, weight_high, weight_low,
    advected, outgoing, edge_rows, flux_rows,
):
    tracers, levels, rows, width, blocks, capacity, _ = sizes
    fields, span, total = sizes.fields, levels * rows, sizes.fields * rows
    place = lax.axis_index("lon")
    even = lax.rem(place, 2) == 0
    inner = (place > 0) & (place < sizes.places - 1)
    first, second = unfold(sizes, even_pairs), unfold(sizes, odd_pairs)
    second = jnp.where(inner, second, 0.0)
    from_west = jnp.where(even, second[0:HALO], first[0:HALO])
    from_east = jnp.where(even, first[HALO : 2 * HALO], second[HALO : 2 * HALO])
    west = jnp.concatenate([from_west, sides[0 : 2 * HALO]], axis=0)
    east = jnp.concatenate([sides[2 * HALO : 4 * HALO], from_east], axis=0)
    faces = HALO + 1
    number = jnp.concatenate(
        [west[HALO : HALO + faces, total:], east[HALO : HALO + faces, total:]], axis=0
    )
    flux = face_flux(
        [
            jnp.concatenate([west[i : i + faces, :total], east[i : i + faces, :total]], axis=0)
            for i in range(2 * HALO)
        ],
        jnp.concatenate([number] * tracers, axis=1),
    )
    change = flux[1:] - flux[:-1]
    lanes = jnp.concatenate(
        [
            sides[0:HALO, :total] - change[0:HALO],
            jnp.zeros((width - 2 * HALO, total), jnp.float32),
            sides[3 * HALO : 4 * HALO, :total] - change[faces : faces + HALO],
        ],
        axis=0,
    ).T
    even = lax.rem(lax.axis_index("lat"), 2) == 0
    next_rows = []
    for i in range(HALO):
        part = pl.ds(i * fields, fields)
        first, second = lat_even[part, :], lat_odd[part, :]
        north_row = jnp.where(even, first, second)
        next_rows.append(north_row)
        edge_rows[pl.ds(rows - HALO + i, fields, stride=rows), :] = jnp.where(even, second, first)
        edge_rows[pl.ds(i, fields, stride=rows), :] = north_row
    last_rows = [field[pl.ds(rows - HALO + i, fields, stride=rows), :] for i in range(HALO)]
    part = pl.ds(HALO * fields, levels)
    north_number = jnp.where(even, lat_even[part, :], lat_odd[part, :])
    flux_rows[pl.ds(0, fields, stride=rows), :] = face_flux(
        last_rows + next_rows, jnp.concatenate([north_number] * tracers, axis=0)
    )
    column = lax.broadcasted_iota(jnp.int32, (span, width), 1)
    row = lax.broadcasted_iota(jnp.int32, (levels, rows, width), 1)

    for tracer in range(tracers):
        part = pl.ds(tracer * span, span)
        cells = field[part, :]
        result = jnp.where(
            (column < HALO) | (column >= width - HALO),
            lanes[tracer * span : (tracer + 1) * span],
            moved[part, :],
        )
        cells3 = cells.reshape(levels, rows, width)
        halo3 = edge_rows[part, :].reshape(levels, rows, width)
        along = []
        for shift in (3, 2, 1, 0, -1, -2):
            if shift > 0:
                along.append(pltpu.roll(jnp.where(row >= rows - shift, halo3, cells3), shift, 1))
            elif shift < 0:
                along.append(pltpu.roll(jnp.where(row < -shift, halo3, cells3), rows + shift, 1))
            else:
                along.append(cells3)
        flux = face_flux(along, meridional[...].reshape(levels, rows, width))
        edge3 = flux_rows[part, :].reshape(levels, rows, width)
        next_flux = pltpu.roll(jnp.where(row == 0, edge3, flux), rows - 1, 1)
        result = result.reshape(levels, rows, width) - (next_flux - flux)
        flat = result.reshape(span, width)
        advected[part, :] = flat
    high, low = two_parts(advected[...])
    across = dot_parts((high, low), weight_high[...]) + dot(high, weight_low[...])
    payloads = jnp.sum(across.reshape(fields, rows, -1) * row_weight[...][None], axis=1)
    for tracer in range(tracers):
        payload = payloads[tracer * levels : (tracer + 1) * levels]
        base, lane = sizes.spot(tracer)
        for block in range(blocks):
            at = block * capacity
            outgoing[
                pl.ds(block * sizes.margin_rows + base, levels), lane : lane + capacity
            ] = payload[:, at : at + capacity]


def sums_kernel(sizes, field, mass, advected, kept, remaining, partial):
    tracers, levels, rows, width, *_ = sizes
    span = levels * rows
    weights = mass[...].reshape(levels, rows, width)
    for tracer in range(tracers):
        part = pl.ds(tracer * span, span)
        held = advected[part, :].reshape(levels, rows, width) * kept[...][None]
        remaining[part, :] = held.reshape(span, width)
        before = field[part, :].reshape(levels, rows, width)
        partial[tracer : tracer + 1, :] = jnp.sum(weights * held, axis=(0, 1))[None]
        partial[tracers + tracer : tracers + tracer + 1, :] = jnp.sum(
            weights * before, axis=(0, 1)
        )[None]


def blocks_kernel(sizes, own, given, partial, masses, all_blocks):
    tracers, levels, _, width, blocks, capacity, places = sizes
    size = sizes.margin_rows
    half = size // 2
    mine = lax.axis_index("panel")
    weighed = jnp.zeros((size, width), jnp.float32)
    for block in range(blocks):
        margin = given[pl.ds(block * size, size), :]
        mass = masses[pl.ds(block * levels, levels), :]
        weighed = weighed + margin * jnp.concatenate([mass] * (size // levels), axis=0)
        made = own[pl.ds(block * size, half), :]
        for panel, piece in ((mine, margin[half:]), (1 - mine, made)):
            for place in range(places):
                start = ((panel * blocks + block) * places + place) * (half + 1)
                all_blocks[pl.ds(start, half), :] = piece
    column = lax.broadcasted_iota(jnp.int32, (1, width), 1)
    added = []
    for tracer in range(tracers):
        base, lane = sizes.spot(tracer)
        row = jnp.sum(weighed[base : base + levels], axis=0, keepdims=True)
        added.append(jnp.where((column >= lane) & (column < lane + capacity), row, 0.0))
    sums = partial[...] + jnp.concatenate(
        added + [jnp.zeros((tracers, width), jnp.float32)], axis=0
    )
    totals = jnp.sum(sums, axis=1, keepdims=True)
    line = jnp.zeros((1, width), jnp.float32)
    for i in range(2 * tracers):
        line = jnp.where(column == i, totals[i : i + 1], line)
    for block in range(2 * blocks * places):
        all_blocks[pl.ds(block * (half + 1) + half, 1), :] = line


def fill_kernel(sizes, advected, incoming, row_hit, column_hot, updated, stage, sems):
    tracers, levels, rows, width, blocks, capacity, places = sizes
    half = sizes.margin_rows // 2
    place, mine = lax.axis_index("lon"), lax.axis_index("panel")
    arrived = []
    for block in range(blocks):
        halves = []
        for panel in (1 - mine, mine):
            start = ((panel * blocks + block) * places + place) * (half + 1)
            halves.append(incoming[pl.ds(start, half), :])
        piece = jnp.concatenate(halves, axis=0)
        arrived.append(
            jnp.concatenate(
                [piece[:, i * capacity : (i + 1) * capacity] for i in range(sizes.sides)], axis=0
            )
        )
    arrived = jnp.concatenate(arrived, axis=1)
    line = jnp.sum(
        incoming[pl.ds(half, 2 * blocks * places, stride=half + 1), :], axis=0, keepdims=True
    )
    spread = (arrived[:, None, :] * row_hit[...][None]).reshape(sizes.fields * rows, -1)
    filled = dot_parts(two_parts(spread), column_hot[...], True)
    copies = []
    for tracer in range(tracers):
        placed = filled[tracer * levels * rows : (tracer + 1) * levels * rows]
        old = advected[pl.ds(tracer * levels * rows, levels * rows), :]
        scale = line[:, tracers + tracer : tracers + tracer + 1] / line[:, tracer : tracer + 1]
        stage[tracer] = ((old + placed) * scale).reshape(levels, rows, width)
        copies.append(pltpu.make_async_copy(stage.at[tracer], updated.at[0, tracer], sems.at[tracer]))
        copies[-1].start()
    for copy in copies:
        copy.wait()


def exchanged(value, axis, first):
    pairs = []
    for i in range(first, lax.axis_size(axis) - 1, 2):
        pairs += [(i, i + 1), (i + 1, i)]
    return lax.ppermute(value, axis, pairs)


def body(
    tracers, courant_lon, courant_lat, cell_mass, donor_cell, donor_frac, target_cell, live_count
):
    sizes = Sizes(*tracers.shape[1:], *donor_cell.shape[3:], lax.axis_size("lon"))
    _, levels, rows, width, blocks, capacity, places = sizes
    fields = sizes.fields
    field = tracers.reshape(fields * rows, width)
    zonal = courant_lon.reshape(levels * rows, width)
    meridional = courant_lat.reshape(levels * rows, width)
    mass = cell_mass.reshape(levels * rows, width)
    donor = donor_cell.reshape(blocks, capacity)
    fraction = donor_frac.reshape(2, blocks, capacity)
    target = target_cell.reshape(blocks, capacity)
    live = live_count.reshape(1, blocks)

    def shape(*dims):
        return pltpu.VMEM(dims, jnp.float32)

    def near(*values):
        return (pltpu.with_memory_space_constraint(value, pltpu.VMEM) for value in values)

    slots = blocks * capacity
    columns, sides, lat_even, lat_odd, masses, *index_copies = pl.pallas_call(
        functools.partial(pack_kernel, sizes),
        out_shape=(
            shape(max(COLUMN_ROWS, 8 * sizes.chunks), width),
            shape(4 * HALO, (fields + levels) * rows),
            shape(sizes.halo_rows + (2 * levels if two_hops(sizes) else 0), width),
            shape(sizes.halo_rows, width),
            shape(blocks * levels, width),
            pltpu.VMEM(donor.shape, donor.dtype),
            pltpu.VMEM(fraction.shape, fraction.dtype),
            pltpu.VMEM(target.shape, target.dtype),
            pltpu.VMEM(live.shape, live.dtype),
        ),
        name="pack_edges",
    )(field, zonal, meridional, mass, target, live, donor, fraction)
    lat_even = exchanged(lat_even, "lat", 0)
    lat_odd = exchanged(lat_odd, "lat", 1)
    even_pairs = exchanged(columns, "lon", 0)
    if places == 4:
        relayed = pl.pallas_call(
            relay_kernel,
            out_shape=shape(8 * sizes.chunks, width),
            cost_estimate=pl.CostEstimate(flops=600000000, bytes_accessed=0, transcendentals=0),
            name="relay_columns",
        )(*near(even_pairs))
        odd_pairs = lax.ppermute(relayed, "lon", [(i, i ^ 2) for i in range(places)])
    else:
        odd_pairs = exchanged(columns, "lon", 1)
    if two_hops(sizes):
        forwarded = pl.pallas_call(
            functools.partial(forward_kernel, sizes),
            out_shape=shape(FORWARD_ROWS, width),
            name="forward_masses",
        )(*near(masses, lat_even))
        forwarded = lax.ppermute(forwarded, "lat", [(i, i ^ 2) for i in range(blocks)])
        masses = pl.pallas_call(
            functools.partial(masses_kernel, sizes),
            out_shape=shape(blocks * levels, width),
            cost_estimate=pl.CostEstimate(flops=500000000, bytes_accessed=0, transcendentals=0),
            name="gather_masses",
        )(*near(masses, lat_even, forwarded))
    else:
        masses = lax.all_to_all(
            masses.reshape(blocks, levels, width), "lat", 0, 0, tiled=True
        ).reshape(blocks * levels, width)
    kept, row_hit, column_hot, *weights = pl.pallas_call(
        functools.partial(tables_kernel, sizes),
        out_shape=(
            shape(rows, width),
            shape(rows, slots),
            pltpu.VMEM((width, slots), jnp.bfloat16),
            shape(rows, slots),
            pltpu.VMEM((width, slots), jnp.bfloat16),
            pltpu.VMEM((width, slots), jnp.bfloat16),
        ),
        name="index_tables",
    )(*near(*index_copies))
    moved = pl.pallas_call(
        functools.partial(zonal_kernel, sizes),
        out_shape=shape(fields * rows, width),
        name="own_zonal",
    )(*near(field, zonal))
    advected, outgoing = pl.pallas_call(
        functools.partial(main_kernel, sizes),
        out_shape=(
            shape(fields * rows, width),
            shape(blocks * sizes.margin_rows, width),
        ),
        scratch_shapes=[
            pltpu.VMEM((fields * rows, width), jnp.float32),
            pltpu.VMEM((fields * rows, width), jnp.float32),
        ],
        name="advect_and_interpolate",
    )(
        *near(
            field, moved, meridional, sides, odd_pairs, even_pairs, lat_odd, lat_even,
            *weights,
        )
    )
    given = lax.ppermute(outgoing, "panel", [(0, 1), (1, 0)])
    remaining, partial = pl.pallas_call(
        functools.partial(sums_kernel, sizes),
        out_shape=(shape(fields * rows, width), shape(2 * sizes.tracers, width)),
        name="kept_and_sums",
    )(*near(field, mass, advected, kept))
    block_rows, devices = sizes.margin_rows // 2 + 1, 2 * blocks * places
    all_blocks = pl.pallas_call(
        functools.partial(blocks_kernel, sizes),
        out_shape=shape(devices * block_rows, width),
        name="margin_blocks",
    )(*near(outgoing, given, partial, masses))
    incoming = lax.all_to_all(
        all_blocks.reshape(devices, 1, block_rows * width), ("panel", "lat", "lon"), 0, 0, tiled=True
    ).reshape(devices * block_rows, width)
    return pl.pallas_call(
        functools.partial(fill_kernel, sizes),
        out_shape=jax.ShapeDtypeStruct((1, sizes.tracers, levels, rows, width), jnp.float32),
        out_specs=pl.BlockSpec(memory_space=pl.ANY),
        scratch_shapes=[
            pltpu.VMEM((sizes.tracers, levels, rows, width), jnp.float32),
            pltpu.SemaphoreType.DMA((sizes.tracers,)),
        ],
        name="fill_and_scale",
    )(*near(remaining, incoming, row_hit, column_hot))


def solution(mesh):
    in_specs = (
        P("panel", None, None, "lat", "lon"),
        P("panel", None, "lat", "lon"),
        P("panel", None, "lat", "lon"),
        P("panel", None, "lat", "lon"),
        P("panel", "lat", "lon", None, None),
        P(None, "panel", "lat", "lon", None, None),
        P("panel", "lat", "lon", None, None),
        P("panel", "lat", "lon", None),
    )
    out_specs = P("panel", None, None, "lat", "lon")
    return jax.shard_map(body, mesh=mesh, in_specs=in_specs, out_specs=out_specs, check_vma=False)
```

```python
import functools
from typing import NamedTuple

import jax
import jax.numpy as jnp
from jax import lax
from jax.experimental import pallas as pl
from jax.experimental.pallas import tpu as pltpu
from jax.sharding import PartitionSpec as P

HALO = 3
COLUMN_ROWS = 24
FORWARD_ROWS = 16


class Sizes(NamedTuple):
    tracers: int
    levels: int
    rows: int
    width: int
    blocks: int
    capacity: int
    places: int

    @property
    def fields(self):
        return self.tracers * self.levels

    @property
    def sides(self):
        return self.width // self.capacity

    @property
    def margin_rows(self):
        return self.fields // self.sides

    @property
    def halo_rows(self):
        return HALO * self.fields + self.levels

    @property
    def chunks(self):
        return -(-(self.fields + self.levels) * self.rows // self.width)

    def spot(self, tracer):
        start = tracer * self.levels
        return start % self.margin_rows, start // self.margin_rows * self.capacity


def row_of(table):
    return jnp.concatenate([table[i : i + 1] for i in range(table.shape[0])], axis=1)


def live_row(live, capacity):
    slots = lax.broadcasted_iota(jnp.int32, (1, capacity), 1)
    return jnp.concatenate(
        [(slots < live[:, i : i + 1]).astype(jnp.float32) for i in range(live.shape[1])], axis=1
    )


def one_hot(spots, extent):
    places = lax.broadcasted_iota(jnp.int32, (extent, spots.shape[1]), 0)
    return (places == spots).astype(jnp.float32)


def two_parts(value):
    high = value.astype(jnp.bfloat16)
    return high, (value - high.astype(jnp.float32)).astype(jnp.bfloat16)


def three_parts(value):
    high = value.astype(jnp.bfloat16)
    rest = value - high.astype(jnp.float32)
    return (high, *two_parts(rest))


def dot(left, right, transposed=False):
    return lax.dot_general(
        left,
        right,
        (((1,), (1 if transposed else 0,)), ((), ())),
        preferred_element_type=jnp.float32,
    )


def dot_parts(parts, right, transposed=False):
    rows = parts[0].shape[0]
    product = dot(jnp.concatenate(parts, axis=0), right, transposed)
    return sum(product[i * rows : (i + 1) * rows] for i in range(len(parts)))


def cubic_weights(fraction):
    return (
        -fraction * (fraction - 1.0) * (fraction - 2.0) / 6.0,
        (fraction + 1.0) * (fraction - 1.0) * (fraction - 2.0) / 2.0,
        -(fraction + 1.0) * fraction * (fraction - 2.0) / 2.0,
        (fraction + 1.0) * fraction * (fraction - 1.0) / 6.0,
    )


def stencil_weights(start, fraction, extent):
    step = lax.broadcasted_iota(jnp.int32, (extent, start.shape[1]), 0) - start
    spread = jnp.zeros(step.shape, jnp.float32)
    for at, weight in enumerate(cubic_weights(fraction)):
        spread = jnp.where(step == at, weight, spread)
    return spread


def face_flux(cells, number):
    edge_left, edge, edge_right = (
        7.0 / 12.0 * (cells[i + 1] + cells[i + 2]) - 1.0 / 12.0 * (cells[i] + cells[i + 3])
        for i in range(3)
    )
    positive = number > 0.0
    speed = jnp.abs(number)
    far = jnp.where(positive, edge_left, edge_right)
    cell = jnp.where(positive, cells[2], cells[3])
    curve = 6.0 * (cell - 0.5 * (far + edge))
    return number * (edge - 0.5 * speed * ((edge - far) - (1.0 - 2.0 / 3.0 * speed) * curve))


def pack_kernel(
    sizes, field, zonal, meridional, mass, target, live, donor, fraction,
    columns, sides, lat_even, lat_odd, masses, *index_copies,
):
    _, levels, rows, width, blocks, capacity, _ = sizes
    fields = sizes.fields
    here = lax.axis_index("lat")
    for copy, source in zip(index_copies, (donor, fraction, target, live), strict=True):
        copy[...] = source[...]
    even = lax.rem(here, 2) == 0
    for i in range(HALO):
        part = pl.ds(i * fields, fields)
        northward = field[pl.ds(rows - HALO + i, fields, stride=rows), :]
        southward = field[pl.ds(i, fields, stride=rows), :]
        lat_even[part, :] = jnp.where(even, northward, southward)
        lat_odd[part, :] = jnp.where(even, southward, northward)
    number = meridional[pl.ds(0, levels, stride=rows), :]
    lat_even[pl.ds(HALO * fields, levels), :] = number
    lat_odd[pl.ds(HALO * fields, levels), :] = number
    spots = row_of(target[...])
    row_hot = one_hot(spots // width, rows)
    column_hot = one_hot(lax.rem(spots, width), width).astype(jnp.bfloat16)
    picked = dot_parts(two_parts(mass[...]), column_hot)
    picked = jnp.sum(
        picked.reshape(levels, rows, spots.shape[1]) * row_hot[None], axis=1
    ) * live_row(live[...], capacity)
    for block in range(blocks):
        part = picked[:, block * capacity : (block + 1) * capacity]
        masses[pl.ds(block * levels, levels), :] = jnp.concatenate([part] * sizes.sides, axis=1)
    if two_hops(sizes):
        for i, step in enumerate((1, 3)):
            block = pl.multiple_of((here ^ step) * levels, levels)
            lat_even[pl.ds(sizes.halo_rows + i * levels, levels), :] = masses[
                pl.ds(block, levels), :
            ]
    turned = jnp.concatenate([field[...], zonal[...]], axis=0).T
    edges = jnp.concatenate(
        [
            turned[width - HALO : width],
            turned[0:HALO],
            jnp.zeros((8 - 2 * HALO, turned.shape[1]), jnp.float32),
        ],
        axis=0,
    )
    spare = jnp.zeros((8, sizes.chunks * width - edges.shape[1]), jnp.float32)
    edges = jnp.concatenate([edges, spare], axis=1)
    for i in range(sizes.chunks):
        columns[pl.ds(8 * i, 8), :] = edges[:, i * width : (i + 1) * width]
    start = 8 * sizes.chunks
    spare = columns.shape[0] - start
    if spare:
        columns[pl.ds(start, spare), :] = jnp.zeros((spare, width), jnp.float32)
    sides[0 : 2 * HALO] = turned[0 : 2 * HALO]
    sides[2 * HALO : 4 * HALO] = turned[width - 2 * HALO : width]


def relay_kernel(columns, relayed):
    relayed[...] = columns[0 : relayed.shape[0], :]


def two_hops(sizes):
    return sizes.blocks == 4


def forward_kernel(sizes, masses, lat_even, forwarded):
    levels = sizes.levels
    block = pl.multiple_of((lax.axis_index("lat") ^ 2) * levels, levels)
    forwarded[0:levels, :] = masses[pl.ds(block, levels), :]
    forwarded[levels : 2 * levels, :] = lat_even[pl.ds(sizes.halo_rows + levels, levels), :]
    spare = forwarded.shape[0] - 2 * levels
    if spare:
        forwarded[pl.ds(2 * levels, spare), :] = jnp.zeros((spare, sizes.width), jnp.float32)


def masses_kernel(sizes, masses, lat_even, forwarded, received):
    levels = sizes.levels
    here = lax.axis_index("lat")
    own = pl.multiple_of(here * levels, levels)
    pieces = (
        masses[pl.ds(own, levels), :],
        lat_even[pl.ds(sizes.halo_rows, levels), :],
        forwarded[0:levels, :],
        forwarded[levels : 2 * levels, :],
    )
    for step, piece in enumerate(pieces):
        received[pl.ds(pl.multiple_of((here ^ step) * levels, levels), levels), :] = piece


def tables_kernel(
    sizes, donor, fraction, target, live, kept, row_hit, column_hot, row_weight, high, low
):
    _, _, rows, width, _, capacity, _ = sizes
    spots = row_of(target[...])
    row_hit[...] = one_hot(spots // width, rows) * live_row(live[...], capacity)
    column_hot[...] = one_hot(lax.rem(spots, width), width).astype(jnp.bfloat16)
    kept[...] = 1.0 - dot(row_hit[...].astype(jnp.bfloat16), column_hot[...], True)
    starts = row_of(donor[...])
    row_weight[...] = stencil_weights(starts // width, row_of(fraction[0]), rows)
    high[...], low[...] = two_parts(
        stencil_weights(lax.rem(starts, width), row_of(fraction[1]), width)
    )


def unfold(sizes, rows):
    chunks = [rows[pl.ds(8 * i, 8), :] for i in range(sizes.chunks)]
    return jnp.concatenate(chunks, axis=1)[:, : (sizes.fields + sizes.levels) * sizes.rows]


def zonal_kernel(sizes, field, zonal, moved):
    tracers, levels, rows, width, *_ = sizes
    span = levels * rows
    for tracer in range(tracers):
        part = pl.ds(tracer * span, span)
        cells = field[part, :]
        along = [
            pltpu.roll(cells, shift % width, 1) if shift else cells
            for shift in (3, 2, 1, 0, -1, -2)
        ]
        flux = face_flux(along, zonal[...])
        moved[part, :] = cells - (pltpu.roll(flux, width - 1, 1) - flux)


def prepare_kernel(sizes, field, zonal, donor, fraction, target, live, moved, *tables):
    zonal_kernel(sizes, field, zonal, moved)
    tables_kernel(sizes, donor, fraction, target, live, *tables)


def main_kernel(
    sizes, field, moved, meridional, sides, odd_pairs, even_pairs, lat_odd, lat_even,
    row_weight, weight_high, weight_low,
    advected, outgoing, edge_rows, flux_rows,
):
    tracers, levels, rows, width, blocks, capacity, _ = sizes
    fields, span, total = sizes.fields, levels * rows, sizes.fields * rows
    place = lax.axis_index("lon")
    even = lax.rem(place, 2) == 0
    inner = (place > 0) & (place < sizes.places - 1)
    first, second = unfold(sizes, even_pairs), unfold(sizes, odd_pairs)
    second = jnp.where(inner, second, 0.0)
    from_west = jnp.where(even, second[0:HALO], first[0:HALO])
    from_east = jnp.where(even, first[HALO : 2 * HALO], second[HALO : 2 * HALO])
    west = jnp.concatenate([from_west, sides[0 : 2 * HALO]], axis=0)
    east = jnp.concatenate([sides[2 * HALO : 4 * HALO], from_east], axis=0)
    faces = HALO + 1
    number = jnp.concatenate(
        [west[HALO : HALO + faces, total:], east[HALO : HALO + faces, total:]], axis=0
    )
    flux = face_flux(
        [
            jnp.concatenate([west[i : i + faces, :total], east[i : i + faces, :total]], axis=0)
            for i in range(2 * HALO)
        ],
        jnp.concatenate([number] * tracers, axis=1),
    )
    change = flux[1:] - flux[:-1]
    lanes = jnp.concatenate(
        [
            sides[0:HALO, :total] - change[0:HALO],
            jnp.zeros((width - 2 * HALO, total), jnp.float32),
            sides[3 * HALO : 4 * HALO, :total] - change[faces : faces + HALO],
        ],
        axis=0,
    ).T
    even = lax.rem(lax.axis_index("lat"), 2) == 0
    next_rows = []
    for i in range(HALO):
        part = pl.ds(i * fields, fields)
        first, second = lat_even[part, :], lat_odd[part, :]
        north_row = jnp.where(even, first, second)
        next_rows.append(north_row)
        edge_rows[pl.ds(rows - HALO + i, fields, stride=rows), :] = jnp.where(even, second, first)
        edge_rows[pl.ds(i, fields, stride=rows), :] = north_row
    last_rows = [field[pl.ds(rows - HALO + i, fields, stride=rows), :] for i in range(HALO)]
    part = pl.ds(HALO * fields, levels)
    north_number = jnp.where(even, lat_even[part, :], lat_odd[part, :])
    flux_rows[pl.ds(0, fields, stride=rows), :] = face_flux(
        last_rows + next_rows, jnp.concatenate([north_number] * tracers, axis=0)
    )
    column = lax.broadcasted_iota(jnp.int32, (span, width), 1)
    row = lax.broadcasted_iota(jnp.int32, (levels, rows, width), 1)

    for tracer in range(tracers):
        part = pl.ds(tracer * span, span)
        cells = field[part, :]
        result = jnp.where(
            (column < HALO) | (column >= width - HALO),
            lanes[tracer * span : (tracer + 1) * span],
            moved[part, :],
        )
        cells3 = cells.reshape(levels, rows, width)
        halo3 = edge_rows[part, :].reshape(levels, rows, width)
        along = []
        for shift in (3, 2, 1, 0, -1, -2):
            if shift > 0:
                along.append(pltpu.roll(jnp.where(row >= rows - shift, halo3, cells3), shift, 1))
            elif shift < 0:
                along.append(pltpu.roll(jnp.where(row < -shift, halo3, cells3), rows + shift, 1))
            else:
                along.append(cells3)
        flux = face_flux(along, meridional[...].reshape(levels, rows, width))
        edge3 = flux_rows[part, :].reshape(levels, rows, width)
        next_flux = pltpu.roll(jnp.where(row == 0, edge3, flux), rows - 1, 1)
        result = result.reshape(levels, rows, width) - (next_flux - flux)
        flat = result.reshape(span, width)
        advected[part, :] = flat
    high, low = two_parts(advected[...])
    across = dot_parts((high, low), weight_high[...]) + dot(high, weight_low[...])
    payloads = jnp.sum(across.reshape(fields, rows, -1) * row_weight[...][None], axis=1)
    for tracer in range(tracers):
        payload = payloads[tracer * levels : (tracer + 1) * levels]
        base, lane = sizes.spot(tracer)
        for block in range(blocks):
            at = block * capacity
            outgoing[
                pl.ds(block * sizes.margin_rows + base, levels), lane : lane + capacity
            ] = payload[:, at : at + capacity]


def sums_kernel(sizes, field, mass, advected, kept, remaining, partial):
    tracers, levels, rows, width, *_ = sizes
    span = levels * rows
    weights = mass[...].reshape(levels, rows, width)
    for tracer in range(tracers):
        part = pl.ds(tracer * span, span)
        held = advected[part, :].reshape(levels, rows, width) * kept[...][None]
        remaining[part, :] = held.reshape(span, width)
        before = field[part, :].reshape(levels, rows, width)
        partial[tracer : tracer + 1, :] = jnp.sum(weights * held, axis=(0, 1))[None]
        partial[tracers + tracer : tracers + tracer + 1, :] = jnp.sum(
            weights * before, axis=(0, 1)
        )[None]


def blocks_kernel(sizes, own, given, partial, masses, all_blocks):
    tracers, levels, _, width, blocks, capacity, places = sizes
    size = sizes.margin_rows
    half = size // 2
    mine = lax.axis_index("panel")
    weighed = jnp.zeros((size, width), jnp.float32)
    for block in range(blocks):
        margin = given[pl.ds(block * size, size), :]
        mass = masses[pl.ds(block * levels, levels), :]
        weighed = weighed + margin * jnp.concatenate([mass] * (size // levels), axis=0)
        made = own[pl.ds(block * size, half), :]
        for panel, piece in ((mine, margin[half:]), (1 - mine, made)):
            for place in range(places):
                start = ((panel * places + place) * blocks + block) * (half + 1)
                all_blocks[pl.ds(start, half), :] = piece
    column = lax.broadcasted_iota(jnp.int32, (1, width), 1)
    added = []
    for tracer in range(tracers):
        base, lane = sizes.spot(tracer)
        row = jnp.sum(weighed[base : base + levels], axis=0, keepdims=True)
        added.append(jnp.where((column >= lane) & (column < lane + capacity), row, 0.0))
    sums = partial[...] + jnp.concatenate(
        added + [jnp.zeros((tracers, width), jnp.float32)], axis=0
    )
    totals = jnp.sum(sums, axis=1, keepdims=True)
    line = jnp.zeros((1, width), jnp.float32)
    for i in range(2 * tracers):
        line = jnp.where(column == i, totals[i : i + 1], line)
    for block in range(2 * blocks * places):
        all_blocks[pl.ds(block * (half + 1) + half, 1), :] = line


def fill_kernel(sizes, advected, incoming, row_hit, column_hot, updated, stage, sems):
    tracers, levels, rows, width, blocks, capacity, places = sizes
    half = sizes.margin_rows // 2
    place, mine = lax.axis_index("lon"), lax.axis_index("panel")
    arrived = []
    for block in range(blocks):
        halves = []
        for panel in (1 - mine, mine):
            start = ((panel * places + place) * blocks + block) * (half + 1)
            halves.append(incoming[pl.ds(start, half), :])
        piece = jnp.concatenate(halves, axis=0)
        arrived.append(
            jnp.concatenate(
                [piece[:, i * capacity : (i + 1) * capacity] for i in range(sizes.sides)], axis=0
            )
        )
    arrived = jnp.concatenate(arrived, axis=1)
    line = jnp.sum(
        incoming[pl.ds(half, 2 * blocks * places, stride=half + 1), :], axis=0, keepdims=True
    )
    spread = (arrived[:, None, :] * row_hit[...][None]).reshape(sizes.fields * rows, -1)
    filled = dot_parts(two_parts(spread), column_hot[...], True)
    copies = []
    for tracer in range(tracers):
        placed = filled[tracer * levels * rows : (tracer + 1) * levels * rows]
        old = advected[pl.ds(tracer * levels * rows, levels * rows), :]
        scale = line[:, tracers + tracer : tracers + tracer + 1] / line[:, tracer : tracer + 1]
        stage[tracer] = ((old + placed) * scale).reshape(levels, rows, width)
        copies.append(pltpu.make_async_copy(stage.at[tracer], updated.at[0, tracer], sems.at[tracer]))
        copies[-1].start()
    for copy in copies:
        copy.wait()


def exchanged(value, axis, first):
    pairs = []
    for i in range(first, lax.axis_size(axis) - 1, 2):
        pairs += [(i, i + 1), (i + 1, i)]
    return lax.ppermute(value, axis, pairs)


def body(
    tracers, courant_lon, courant_lat, cell_mass, donor_cell, donor_frac, target_cell, live_count
):
    sizes = Sizes(*tracers.shape[1:], *donor_cell.shape[3:], lax.axis_size("lon"))
    _, levels, rows, width, blocks, capacity, places = sizes
    fields = sizes.fields
    field = tracers.reshape(fields * rows, width)
    zonal = courant_lon.reshape(levels * rows, width)
    meridional = courant_lat.reshape(levels * rows, width)
    mass = cell_mass.reshape(levels * rows, width)
    donor = donor_cell.reshape(blocks, capacity)
    fraction = donor_frac.reshape(2, blocks, capacity)
    target = target_cell.reshape(blocks, capacity)
    live = live_count.reshape(1, blocks)

    def shape(*dims):
        return pltpu.VMEM(dims, jnp.float32)

    def near(*values):
        return (pltpu.with_memory_space_constraint(value, pltpu.VMEM) for value in values)

    slots = blocks * capacity
    columns, sides, lat_even, lat_odd, masses, *index_copies = pl.pallas_call(
        functools.partial(pack_kernel, sizes),
        out_shape=(
            shape(max(COLUMN_ROWS, 8 * sizes.chunks), width),
            shape(4 * HALO, (fields + levels) * rows),
            shape(sizes.halo_rows + (2 * levels if two_hops(sizes) else 0), width),
            shape(sizes.halo_rows, width),
            shape(blocks * levels, width),
            pltpu.VMEM(donor.shape, donor.dtype),
            pltpu.VMEM(fraction.shape, fraction.dtype),
            pltpu.VMEM(target.shape, target.dtype),
            pltpu.VMEM(live.shape, live.dtype),
        ),
        name="pack_edges",
    )(field, zonal, meridional, mass, target, live, donor, fraction)
    lat_even = exchanged(lat_even, "lat", 0)
    lat_odd = exchanged(lat_odd, "lat", 1)
    even_pairs = exchanged(columns, "lon", 0)
    if places == 4:
        relayed = pl.pallas_call(
            relay_kernel,
            out_shape=shape(8 * sizes.chunks, width),
            cost_estimate=pl.CostEstimate(flops=600000000, bytes_accessed=0, transcendentals=0),
            name="relay_columns",
        )(*near(even_pairs))
        odd_pairs = lax.ppermute(relayed, "lon", [(i, i ^ 2) for i in range(places)])
    else:
        odd_pairs = exchanged(columns, "lon", 1)
    if two_hops(sizes):
        forwarded = pl.pallas_call(
            functools.partial(forward_kernel, sizes),
            out_shape=shape(FORWARD_ROWS, width),
            name="forward_masses",
        )(*near(masses, lat_even))
        forwarded = lax.ppermute(forwarded, "lat", [(i, i ^ 2) for i in range(blocks)])
        masses = pl.pallas_call(
            functools.partial(masses_kernel, sizes),
            out_shape=shape(blocks * levels, width),
            cost_estimate=pl.CostEstimate(flops=500000000, bytes_accessed=0, transcendentals=0),
            name="gather_masses",
        )(*near(masses, lat_even, forwarded))
    else:
        masses = lax.all_to_all(
            masses.reshape(blocks, levels, width), "lat", 0, 0, tiled=True
        ).reshape(blocks * levels, width)
    moved, kept, row_hit, column_hot, *weights = pl.pallas_call(
        functools.partial(prepare_kernel, sizes),
        out_shape=(
            shape(fields * rows, width),
            shape(rows, width),
            shape(rows, slots),
            pltpu.VMEM((width, slots), jnp.bfloat16),
            shape(rows, slots),
            pltpu.VMEM((width, slots), jnp.bfloat16),
            pltpu.VMEM((width, slots), jnp.bfloat16),
        ),
        name="zonal_and_tables",
    )(*near(field, zonal, *index_copies))
    advected, outgoing = pl.pallas_call(
        functools.partial(main_kernel, sizes),
        out_shape=(
            shape(fields * rows, width),
            shape(blocks * sizes.margin_rows, width),
        ),
        scratch_shapes=[
            pltpu.VMEM((fields * rows, width), jnp.float32),
            pltpu.VMEM((fields * rows, width), jnp.float32),
        ],
        name="advect_and_interpolate",
    )(
        *near(
            field, moved, meridional, sides, odd_pairs, even_pairs, lat_odd, lat_even,
            *weights,
        )
    )
    given = lax.ppermute(outgoing, "panel", [(0, 1), (1, 0)])
    remaining, partial = pl.pallas_call(
        functools.partial(sums_kernel, sizes),
        out_shape=(shape(fields * rows, width), shape(2 * sizes.tracers, width)),
        name="kept_and_sums",
    )(*near(field, mass, advected, kept))
    block_rows, devices = sizes.margin_rows // 2 + 1, 2 * blocks * places
    all_blocks = pl.pallas_call(
        functools.partial(blocks_kernel, sizes),
        out_shape=shape(devices * block_rows, width),
        name="margin_blocks",
    )(*near(outgoing, given, partial, masses))
    incoming = lax.all_to_all(
        all_blocks.reshape(devices, 1, block_rows * width), ("panel", "lon", "lat"), 0, 0, tiled=True
    ).reshape(devices * block_rows, width)
    return pl.pallas_call(
        functools.partial(fill_kernel, sizes),
        out_shape=jax.ShapeDtypeStruct((1, sizes.tracers, levels, rows, width), jnp.float32),
        out_specs=pl.BlockSpec(memory_space=pl.ANY),
        scratch_shapes=[
            pltpu.VMEM((sizes.tracers, levels, rows, width), jnp.float32),
            pltpu.SemaphoreType.DMA((sizes.tracers,)),
        ],
        name="fill_and_scale",
    )(*near(remaining, incoming, row_hit, column_hot))


def solution(mesh):
    in_specs = (
        P("panel", None, None, "lat", "lon"),
        P("panel", None, "lat", "lon"),
        P("panel", None, "lat", "lon"),
        P("panel", None, "lat", "lon"),
        P("panel", "lat", "lon", None, None),
        P(None, "panel", "lat", "lon", None, None),
        P("panel", "lat", "lon", None, None),
        P("panel", "lat", "lon", None),
    )
    out_specs = P("panel", None, None, "lat", "lon")
    return jax.shard_map(body, mesh=mesh, in_specs=in_specs, out_specs=out_specs, check_vma=False)
```

```python
import functools
from typing import NamedTuple

import jax
import jax.numpy as jnp
from jax import lax
from jax.experimental import pallas as pl
from jax.experimental.pallas import tpu as pltpu
from jax.sharding import PartitionSpec as P

HALO = 3
COLUMN_ROWS = 24
FORWARD_ROWS = 16


class Sizes(NamedTuple):
    tracers: int
    levels: int
    rows: int
    width: int
    blocks: int
    capacity: int
    places: int

    @property
    def fields(self):
        return self.tracers * self.levels

    @property
    def sides(self):
        return self.width // self.capacity

    @property
    def margin_rows(self):
        return self.fields // self.sides

    @property
    def halo_rows(self):
        return HALO * self.fields + self.levels

    @property
    def chunks(self):
        return -(-(self.fields + self.levels) * self.rows // self.width)

    def spot(self, tracer):
        start = tracer * self.levels
        return start % self.margin_rows, start // self.margin_rows * self.capacity


def row_of(table):
    return jnp.concatenate([table[i : i + 1] for i in range(table.shape[0])], axis=1)


def live_row(live, capacity):
    slots = lax.broadcasted_iota(jnp.int32, (1, capacity), 1)
    return jnp.concatenate(
        [(slots < live[:, i : i + 1]).astype(jnp.float32) for i in range(live.shape[1])], axis=1
    )


def one_hot(spots, extent):
    places = lax.broadcasted_iota(jnp.int32, (extent, spots.shape[1]), 0)
    return (places == spots).astype(jnp.float32)


def two_parts(value):
    high = value.astype(jnp.bfloat16)
    return high, (value - high.astype(jnp.float32)).astype(jnp.bfloat16)


def three_parts(value):
    high = value.astype(jnp.bfloat16)
    rest = value - high.astype(jnp.float32)
    return (high, *two_parts(rest))


def dot(left, right, transposed=False):
    return lax.dot_general(
        left,
        right,
        (((1,), (1 if transposed else 0,)), ((), ())),
        preferred_element_type=jnp.float32,
    )


def dot_parts(parts, right, transposed=False):
    rows = parts[0].shape[0]
    product = dot(jnp.concatenate(parts, axis=0), right, transposed)
    return sum(product[i * rows : (i + 1) * rows] for i in range(len(parts)))


def cubic_weights(fraction):
    return (
        -fraction * (fraction - 1.0) * (fraction - 2.0) / 6.0,
        (fraction + 1.0) * (fraction - 1.0) * (fraction - 2.0) / 2.0,
        -(fraction + 1.0) * fraction * (fraction - 2.0) / 2.0,
        (fraction + 1.0) * fraction * (fraction - 1.0) / 6.0,
    )


def stencil_weights(start, fraction, extent):
    step = lax.broadcasted_iota(jnp.int32, (extent, start.shape[1]), 0) - start
    spread = jnp.zeros(step.shape, jnp.float32)
    for at, weight in enumerate(cubic_weights(fraction)):
        spread = jnp.where(step == at, weight, spread)
    return spread


def face_flux(cells, number):
    edge_left, edge, edge_right = (
        7.0 / 12.0 * (cells[i + 1] + cells[i + 2]) - 1.0 / 12.0 * (cells[i] + cells[i + 3])
        for i in range(3)
    )
    positive = number > 0.0
    speed = jnp.abs(number)
    far = jnp.where(positive, edge_left, edge_right)
    cell = jnp.where(positive, cells[2], cells[3])
    curve = 6.0 * (cell - 0.5 * (far + edge))
    return number * (edge - 0.5 * speed * ((edge - far) - (1.0 - 2.0 / 3.0 * speed) * curve))


def pack_kernel(
    sizes, field, zonal, meridional, mass, target, live, donor, fraction,
    columns, sides, lat_even, lat_odd, masses, *index_copies,
):
    _, levels, rows, width, blocks, capacity, _ = sizes
    fields = sizes.fields
    here = lax.axis_index("lat")
    for copy, source in zip(index_copies, (donor, fraction, target, live), strict=True):
        copy[...] = source[...]
    even = lax.rem(here, 2) == 0
    for i in range(HALO):
        part = pl.ds(i * fields, fields)
        northward = field[pl.ds(rows - HALO + i, fields, stride=rows), :]
        southward = field[pl.ds(i, fields, stride=rows), :]
        lat_even[part, :] = jnp.where(even, northward, southward)
        lat_odd[part, :] = jnp.where(even, southward, northward)
    number = meridional[pl.ds(0, levels, stride=rows), :]
    lat_even[pl.ds(HALO * fields, levels), :] = number
    lat_odd[pl.ds(HALO * fields, levels), :] = number
    spots = row_of(target[...])
    row_hot = one_hot(spots // width, rows)
    column_hot = one_hot(lax.rem(spots, width), width).astype(jnp.bfloat16)
    picked = dot_parts(two_parts(mass[...]), column_hot)
    picked = jnp.sum(
        picked.reshape(levels, rows, spots.shape[1]) * row_hot[None], axis=1
    ) * live_row(live[...], capacity)
    for block in range(blocks):
        part = picked[:, block * capacity : (block + 1) * capacity]
        masses[pl.ds(block * levels, levels), :] = jnp.concatenate([part] * sizes.sides, axis=1)
    if two_hops(sizes):
        for i, step in enumerate((1, 3)):
            block = pl.multiple_of((here ^ step) * levels, levels)
            lat_even[pl.ds(sizes.halo_rows + i * levels, levels), :] = masses[
                pl.ds(block, levels), :
            ]
    turned = jnp.concatenate([field[...], zonal[...]], axis=0).T
    edges = jnp.concatenate(
        [
            turned[width - HALO : width],
            turned[0:HALO],
            jnp.zeros((8 - 2 * HALO, turned.shape[1]), jnp.float32),
        ],
        axis=0,
    )
    spare = jnp.zeros((8, sizes.chunks * width - edges.shape[1]), jnp.float32)
    edges = jnp.concatenate([edges, spare], axis=1)
    for i in range(sizes.chunks):
        columns[pl.ds(8 * i, 8), :] = edges[:, i * width : (i + 1) * width]
    start = 8 * sizes.chunks
    spare = columns.shape[0] - start
    if spare:
        columns[pl.ds(start, spare), :] = jnp.zeros((spare, width), jnp.float32)
    sides[0 : 2 * HALO] = turned[0 : 2 * HALO]
    sides[2 * HALO : 4 * HALO] = turned[width - 2 * HALO : width]


def passed_on(sizes):
    return sizes.places == 4


def relay_kernel(columns, relayed):
    relayed[...] = columns[0 : relayed.shape[0], :]


def two_hops(sizes):
    return sizes.blocks == 4


def forward_kernel(sizes, masses, lat_even, forwarded):
    levels = sizes.levels
    block = pl.multiple_of((lax.axis_index("lat") ^ 2) * levels, levels)
    forwarded[0:levels, :] = masses[pl.ds(block, levels), :]
    forwarded[levels : 2 * levels, :] = lat_even[pl.ds(sizes.halo_rows + levels, levels), :]
    spare = forwarded.shape[0] - 2 * levels
    if spare:
        forwarded[pl.ds(2 * levels, spare), :] = jnp.zeros((spare, sizes.width), jnp.float32)


def masses_kernel(sizes, masses, lat_even, forwarded, received):
    levels = sizes.levels
    here = lax.axis_index("lat")
    own = pl.multiple_of(here * levels, levels)
    pieces = (
        masses[pl.ds(own, levels), :],
        lat_even[pl.ds(sizes.halo_rows, levels), :],
        forwarded[0:levels, :],
        forwarded[levels : 2 * levels, :],
    )
    for step, piece in enumerate(pieces):
        received[pl.ds(pl.multiple_of((here ^ step) * levels, levels), levels), :] = piece


def tables_kernel(
    sizes, donor, fraction, target, live, kept, row_hit, column_hot, row_weight, high, low
):
    _, _, rows, width, _, capacity, _ = sizes
    spots = row_of(target[...])
    row_hit[...] = one_hot(spots // width, rows) * live_row(live[...], capacity)
    column_hot[...] = one_hot(lax.rem(spots, width), width).astype(jnp.bfloat16)
    kept[...] = 1.0 - dot(row_hit[...].astype(jnp.bfloat16), column_hot[...], True)
    starts = row_of(donor[...])
    row_weight[...] = stencil_weights(starts // width, row_of(fraction[0]), rows)
    high[...], low[...] = two_parts(
        stencil_weights(lax.rem(starts, width), row_of(fraction[1]), width)
    )


def unfold(sizes, rows):
    chunks = [rows[pl.ds(8 * i, 8), :] for i in range(sizes.chunks)]
    return jnp.concatenate(chunks, axis=1)[:, : (sizes.fields + sizes.levels) * sizes.rows]


def zonal_kernel(sizes, field, zonal, moved):
    tracers, levels, rows, width, *_ = sizes
    span = levels * rows
    for tracer in range(tracers):
        part = pl.ds(tracer * span, span)
        cells = field[part, :]
        along = [
            pltpu.roll(cells, shift % width, 1) if shift else cells
            for shift in (3, 2, 1, 0, -1, -2)
        ]
        flux = face_flux(along, zonal[...])
        moved[part, :] = cells - (pltpu.roll(flux, width - 1, 1) - flux)


def prepare_kernel(sizes, field, zonal, donor, fraction, target, live, moved, *tables):
    zonal_kernel(sizes, field, zonal, moved)
    tables_kernel(sizes, donor, fraction, target, live, *tables)


def main_kernel(
    sizes, field, moved, meridional, sides, odd_pairs, even_pairs, lat_odd, lat_even,
    row_weight, weight_high, weight_low,
    advected, outgoing, edge_rows, flux_rows,
):
    tracers, levels, rows, width, blocks, capacity, _ = sizes
    fields, span, total = sizes.fields, levels * rows, sizes.fields * rows
    place = lax.axis_index("lon")
    even = lax.rem(place, 2) == 0
    first, second = unfold(sizes, even_pairs), unfold(sizes, odd_pairs)
    if passed_on(sizes):
        second = jnp.where((place > 0) & (place < sizes.places - 1), second, 0.0)
    from_west = jnp.where(even, second[0:HALO], first[0:HALO])
    from_east = jnp.where(even, first[HALO : 2 * HALO], second[HALO : 2 * HALO])
    west = jnp.concatenate([from_west, sides[0 : 2 * HALO]], axis=0)
    east = jnp.concatenate([sides[2 * HALO : 4 * HALO], from_east], axis=0)
    faces = HALO + 1
    number = jnp.concatenate(
        [west[HALO : HALO + faces, total:], east[HALO : HALO + faces, total:]], axis=0
    )
    flux = face_flux(
        [
            jnp.concatenate([west[i : i + faces, :total], east[i : i + faces, :total]], axis=0)
            for i in range(2 * HALO)
        ],
        jnp.concatenate([number] * tracers, axis=1),
    )
    change = flux[1:] - flux[:-1]
    lanes = jnp.concatenate(
        [
            sides[0:HALO, :total] - change[0:HALO],
            jnp.zeros((width - 2 * HALO, total), jnp.float32),
            sides[3 * HALO : 4 * HALO, :total] - change[faces : faces + HALO],
        ],
        axis=0,
    ).T
    even = lax.rem(lax.axis_index("lat"), 2) == 0
    next_rows = []
    for i in range(HALO):
        part = pl.ds(i * fields, fields)
        first, second = lat_even[part, :], lat_odd[part, :]
        north_row = jnp.where(even, first, second)
        next_rows.append(north_row)
        edge_rows[pl.ds(rows - HALO + i, fields, stride=rows), :] = jnp.where(even, second, first)
        edge_rows[pl.ds(i, fields, stride=rows), :] = north_row
    last_rows = [field[pl.ds(rows - HALO + i, fields, stride=rows), :] for i in range(HALO)]
    part = pl.ds(HALO * fields, levels)
    north_number = jnp.where(even, lat_even[part, :], lat_odd[part, :])
    flux_rows[pl.ds(0, fields, stride=rows), :] = face_flux(
        last_rows + next_rows, jnp.concatenate([north_number] * tracers, axis=0)
    )
    column = lax.broadcasted_iota(jnp.int32, (span, width), 1)
    row = lax.broadcasted_iota(jnp.int32, (levels, rows, width), 1)

    for tracer in range(tracers):
        part = pl.ds(tracer * span, span)
        cells = field[part, :]
        result = jnp.where(
            (column < HALO) | (column >= width - HALO),
            lanes[tracer * span : (tracer + 1) * span],
            moved[part, :],
        )
        cells3 = cells.reshape(levels, rows, width)
        halo3 = edge_rows[part, :].reshape(levels, rows, width)
        along = []
        for shift in (3, 2, 1, 0, -1, -2):
            if shift > 0:
                along.append(pltpu.roll(jnp.where(row >= rows - shift, halo3, cells3), shift, 1))
            elif shift < 0:
                along.append(pltpu.roll(jnp.where(row < -shift, halo3, cells3), rows + shift, 1))
            else:
                along.append(cells3)
        flux = face_flux(along, meridional[...].reshape(levels, rows, width))
        edge3 = flux_rows[part, :].reshape(levels, rows, width)
        next_flux = pltpu.roll(jnp.where(row == 0, edge3, flux), rows - 1, 1)
        result = result.reshape(levels, rows, width) - (next_flux - flux)
        flat = result.reshape(span, width)
        advected[part, :] = flat
    high, low = two_parts(advected[...])
    across = dot_parts((high, low), weight_high[...]) + dot(high, weight_low[...])
    payloads = jnp.sum(across.reshape(fields, rows, -1) * row_weight[...][None], axis=1)
    for tracer in range(tracers):
        payload = payloads[tracer * levels : (tracer + 1) * levels]
        base, lane = sizes.spot(tracer)
        for block in range(blocks):
            at = block * capacity
            outgoing[
                pl.ds(block * sizes.margin_rows + base, levels), lane : lane + capacity
            ] = payload[:, at : at + capacity]


def sums_kernel(sizes, field, mass, advected, kept, remaining, partial):
    tracers, levels, rows, width, *_ = sizes
    span = levels * rows
    weights = mass[...].reshape(levels, rows, width)
    for tracer in range(tracers):
        part = pl.ds(tracer * span, span)
        held = advected[part, :].reshape(levels, rows, width) * kept[...][None]
        remaining[part, :] = held.reshape(span, width)
        before = field[part, :].reshape(levels, rows, width)
        partial[tracer : tracer + 1, :] = jnp.sum(weights * held, axis=(0, 1))[None]
        partial[tracers + tracer : tracers + tracer + 1, :] = jnp.sum(
            weights * before, axis=(0, 1)
        )[None]


def blocks_kernel(sizes, own, given, partial, masses, all_blocks):
    tracers, levels, _, width, blocks, capacity, places = sizes
    size = sizes.margin_rows
    half = size // 2
    mine = lax.axis_index("panel")
    weighed = jnp.zeros((size, width), jnp.float32)
    for block in range(blocks):
        margin = given[pl.ds(block * size, size), :]
        mass = masses[pl.ds(block * levels, levels), :]
        weighed = weighed + margin * jnp.concatenate([mass] * (size // levels), axis=0)
        made = own[pl.ds(block * size, half), :]
        for panel, piece in ((mine, margin[half:]), (1 - mine, made)):
            for place in range(places):
                start = ((panel * places + place) * blocks + block) * (half + 1)
                all_blocks[pl.ds(start, half), :] = piece
    column = lax.broadcasted_iota(jnp.int32, (1, width), 1)
    added = []
    for tracer in range(tracers):
        base, lane = sizes.spot(tracer)
        row = jnp.sum(weighed[base : base + levels], axis=0, keepdims=True)
        added.append(jnp.where((column >= lane) & (column < lane + capacity), row, 0.0))
    sums = partial[...] + jnp.concatenate(
        added + [jnp.zeros((tracers, width), jnp.float32)], axis=0
    )
    totals = jnp.sum(sums, axis=1, keepdims=True)
    line = jnp.zeros((1, width), jnp.float32)
    for i in range(2 * tracers):
        line = jnp.where(column == i, totals[i : i + 1], line)
    for block in range(2 * blocks * places):
        all_blocks[pl.ds(block * (half + 1) + half, 1), :] = line


def fill_kernel(sizes, advected, incoming, row_hit, column_hot, updated, stage, sems):
    tracers, levels, rows, width, blocks, capacity, places = sizes
    half = sizes.margin_rows // 2
    place, mine = lax.axis_index("lon"), lax.axis_index("panel")
    arrived = []
    for block in range(blocks):
        halves = []
        for panel in (1 - mine, mine):
            start = ((panel * places + place) * blocks + block) * (half + 1)
            halves.append(incoming[pl.ds(start, half), :])
        piece = jnp.concatenate(halves, axis=0)
        arrived.append(
            jnp.concatenate(
                [piece[:, i * capacity : (i + 1) * capacity] for i in range(sizes.sides)], axis=0
            )
        )
    arrived = jnp.concatenate(arrived, axis=1)
    line = jnp.sum(
        incoming[pl.ds(half, 2 * blocks * places, stride=half + 1), :], axis=0, keepdims=True
    )
    spread = (arrived[:, None, :] * row_hit[...][None]).reshape(sizes.fields * rows, -1)
    filled = dot_parts(two_parts(spread), column_hot[...], True)
    copies = []
    for tracer in range(tracers):
        placed = filled[tracer * levels * rows : (tracer + 1) * levels * rows]
        old = advected[pl.ds(tracer * levels * rows, levels * rows), :]
        scale = line[:, tracers + tracer : tracers + tracer + 1] / line[:, tracer : tracer + 1]
        stage[tracer] = ((old + placed) * scale).reshape(levels, rows, width)
        copies.append(pltpu.make_async_copy(stage.at[tracer], updated.at[0, tracer], sems.at[tracer]))
        copies[-1].start()
    for copy in copies:
        copy.wait()


def exchanged(value, axis, first):
    pairs = []
    for i in range(first, lax.axis_size(axis) - 1, 2):
        pairs += [(i, i + 1), (i + 1, i)]
    return lax.ppermute(value, axis, pairs)


def body(
    tracers, courant_lon, courant_lat, cell_mass, donor_cell, donor_frac, target_cell, live_count
):
    sizes = Sizes(*tracers.shape[1:], *donor_cell.shape[3:], lax.axis_size("lon"))
    _, levels, rows, width, blocks, capacity, places = sizes
    fields = sizes.fields
    field = tracers.reshape(fields * rows, width)
    zonal = courant_lon.reshape(levels * rows, width)
    meridional = courant_lat.reshape(levels * rows, width)
    mass = cell_mass.reshape(levels * rows, width)
    donor = donor_cell.reshape(blocks, capacity)
    fraction = donor_frac.reshape(2, blocks, capacity)
    target = target_cell.reshape(blocks, capacity)
    live = live_count.reshape(1, blocks)

    def shape(*dims):
        return pltpu.VMEM(dims, jnp.float32)

    def near(*values):
        return (pltpu.with_memory_space_constraint(value, pltpu.VMEM) for value in values)

    slots = blocks * capacity
    columns, sides, lat_even, lat_odd, masses, *index_copies = pl.pallas_call(
        functools.partial(pack_kernel, sizes),
        out_shape=(
            shape(max(COLUMN_ROWS, 8 * sizes.chunks), width),
            shape(4 * HALO, (fields + levels) * rows),
            shape(sizes.halo_rows + (2 * levels if two_hops(sizes) else 0), width),
            shape(sizes.halo_rows, width),
            shape(blocks * levels, width),
            pltpu.VMEM(donor.shape, donor.dtype),
            pltpu.VMEM(fraction.shape, fraction.dtype),
            pltpu.VMEM(target.shape, target.dtype),
            pltpu.VMEM(live.shape, live.dtype),
        ),
        name="pack_edges",
    )(field, zonal, meridional, mass, target, live, donor, fraction)
    lat_even = exchanged(lat_even, "lat", 0)
    lat_odd = exchanged(lat_odd, "lat", 1)
    even_pairs = exchanged(columns, "lon", 0)
    if passed_on(sizes):
        relayed = pl.pallas_call(
            relay_kernel,
            out_shape=shape(8 * sizes.chunks, width),
            cost_estimate=pl.CostEstimate(flops=600000000, bytes_accessed=0, transcendentals=0),
            name="relay_columns",
        )(*near(even_pairs))
        odd_pairs = lax.ppermute(relayed, "lon", [(i, i ^ 2) for i in range(places)])
    else:
        odd_pairs = exchanged(columns, "lon", 1)
    if two_hops(sizes):
        forwarded = pl.pallas_call(
            functools.partial(forward_kernel, sizes),
            out_shape=shape(FORWARD_ROWS, width),
            name="forward_masses",
        )(*near(masses, lat_even))
        forwarded = lax.ppermute(forwarded, "lat", [(i, i ^ 2) for i in range(blocks)])
        masses = pl.pallas_call(
            functools.partial(masses_kernel, sizes),
            out_shape=shape(blocks * levels, width),
            cost_estimate=pl.CostEstimate(flops=500000000, bytes_accessed=0, transcendentals=0),
            name="gather_masses",
        )(*near(masses, lat_even, forwarded))
    else:
        masses = lax.all_to_all(
            masses.reshape(blocks, levels, width), "lat", 0, 0, tiled=True
        ).reshape(blocks * levels, width)
    moved, kept, row_hit, column_hot, *weights = pl.pallas_call(
        functools.partial(prepare_kernel, sizes),
        out_shape=(
            shape(fields * rows, width),
            shape(rows, width),
            shape(rows, slots),
            pltpu.VMEM((width, slots), jnp.bfloat16),
            shape(rows, slots),
            pltpu.VMEM((width, slots), jnp.bfloat16),
            pltpu.VMEM((width, slots), jnp.bfloat16),
        ),
        name="zonal_and_tables",
    )(*near(field, zonal, *index_copies))
    advected, outgoing = pl.pallas_call(
        functools.partial(main_kernel, sizes),
        out_shape=(
            shape(fields * rows, width),
            shape(blocks * sizes.margin_rows, width),
        ),
        scratch_shapes=[
            pltpu.VMEM((fields * rows, width), jnp.float32),
            pltpu.VMEM((fields * rows, width), jnp.float32),
        ],
        name="advect_and_interpolate",
    )(
        *near(
            field, moved, meridional, sides, odd_pairs, even_pairs, lat_odd, lat_even,
            *weights,
        )
    )
    given = lax.ppermute(outgoing, "panel", [(0, 1), (1, 0)])
    remaining, partial = pl.pallas_call(
        functools.partial(sums_kernel, sizes),
        out_shape=(shape(fields * rows, width), shape(2 * sizes.tracers, width)),
        name="kept_and_sums",
    )(*near(field, mass, advected, kept))
    block_rows, devices = sizes.margin_rows // 2 + 1, 2 * blocks * places
    all_blocks = pl.pallas_call(
        functools.partial(blocks_kernel, sizes),
        out_shape=shape(devices * block_rows, width),
        name="margin_blocks",
    )(*near(outgoing, given, partial, masses))
    incoming = lax.all_to_all(
        all_blocks.reshape(devices, 1, block_rows * width), ("panel", "lon", "lat"), 0, 0, tiled=True
    ).reshape(devices * block_rows, width)
    return pl.pallas_call(
        functools.partial(fill_kernel, sizes),
        out_shape=jax.ShapeDtypeStruct((1, sizes.tracers, levels, rows, width), jnp.float32),
        out_specs=pl.BlockSpec(memory_space=pl.ANY),
        scratch_shapes=[
            pltpu.VMEM((sizes.tracers, levels, rows, width), jnp.float32),
            pltpu.SemaphoreType.DMA((sizes.tracers,)),
        ],
        name="fill_and_scale",
    )(*near(remaining, incoming, row_hit, column_hot))


def solution(mesh):
    in_specs = (
        P("panel", None, None, "lat", "lon"),
        P("panel", None, "lat", "lon"),
        P("panel", None, "lat", "lon"),
        P("panel", None, "lat", "lon"),
        P("panel", "lat", "lon", None, None),
        P(None, "panel", "lat", "lon", None, None),
        P("panel", "lat", "lon", None, None),
        P("panel", "lat", "lon", None),
    )
    out_specs = P("panel", None, None, "lat", "lon")
    return jax.shard_map(body, mesh=mesh, in_specs=in_specs, out_specs=out_specs, check_vma=False)
```

```python
import functools
from typing import NamedTuple

import jax
import jax.numpy as jnp
from jax import lax
from jax.experimental import pallas as pl
from jax.experimental.pallas import tpu as pltpu
from jax.sharding import PartitionSpec as P

HALO = 3
COLUMN_ROWS = 24
FORWARD_ROWS = 16


class Sizes(NamedTuple):
    tracers: int
    levels: int
    rows: int
    width: int
    blocks: int
    capacity: int
    places: int

    @property
    def fields(self):
        return self.tracers * self.levels

    @property
    def sides(self):
        return self.width // self.capacity

    @property
    def margin_rows(self):
        return self.fields // self.sides

    @property
    def halo_rows(self):
        return HALO * self.fields + self.levels

    @property
    def chunks(self):
        return -(-(self.fields + self.levels) * self.rows // self.width)

    def spot(self, tracer):
        start = tracer * self.levels
        return start % self.margin_rows, start // self.margin_rows * self.capacity


def row_of(table):
    return jnp.concatenate([table[i : i + 1] for i in range(table.shape[0])], axis=1)


def live_row(live, capacity):
    slots = lax.broadcasted_iota(jnp.int32, (1, capacity), 1)
    return jnp.concatenate(
        [(slots < live[:, i : i + 1]).astype(jnp.float32) for i in range(live.shape[1])], axis=1
    )


def one_hot(spots, extent):
    places = lax.broadcasted_iota(jnp.int32, (extent, spots.shape[1]), 0)
    return (places == spots).astype(jnp.float32)


def two_parts(value):
    high = value.astype(jnp.bfloat16)
    return high, (value - high.astype(jnp.float32)).astype(jnp.bfloat16)


def three_parts(value):
    high = value.astype(jnp.bfloat16)
    rest = value - high.astype(jnp.float32)
    return (high, *two_parts(rest))


def dot(left, right, transposed=False):
    return lax.dot_general(
        left,
        right,
        (((1,), (1 if transposed else 0,)), ((), ())),
        preferred_element_type=jnp.float32,
    )


def dot_parts(parts, right, transposed=False):
    rows = parts[0].shape[0]
    product = dot(jnp.concatenate(parts, axis=0), right, transposed)
    return sum(product[i * rows : (i + 1) * rows] for i in range(len(parts)))


def cubic_weights(fraction):
    return (
        -fraction * (fraction - 1.0) * (fraction - 2.0) / 6.0,
        (fraction + 1.0) * (fraction - 1.0) * (fraction - 2.0) / 2.0,
        -(fraction + 1.0) * fraction * (fraction - 2.0) / 2.0,
        (fraction + 1.0) * fraction * (fraction - 1.0) / 6.0,
    )


def stencil_weights(start, fraction, extent):
    step = lax.broadcasted_iota(jnp.int32, (extent, start.shape[1]), 0) - start
    spread = jnp.zeros(step.shape, jnp.float32)
    for at, weight in enumerate(cubic_weights(fraction)):
        spread = jnp.where(step == at, weight, spread)
    return spread


def face_flux(cells, number):
    edge_left, edge, edge_right = (
        7.0 / 12.0 * (cells[i + 1] + cells[i + 2]) - 1.0 / 12.0 * (cells[i] + cells[i + 3])
        for i in range(3)
    )
    positive = number > 0.0
    speed = jnp.abs(number)
    far = jnp.where(positive, edge_left, edge_right)
    cell = jnp.where(positive, cells[2], cells[3])
    curve = 6.0 * (cell - 0.5 * (far + edge))
    return number * (edge - 0.5 * speed * ((edge - far) - (1.0 - 2.0 / 3.0 * speed) * curve))


def pack_kernel(
    sizes, field, zonal, meridional, mass, target, live, donor, fraction,
    columns, sides, lat_even, lat_odd, masses, *near_copies,
):
    _, levels, rows, width, blocks, capacity, _ = sizes
    fields = sizes.fields
    here = lax.axis_index("lat")
    sources = (donor, fraction, target, live, field, zonal, meridional, mass)
    for copy, source in zip(near_copies, sources, strict=True):
        copy[...] = source[...]
    even = lax.rem(here, 2) == 0
    for i in range(HALO):
        part = pl.ds(i * fields, fields)
        northward = field[pl.ds(rows - HALO + i, fields, stride=rows), :]
        southward = field[pl.ds(i, fields, stride=rows), :]
        lat_even[part, :] = jnp.where(even, northward, southward)
        lat_odd[part, :] = jnp.where(even, southward, northward)
    number = meridional[pl.ds(0, levels, stride=rows), :]
    lat_even[pl.ds(HALO * fields, levels), :] = number
    lat_odd[pl.ds(HALO * fields, levels), :] = number
    spots = row_of(target[...])
    row_hot = one_hot(spots // width, rows)
    column_hot = one_hot(lax.rem(spots, width), width).astype(jnp.bfloat16)
    picked = dot_parts(two_parts(mass[...]), column_hot)
    picked = jnp.sum(
        picked.reshape(levels, rows, spots.shape[1]) * row_hot[None], axis=1
    ) * live_row(live[...], capacity)
    for block in range(blocks):
        part = picked[:, block * capacity : (block + 1) * capacity]
        masses[pl.ds(block * levels, levels), :] = jnp.concatenate([part] * sizes.sides, axis=1)
    if two_hops(sizes):
        for i, step in enumerate((1, 3)):
            block = pl.multiple_of((here ^ step) * levels, levels)
            lat_even[pl.ds(sizes.halo_rows + i * levels, levels), :] = masses[
                pl.ds(block, levels), :
            ]
    turned = jnp.concatenate([field[...], zonal[...]], axis=0).T
    edges = jnp.concatenate(
        [
            turned[width - HALO : width],
            turned[0:HALO],
            jnp.zeros((8 - 2 * HALO, turned.shape[1]), jnp.float32),
        ],
        axis=0,
    )
    spare = jnp.zeros((8, sizes.chunks * width - edges.shape[1]), jnp.float32)
    edges = jnp.concatenate([edges, spare], axis=1)
    for i in range(sizes.chunks):
        columns[pl.ds(8 * i, 8), :] = edges[:, i * width : (i + 1) * width]
    start = 8 * sizes.chunks
    spare = columns.shape[0] - start
    if spare:
        columns[pl.ds(start, spare), :] = jnp.zeros((spare, width), jnp.float32)
    sides[0 : 2 * HALO] = turned[0 : 2 * HALO]
    sides[2 * HALO : 4 * HALO] = turned[width - 2 * HALO : width]


def passed_on(sizes):
    return sizes.places == 4


def relay_kernel(columns, relayed):
    relayed[...] = columns[0 : relayed.shape[0], :]


def two_hops(sizes):
    return sizes.blocks == 4


def forward_kernel(sizes, masses, lat_even, forwarded):
    levels = sizes.levels
    block = pl.multiple_of((lax.axis_index("lat") ^ 2) * levels, levels)
    forwarded[0:levels, :] = masses[pl.ds(block, levels), :]
    forwarded[levels : 2 * levels, :] = lat_even[pl.ds(sizes.halo_rows + levels, levels), :]
    spare = forwarded.shape[0] - 2 * levels
    if spare:
        forwarded[pl.ds(2 * levels, spare), :] = jnp.zeros((spare, sizes.width), jnp.float32)


def masses_kernel(sizes, masses, lat_even, forwarded, received):
    levels = sizes.levels
    here = lax.axis_index("lat")
    own = pl.multiple_of(here * levels, levels)
    pieces = (
        masses[pl.ds(own, levels), :],
        lat_even[pl.ds(sizes.halo_rows, levels), :],
        forwarded[0:levels, :],
        forwarded[levels : 2 * levels, :],
    )
    for step, piece in enumerate(pieces):
        received[pl.ds(pl.multiple_of((here ^ step) * levels, levels), levels), :] = piece


def tables_kernel(
    sizes, donor, fraction, target, live, kept, row_hit, column_hot, row_weight, high, low
):
    _, _, rows, width, _, capacity, _ = sizes
    spots = row_of(target[...])
    row_hit[...] = one_hot(spots // width, rows) * live_row(live[...], capacity)
    column_hot[...] = one_hot(lax.rem(spots, width), width).astype(jnp.bfloat16)
    kept[...] = 1.0 - dot(row_hit[...].astype(jnp.bfloat16), column_hot[...], True)
    starts = row_of(donor[...])
    row_weight[...] = stencil_weights(starts // width, row_of(fraction[0]), rows)
    high[...], low[...] = two_parts(
        stencil_weights(lax.rem(starts, width), row_of(fraction[1]), width)
    )


def unfold(sizes, rows):
    chunks = [rows[pl.ds(8 * i, 8), :] for i in range(sizes.chunks)]
    return jnp.concatenate(chunks, axis=1)[:, : (sizes.fields + sizes.levels) * sizes.rows]


def zonal_kernel(sizes, field, zonal, moved):
    tracers, levels, rows, width, *_ = sizes
    span = levels * rows
    for tracer in range(tracers):
        part = pl.ds(tracer * span, span)
        cells = field[part, :]
        along = [
            pltpu.roll(cells, shift % width, 1) if shift else cells
            for shift in (3, 2, 1, 0, -1, -2)
        ]
        flux = face_flux(along, zonal[...])
        moved[part, :] = cells - (pltpu.roll(flux, width - 1, 1) - flux)


def prepare_kernel(sizes, field, zonal, donor, fraction, target, live, moved, *tables):
    zonal_kernel(sizes, field, zonal, moved)
    tables_kernel(sizes, donor, fraction, target, live, *tables)


def main_kernel(
    sizes, field, moved, meridional, sides, odd_pairs, even_pairs, lat_odd, lat_even,
    row_weight, weight_high, weight_low,
    advected, outgoing, edge_rows, flux_rows,
):
    tracers, levels, rows, width, blocks, capacity, _ = sizes
    fields, span, total = sizes.fields, levels * rows, sizes.fields * rows
    place = lax.axis_index("lon")
    even = lax.rem(place, 2) == 0
    first, second = unfold(sizes, even_pairs), unfold(sizes, odd_pairs)
    if passed_on(sizes):
        second = jnp.where((place > 0) & (place < sizes.places - 1), second, 0.0)
    from_west = jnp.where(even, second[0:HALO], first[0:HALO])
    from_east = jnp.where(even, first[HALO : 2 * HALO], second[HALO : 2 * HALO])
    west = jnp.concatenate([from_west, sides[0 : 2 * HALO]], axis=0)
    east = jnp.concatenate([sides[2 * HALO : 4 * HALO], from_east], axis=0)
    faces = HALO + 1
    number = jnp.concatenate(
        [west[HALO : HALO + faces, total:], east[HALO : HALO + faces, total:]], axis=0
    )
    flux = face_flux(
        [
            jnp.concatenate([west[i : i + faces, :total], east[i : i + faces, :total]], axis=0)
            for i in range(2 * HALO)
        ],
        jnp.concatenate([number] * tracers, axis=1),
    )
    change = flux[1:] - flux[:-1]
    lanes = jnp.concatenate(
        [
            sides[0:HALO, :total] - change[0:HALO],
            jnp.zeros((width - 2 * HALO, total), jnp.float32),
            sides[3 * HALO : 4 * HALO, :total] - change[faces : faces + HALO],
        ],
        axis=0,
    ).T
    even = lax.rem(lax.axis_index("lat"), 2) == 0
    next_rows = []
    for i in range(HALO):
        part = pl.ds(i * fields, fields)
        first, second = lat_even[part, :], lat_odd[part, :]
        north_row = jnp.where(even, first, second)
        next_rows.append(north_row)
        edge_rows[pl.ds(rows - HALO + i, fields, stride=rows), :] = jnp.where(even, second, first)
        edge_rows[pl.ds(i, fields, stride=rows), :] = north_row
    last_rows = [field[pl.ds(rows - HALO + i, fields, stride=rows), :] for i in range(HALO)]
    part = pl.ds(HALO * fields, levels)
    north_number = jnp.where(even, lat_even[part, :], lat_odd[part, :])
    flux_rows[pl.ds(0, fields, stride=rows), :] = face_flux(
        last_rows + next_rows, jnp.concatenate([north_number] * tracers, axis=0)
    )
    column = lax.broadcasted_iota(jnp.int32, (span, width), 1)
    row = lax.broadcasted_iota(jnp.int32, (levels, rows, width), 1)

    for tracer in range(tracers):
        part = pl.ds(tracer * span, span)
        cells = field[part, :]
        result = jnp.where(
            (column < HALO) | (column >= width - HALO),
            lanes[tracer * span : (tracer + 1) * span],
            moved[part, :],
        )
        cells3 = cells.reshape(levels, rows, width)
        halo3 = edge_rows[part, :].reshape(levels, rows, width)
        along = []
        for shift in (3, 2, 1, 0, -1, -2):
            if shift > 0:
                along.append(pltpu.roll(jnp.where(row >= rows - shift, halo3, cells3), shift, 1))
            elif shift < 0:
                along.append(pltpu.roll(jnp.where(row < -shift, halo3, cells3), rows + shift, 1))
            else:
                along.append(cells3)
        flux = face_flux(along, meridional[...].reshape(levels, rows, width))
        edge3 = flux_rows[part, :].reshape(levels, rows, width)
        next_flux = pltpu.roll(jnp.where(row == 0, edge3, flux), rows - 1, 1)
        result = result.reshape(levels, rows, width) - (next_flux - flux)
        flat = result.reshape(span, width)
        advected[part, :] = flat
    high, low = two_parts(advected[...])
    across = dot_parts((high, low), weight_high[...]) + dot(high, weight_low[...])
    payloads = jnp.sum(across.reshape(fields, rows, -1) * row_weight[...][None], axis=1)
    for tracer in range(tracers):
        payload = payloads[tracer * levels : (tracer + 1) * levels]
        base, lane = sizes.spot(tracer)
        for block in range(blocks):
            at = block * capacity
            outgoing[
                pl.ds(block * sizes.margin_rows + base, levels), lane : lane + capacity
            ] = payload[:, at : at + capacity]


def sums_kernel(sizes, field, mass, advected, kept, remaining, partial):
    tracers, levels, rows, width, *_ = sizes
    span = levels * rows
    weights = mass[...].reshape(levels, rows, width)
    for tracer in range(tracers):
        part = pl.ds(tracer * span, span)
        held = advected[part, :].reshape(levels, rows, width) * kept[...][None]
        remaining[part, :] = held.reshape(span, width)
        before = field[part, :].reshape(levels, rows, width)
        partial[tracer : tracer + 1, :] = jnp.sum(weights * held, axis=(0, 1))[None]
        partial[tracers + tracer : tracers + tracer + 1, :] = jnp.sum(
            weights * before, axis=(0, 1)
        )[None]


def blocks_kernel(sizes, own, given, partial, masses, all_blocks):
    tracers, levels, _, width, blocks, capacity, places = sizes
    size = sizes.margin_rows
    half = size // 2
    mine = lax.axis_index("panel")
    weighed = jnp.zeros((size, width), jnp.float32)
    for block in range(blocks):
        margin = given[pl.ds(block * size, size), :]
        mass = masses[pl.ds(block * levels, levels), :]
        weighed = weighed + margin * jnp.concatenate([mass] * (size // levels), axis=0)
        made = own[pl.ds(block * size, half), :]
        for panel, piece in ((mine, margin[half:]), (1 - mine, made)):
            for place in range(places):
                start = ((panel * places + place) * blocks + block) * (half + 1)
                all_blocks[pl.ds(start, half), :] = piece
    column = lax.broadcasted_iota(jnp.int32, (1, width), 1)
    added = []
    for tracer in range(tracers):
        base, lane = sizes.spot(tracer)
        row = jnp.sum(weighed[base : base + levels], axis=0, keepdims=True)
        added.append(jnp.where((column >= lane) & (column < lane + capacity), row, 0.0))
    sums = partial[...] + jnp.concatenate(
        added + [jnp.zeros((tracers, width), jnp.float32)], axis=0
    )
    totals = jnp.sum(sums, axis=1, keepdims=True)
    line = jnp.zeros((1, width), jnp.float32)
    for i in range(2 * tracers):
        line = jnp.where(column == i, totals[i : i + 1], line)
    for block in range(2 * blocks * places):
        all_blocks[pl.ds(block * (half + 1) + half, 1), :] = line


def fill_kernel(sizes, advected, incoming, row_hit, column_hot, updated, stage, sems):
    tracers, levels, rows, width, blocks, capacity, places = sizes
    half = sizes.margin_rows // 2
    place, mine = lax.axis_index("lon"), lax.axis_index("panel")
    arrived = []
    for block in range(blocks):
        halves = []
        for panel in (1 - mine, mine):
            start = ((panel * places + place) * blocks + block) * (half + 1)
            halves.append(incoming[pl.ds(start, half), :])
        piece = jnp.concatenate(halves, axis=0)
        arrived.append(
            jnp.concatenate(
                [piece[:, i * capacity : (i + 1) * capacity] for i in range(sizes.sides)], axis=0
            )
        )
    arrived = jnp.concatenate(arrived, axis=1)
    line = jnp.sum(
        incoming[pl.ds(half, 2 * blocks * places, stride=half + 1), :], axis=0, keepdims=True
    )
    spread = (arrived[:, None, :] * row_hit[...][None]).reshape(sizes.fields * rows, -1)
    filled = dot_parts(two_parts(spread), column_hot[...], True)
    copies = []
    for tracer in range(tracers):
        placed = filled[tracer * levels * rows : (tracer + 1) * levels * rows]
        old = advected[pl.ds(tracer * levels * rows, levels * rows), :]
        scale = line[:, tracers + tracer : tracers + tracer + 1] / line[:, tracer : tracer + 1]
        stage[tracer] = ((old + placed) * scale).reshape(levels, rows, width)
        copies.append(pltpu.make_async_copy(stage.at[tracer], updated.at[0, tracer], sems.at[tracer]))
        copies[-1].start()
    for copy in copies:
        copy.wait()


def exchanged(value, axis, first):
    pairs = []
    for i in range(first, lax.axis_size(axis) - 1, 2):
        pairs += [(i, i + 1), (i + 1, i)]
    return lax.ppermute(value, axis, pairs)


def body(
    tracers, courant_lon, courant_lat, cell_mass, donor_cell, donor_frac, target_cell, live_count
):
    sizes = Sizes(*tracers.shape[1:], *donor_cell.shape[3:], lax.axis_size("lon"))
    _, levels, rows, width, blocks, capacity, places = sizes
    fields = sizes.fields
    field = tracers.reshape(fields * rows, width)
    zonal = courant_lon.reshape(levels * rows, width)
    meridional = courant_lat.reshape(levels * rows, width)
    mass = cell_mass.reshape(levels * rows, width)
    donor = donor_cell.reshape(blocks, capacity)
    fraction = donor_frac.reshape(2, blocks, capacity)
    target = target_cell.reshape(blocks, capacity)
    live = live_count.reshape(1, blocks)

    def shape(*dims):
        return pltpu.VMEM(dims, jnp.float32)

    def near(*values):
        return (pltpu.with_memory_space_constraint(value, pltpu.VMEM) for value in values)

    slots = blocks * capacity
    columns, sides, lat_even, lat_odd, masses, *near_copies = pl.pallas_call(
        functools.partial(pack_kernel, sizes),
        out_shape=(
            shape(max(COLUMN_ROWS, 8 * sizes.chunks), width),
            shape(4 * HALO, (fields + levels) * rows),
            shape(sizes.halo_rows + (2 * levels if two_hops(sizes) else 0), width),
            shape(sizes.halo_rows, width),
            shape(blocks * levels, width),
            pltpu.VMEM(donor.shape, donor.dtype),
            pltpu.VMEM(fraction.shape, fraction.dtype),
            pltpu.VMEM(target.shape, target.dtype),
            pltpu.VMEM(live.shape, live.dtype),
            shape(*field.shape),
            shape(*zonal.shape),
            shape(*meridional.shape),
            shape(*mass.shape),
        ),
        name="pack_edges",
    )(field, zonal, meridional, mass, target, live, donor, fraction)
    *index_copies, field, zonal, meridional, mass = near_copies
    lat_even = exchanged(lat_even, "lat", 0)
    lat_odd = exchanged(lat_odd, "lat", 1)
    even_pairs = exchanged(columns, "lon", 0)
    if passed_on(sizes):
        relayed = pl.pallas_call(
            relay_kernel,
            out_shape=shape(8 * sizes.chunks, width),
            cost_estimate=pl.CostEstimate(flops=600000000, bytes_accessed=0, transcendentals=0),
            name="relay_columns",
        )(*near(even_pairs))
        odd_pairs = lax.ppermute(relayed, "lon", [(i, i ^ 2) for i in range(places)])
    else:
        odd_pairs = exchanged(columns, "lon", 1)
    if two_hops(sizes):
        forwarded = pl.pallas_call(
            functools.partial(forward_kernel, sizes),
            out_shape=shape(FORWARD_ROWS, width),
            name="forward_masses",
        )(*near(masses, lat_even))
        forwarded = lax.ppermute(forwarded, "lat", [(i, i ^ 2) for i in range(blocks)])
        masses = pl.pallas_call(
            functools.partial(masses_kernel, sizes),
            out_shape=shape(blocks * levels, width),
            cost_estimate=pl.CostEstimate(flops=500000000, bytes_accessed=0, transcendentals=0),
            name="gather_masses",
        )(*near(masses, lat_even, forwarded))
    else:
        masses = lax.all_to_all(
            masses.reshape(blocks, levels, width), "lat", 0, 0, tiled=True
        ).reshape(blocks * levels, width)
    moved, kept, row_hit, column_hot, *weights = pl.pallas_call(
        functools.partial(prepare_kernel, sizes),
        out_shape=(
            shape(fields * rows, width),
            shape(rows, width),
            shape(rows, slots),
            pltpu.VMEM((width, slots), jnp.bfloat16),
            shape(rows, slots),
            pltpu.VMEM((width, slots), jnp.bfloat16),
            pltpu.VMEM((width, slots), jnp.bfloat16),
        ),
        name="zonal_and_tables",
    )(*near(field, zonal, *index_copies))
    advected, outgoing = pl.pallas_call(
        functools.partial(main_kernel, sizes),
        out_shape=(
            shape(fields * rows, width),
            shape(blocks * sizes.margin_rows, width),
        ),
        scratch_shapes=[
            pltpu.VMEM((fields * rows, width), jnp.float32),
            pltpu.VMEM((fields * rows, width), jnp.float32),
        ],
        name="advect_and_interpolate",
    )(
        *near(
            field, moved, meridional, sides, odd_pairs, even_pairs, lat_odd, lat_even,
            *weights,
        )
    )
    given = lax.ppermute(outgoing, "panel", [(0, 1), (1, 0)])
    remaining, partial = pl.pallas_call(
        functools.partial(sums_kernel, sizes),
        out_shape=(shape(fields * rows, width), shape(2 * sizes.tracers, width)),
        name="kept_and_sums",
    )(*near(field, mass, advected, kept))
    block_rows, devices = sizes.margin_rows // 2 + 1, 2 * blocks * places
    all_blocks = pl.pallas_call(
        functools.partial(blocks_kernel, sizes),
        out_shape=shape(devices * block_rows, width),
        name="margin_blocks",
    )(*near(outgoing, given, partial, masses))
    incoming = lax.all_to_all(
        all_blocks.reshape(devices, 1, block_rows * width), ("panel", "lon", "lat"), 0, 0, tiled=True
    ).reshape(devices * block_rows, width)
    return pl.pallas_call(
        functools.partial(fill_kernel, sizes),
        out_shape=jax.ShapeDtypeStruct((1, sizes.tracers, levels, rows, width), jnp.float32),
        out_specs=pl.BlockSpec(memory_space=pl.ANY),
        scratch_shapes=[
            pltpu.VMEM((sizes.tracers, levels, rows, width), jnp.float32),
            pltpu.SemaphoreType.DMA((sizes.tracers,)),
        ],
        name="fill_and_scale",
    )(*near(remaining, incoming, row_hit, column_hot))


def solution(mesh):
    in_specs = (
        P("panel", None, None, "lat", "lon"),
        P("panel", None, "lat", "lon"),
        P("panel", None, "lat", "lon"),
        P("panel", None, "lat", "lon"),
        P("panel", "lat", "lon", None, None),
        P(None, "panel", "lat", "lon", None, None),
        P("panel", "lat", "lon", None, None),
        P("panel", "lat", "lon", None),
    )
    out_specs = P("panel", None, None, "lat", "lon")
    return jax.shard_map(body, mesh=mesh, in_specs=in_specs, out_specs=out_specs, check_vma=False)
```
